256 devices in a mesh: rollout: 16 (over x, y_lo, core), ctx: 16 (over y_hi, z).
Axes of the slice: x: 4, y: 4 (y_hi: 2, y_lo: 2; y = y_hi * 2 + y_lo), z: 8, core: 2. Of those that a mesh axis runs over, the one named last changes fastest.
Arguments:
- prompt_inputs: bfloat16 [32768, 2560], P(('rollout', 'ctx')), may hold values from -6 to 6
- prompt_keys: bfloat16 [32768, 128], P(('rollout', 'ctx')), may hold values from -0.5 to 0.5
- prompt_steps: float32 [40, 32768], P(None, ('rollout', 'ctx')), may hold values from 0.045 to 1.5
- reply_inputs: bfloat16 [16, 2048, 2560], P('rollout', 'ctx'), may hold values from -6 to 6
- reply_keys: bfloat16 [16, 2048, 128], P('rollout', 'ctx'), may hold values from -0.5 to 0.5
- reply_queries: bfloat16 [16, 2048, 128], P('rollout', 'ctx'), may hold values from -0.5 to 0.5
- reply_steps: float32 [16, 40, 2048], P('rollout', None, 'ctx'), may hold values from 0.3 to 1.5
- decay_log: float32 [40], replicated, may hold values from -20 to -2, as said below
- upstream: bfloat16 [16, 2048, 2560], P('rollout', 'ctx'), may hold values from -6 to 6
- loss_mask: int32 [16, 2048], P('rollout', 'ctx'), may hold values 0 or 1
- advantage_index: int32 [16], P('rollout'), may hold values from 0 to 15
- advantage_table: float32 [16], replicated, may hold values from -1.5 to 1.5
Outputs:
- gradient_prompt_inputs: bfloat16 [32768, 2560], P(('rollout', 'ctx'))
- gradient_prompt_keys: bfloat16 [32768, 128], P(('rollout', 'ctx'))
- gradient_prompt_steps: float32 [40, 32768], P(None, ('rollout', 'ctx'))
- gradient_reply_inputs: bfloat16 [16, 2048, 2560], P('rollout', 'ctx')
- gradient_reply_keys: bfloat16 [16, 2048, 128], P('rollout', 'ctx')
- gradient_reply_queries: bfloat16 [16, 2048, 128], P('rollout', 'ctx')
- gradient_reply_steps: float32 [16, 40, 2048], P('rollout', None, 'ctx')
- gradient_decay_log: float32 [40], replicated
The draws below stay inside these ranges and needn't reach their ends.
Inputs may be any that keep to these rules, and one draw needn't show every extreme that they name: `decay_log`: each head's decay rate is positive.
All inputs are finite; a program needn't handle non-finite values. No bound on the sum of `loss_mask` on one device may be relied on, other than what follows from the above.
Results may differ from the reference program's by a relative error of at most 0.0015.
Values sent between devices are 32-bit elements; how exact they have to be, the bound alone decides.
No kernel may reach another device: no remote copies, remote signals or barrier semaphores. Data moves between devices by JAX's collectives and lax.ppermute only.
A program may use at most 192 MiB of HBM per device.

```python
import math
import jax
import jax.numpy as jnp
from jax import lax

HEADS = 40
HEAD_DIM = 64
STATE = 128
BLOCK = 128
LEVELS = 16
PROMPT_DEV = 128
PROMPT = 32768
REPLY_LEN = 2048
ROWS = 16
CHANNELS = 2560


def draw_decay_log(key, part):
    key = jax.random.fold_in(key, 7)
    pick_key, slow_key, fast_key = jax.random.split(key, 3)
    chain_length = PROMPT + REPLY_LEN
    slow_share = 0.5
    slow = jax.random.uniform(pick_key, (HEADS,)) < slow_share
    slow_rate = jax.random.uniform(slow_key, (HEADS,), minval=0.1, maxval=1.5) / chain_length
    fast_rate = jax.random.uniform(fast_key, (HEADS,), minval=0.02, maxval=0.1)
    return jnp.log(jnp.where(slow, slow_rate, fast_rate)).astype(jnp.float32)


def draw_prompt_steps(key, part):
    key = jax.random.fold_in(key, 11)
    base_key, piece_key = jax.random.split(key, 2)
    base = jnp.exp(jax.random.uniform(base_key, (HEADS, PROMPT), minval=jnp.log(0.3), maxval=jnp.log(1.5)))
    pieces = PROMPT // PROMPT_DEV
    factor = jnp.exp(jax.random.uniform(piece_key, (HEADS, pieces, 1), minval=jnp.log(0.15), maxval=0.0))
    spread = jnp.broadcast_to(factor, (HEADS, pieces, PROMPT_DEV)).reshape(HEADS, PROMPT)
    return (base * spread).astype(jnp.float32)


def touch_ends(values, key, smallest, top_value):
    spot = [jax.random.randint(jax.random.fold_in(key, axis), (), 0, length) for axis, length in enumerate(values.shape)]
    main_axis = values.shape.index(max(values.shape))
    next_to = spot[:main_axis] + [(spot[main_axis] + 1) % values.shape[main_axis]] + spot[main_axis + 1:]
    return values.at[tuple(spot)].set(smallest).at[tuple(next_to)].set(top_value)


def block_scale(own_key, shape, cuts, smallest, top_value):
    loudness = 1.0
    for axis_at, parts in cuts:
        draws = jax.random.uniform(jax.random.fold_in(jax.random.fold_in(own_key, 6), axis_at), (parts,), jnp.float32, smallest / len(cuts), top_value / len(cuts))
        loudness = loudness * jnp.repeat(jnp.exp(draws), shape[axis_at] // parts).reshape((-1,) + (1,) * (len(shape) - 1 - axis_at))
    return loudness


def gaussian(rng, extent, scale, bound, cuts=(), kind=jnp.bfloat16):
    array = scale * jax.random.normal(rng, extent, jnp.float32)
    if cuts:
        array = array * block_scale(rng, extent, cuts, -0.22, 0.18)
    return jnp.clip(array, -bound, bound).astype(kind)


def setup_inputs(seed: int = 0) -> dict:
    streams_of = jax.random.split(jax.random.key(seed), 13)
    return {
        "prompt_inputs": gaussian(streams_of[0], (PROMPT, CHANNELS), 1.0, 6.0, ((0, 256),)),
        "prompt_keys": gaussian(streams_of[1], (PROMPT, STATE), STATE ** -0.5, 0.5, ((0, 256),)),
        "prompt_steps": draw_prompt_steps(jax.random.fold_in(streams_of[12], 71), 0),
        "reply_inputs": gaussian(streams_of[3], (ROWS, REPLY_LEN, CHANNELS), 1.0, 6.0, ((0, 16), (1, 16))),
        "reply_keys": gaussian(streams_of[4], (ROWS, REPLY_LEN, STATE), STATE ** -0.5, 0.5, ((0, 16), (1, 16))),
        "reply_queries": gaussian(streams_of[5], (ROWS, REPLY_LEN, STATE), STATE ** -0.5, 0.5, ((0, 16), (1, 16))),
        "reply_steps": jnp.clip(jnp.exp(math.log(1.5) - 1.60943787 * jax.random.uniform(streams_of[6], (ROWS, HEADS, REPLY_LEN), jnp.float32) ** block_scale(streams_of[6], (ROWS, HEADS, REPLY_LEN), ((0, 16), (2, 16)), -0.2, 0.2)), 0.3, 1.5),
        "decay_log": draw_decay_log(jax.random.fold_in(streams_of[12], 71), 0),
        "upstream": gaussian(streams_of[8], (ROWS, REPLY_LEN, CHANNELS), 1.0, 6.0, ((0, 16), (1, 16))),
        "loss_mask": touch_ends((jax.random.randint(streams_of[9], (ROWS, REPLY_LEN), 0, 4) < 3).astype(jnp.int32), jax.random.fold_in(streams_of[9], 1), 0, 1),
        "advantage_index": touch_ends(jax.random.randint(streams_of[10], (ROWS,), 0, LEVELS), jax.random.fold_in(streams_of[10], 1), 0, LEVELS - 1).astype(jnp.int32),
        "advantage_table": jnp.clip(jax.random.uniform(streams_of[11], (LEVELS,), jnp.float32, -1.5, 1.5), -1.5, 1.5),
    }


def product(pattern, *operands):
    return jnp.einsum(pattern, *operands, precision=lax.Precision.HIGHEST)

def span_logs(step_sizes, decay_log):
    log_decays = -step_sizes * jnp.exp(decay_log)[:, None]
    return jnp.cumsum(log_decays.reshape(HEADS, step_sizes.shape[1] // BLOCK, BLOCK), axis=2)

def scaled_inputs(inputs, step_sizes, block_count):
    spread = jnp.transpose(step_sizes.reshape(HEADS, block_count, BLOCK), (1, 2, 0))
    return inputs.astype(jnp.float32).reshape(block_count, BLOCK, HEADS, HEAD_DIM) * spread[..., None]

def block_states(running, keyed_rows, feeding):
    to_end = jnp.exp(running[:, :, -1:] - running)
    return product('hkj,kjn,kjhp->khpn', to_end, keyed_rows, feeding)

def carry_along(totals, states, start_state):

    def advance(running_state, block_item):
        return (block_item[0][:, None, None] * running_state + block_item[1], running_state)
    return lax.scan(advance, start_state, (jnp.transpose(totals), states))

def segment_state(inputs, key_rows, step_sizes, decay_log, start_state):
    running = span_logs(step_sizes, decay_log)
    block_count = running.shape[1]
    feeding = scaled_inputs(inputs, step_sizes, block_count)
    keyed_rows = key_rows.astype(jnp.float32).reshape(block_count, BLOCK, STATE)
    closing, openings = carry_along(jnp.exp(running[:, :, -1]), block_states(running, keyed_rows, feeding), start_state)
    return closing

def segment_output(inputs, key_rows, queries, step_sizes, decay_log, start_state):
    running = span_logs(step_sizes, decay_log)
    block_count = running.shape[1]
    feeding = scaled_inputs(inputs, step_sizes, block_count)
    keyed_rows = key_rows.astype(jnp.float32).reshape(block_count, BLOCK, STATE)
    queried = queries.astype(jnp.float32).reshape(block_count, BLOCK, STATE)
    scores = product('kin,kjn->kij', queried, keyed_rows)
    row_index = lax.broadcasted_iota(jnp.int32, (BLOCK, BLOCK), 0)
    col_index = lax.broadcasted_iota(jnp.int32, (BLOCK, BLOCK), 1)
    causal = row_index >= col_index
    log_gaps = running[:, :, :, None] - running[:, :, None, :]
    mixing = jnp.where(causal, jnp.exp(jnp.where(causal, log_gaps, 0.0)), 0.0)
    within = product('hkij,kij,kjhp->kihp', mixing, scores, feeding)
    closing, openings = carry_along(jnp.exp(running[:, :, -1]), block_states(running, keyed_rows, feeding), start_state)
    across = product('kin,hki,khpn->kihp', queried, jnp.exp(running), openings)
    return ((within + across).reshape(block_count * BLOCK, HEADS * HEAD_DIM), closing)

def reference(prompt_inputs, prompt_keys, prompt_steps, reply_inputs, reply_keys, reply_queries, reply_steps, decay_log, upstream, loss_mask, advantage_index, advantage_table):
    empty_state = jnp.zeros((HEADS, HEAD_DIM, STATE), jnp.float32)

    def prompt_forward(inputs, key_rows, step_sizes, rates_log):
        return segment_state(inputs, key_rows, step_sizes, rates_log, empty_state)
    end_state, prompt_pullback = jax.vjp(prompt_forward, prompt_inputs, prompt_keys, prompt_steps, decay_log)

    def row_step(totals, row_item):
        end_total, decay_total = totals
        inputs, key_rows, queries, step_sizes, upper, marks, index = row_item
        weight = advantage_table[index]
        cotangent = upper.astype(jnp.float32) * marks[:, None].astype(jnp.float32) * weight
        (outputs, closing), pullback = jax.vjp(segment_output, inputs, key_rows, queries, step_sizes, decay_log, end_state)
        pulled = pullback((cotangent, jnp.zeros_like(closing)))
        return ((end_total + pulled[5], decay_total + pulled[4]), (pulled[0], pulled[1], pulled[2], pulled[3]))
    start_totals = (empty_state, jnp.zeros((HEADS,), jnp.float32))
    (end_gradient, decay_gradient), row_grads = lax.scan(row_step, start_totals, (reply_inputs, reply_keys, reply_queries, reply_steps, upstream, loss_mask, advantage_index))
    prompt_grads = prompt_pullback(end_gradient)
    return (prompt_grads[0], prompt_grads[1], prompt_grads[2], row_grads[0], row_grads[1], row_grads[2], row_grads[3], decay_gradient + prompt_grads[3])
```

```python
import jax
import jax.numpy as jnp
from jax import lax
from jax.experimental import pallas as pl
from jax.experimental.pallas import tpu as pltpu
from jax.sharding import PartitionSpec as P

HEADS = 40
HEAD_DIM = 64
STATE = 128
TOKENS = 128
CHANNELS = HEADS * HEAD_DIM
PAIRS = HEADS // 2
SLICES = 16
ROWS = CHANNELS // SLICES
PIECE = 32
PER_SLICE = ROWS // PIECE
PACK = 3 * ROWS + 8
F32 = jnp.float32
BF16 = jnp.bfloat16
HIGHEST = lax.Precision.HIGHEST
VMEM_LIMIT = 48 * 1024 * 1024


def iota(shape, axis):
    return lax.broadcasted_iota(jnp.int32, shape, axis)


def halves(value):
    high = value.astype(BF16)
    return high, (value - high.astype(F32)).astype(BF16)


def dot(left, right):
    return jnp.dot(left, right, preferred_element_type=F32)


def dot_t(left, right, precision=None):
    return lax.dot_general(
        left, right, (((1,), (1,)), ((), ())), preferred_element_type=F32, precision=precision
    )


def exact_dot(left, right):
    return jnp.dot(left, right, preferred_element_type=F32, precision=HIGHEST)


def running_logs(steps, rate):
    earlier = (iota((TOKENS, TOKENS), 0) <= iota((TOKENS, TOKENS), 1)).astype(F32)
    return exact_dot(-steps * rate, earlier)


def transposed(rows):
    pad = jnp.zeros((TOKENS - rows.shape[0], TOKENS), F32)
    return jnp.concatenate([rows, pad], axis=0).T


def pair_rows(rows, pair):
    first = jnp.broadcast_to(rows[2 * pair : 2 * pair + 1], (HEAD_DIM, TOKENS))
    second = jnp.broadcast_to(rows[2 * pair + 1 : 2 * pair + 2], (HEAD_DIM, TOKENS))
    return jnp.concatenate([first, second], axis=0)


def column(columns, head):
    return jnp.broadcast_to(columns[:, head : head + 1], (TOKENS, TOKENS))


def pair_columns(columns, pair, first_half):
    return jnp.where(first_half, column(columns, 2 * pair), column(columns, 2 * pair + 1))


def pieces(pair):
    for part in range(4):
        place = 4 * pair + part
        yield part * PIECE, place // PER_SLICE, (place % PER_SLICE) * PIECE


def local_states_kernel(
    prompt_inputs, prompt_keys, prompt_steps, reply_inputs, reply_keys, reply_queries,
    reply_steps, rate, upstream, mask, weight, pack, prompt_logs, reply_logs,
):
    prompt_running = running_logs(prompt_steps[...], rate[...])
    reply_running = running_logs(reply_steps[...], rate[...])
    prompt_logs[...] = prompt_running
    reply_logs[...] = reply_running
    prompt_last = prompt_running[:, TOKENS - 1 :]
    reply_last = reply_running[:, TOKENS - 1 :]
    prompt_rows = jnp.exp(prompt_last - prompt_running) * prompt_steps[...]
    reply_rows = jnp.exp(reply_last - reply_running) * reply_steps[...]
    pull_rows = jnp.exp(reply_running) * (mask[...].astype(F32) * weight[0, 0])
    first = jnp.broadcast_to(reply_last, (HEADS, TOKENS))
    second = jnp.broadcast_to(prompt_last, (HEADS, TOKENS))
    totals = jnp.concatenate([transposed(first)[0:1], transposed(second)[0:1]], axis=0)
    totals = jnp.concatenate([totals, jnp.zeros((6, TOKENS), F32)], axis=0)
    for owner in range(SLICES):
        pack[owner, 3 * ROWS :, :] = totals
    keyed = (
        (0, reply_inputs, reply_rows, reply_keys[...]),
        (ROWS, upstream, pull_rows, reply_queries[...]),
        (2 * ROWS, prompt_inputs, prompt_rows, prompt_keys[...]),
    )
    for base, tokens, rows, keys in keyed:
        twice = jnp.concatenate([keys, keys], axis=0)
        for pair in range(PAIRS):
            block = tokens[:, pair * TOKENS : (pair + 1) * TOKENS].astype(F32).T
            high, low = halves(block * pair_rows(rows, pair))
            states = dot(jnp.concatenate([high, low], axis=1), twice)
            for at, owner, offset in pieces(pair):
                pack[owner, base + offset : base + offset + PIECE, :] = states[at : at + PIECE]


def within_kernel(
    inputs, keys, queries, steps, upstream, mask_column, logs, near, mixed, row_sums, column_sums
):
    running = logs[...]
    columns = transposed(jnp.log(steps[...]) - running)
    causal = iota((TOKENS, TOKENS), 1) >= iota((TOKENS, TOKENS), 0)
    first_half = iota((TOKENS, TOKENS), 1) < HEAD_DIM
    lanes = iota((TOKENS, TOKENS), 1)
    scores = dot_t(keys[...], queries[...])
    mask = mask_column[...]
    total = jnp.zeros((TOKENS, TOKENS), F32)
    gathered = jnp.zeros((TOKENS, TOKENS), F32)
    zero = jnp.zeros((), BF16)
    for pair in range(PAIRS):
        span = slice(pair * TOKENS, (pair + 1) * TOKENS)
        block = inputs[:, span]
        pulled = upstream[:, span] * mask
        stacked = jnp.concatenate(
            [jnp.where(first_half, block, zero), jnp.where(first_half, zero, block)], axis=0
        )
        products = dot_t(stacked, pulled)
        highs, lows = [], []
        for side in range(2):
            head = 2 * pair + side
            gaps = running[head : head + 1] + column(columns, head)
            mixing = jnp.where(causal, jnp.exp(gaps), 0.0)
            weighted = mixing * products[side * TOKENS : (side + 1) * TOKENS]
            total = total + weighted
            terms = weighted * scores
            row_sums[head : head + 1, :] = jnp.sum(terms, axis=0, keepdims=True)
            gathered = jnp.where(lanes == head, jnp.sum(terms, axis=1, keepdims=True), gathered)
            high, low = halves(mixing * scores)
            highs.append(high)
            lows.append(low)
        sides = jnp.concatenate(
            [jnp.where(first_half, pulled, zero), jnp.where(first_half, zero, pulled)], axis=0
        )
        near[:, span] = dot(jnp.concatenate(highs, axis=1), sides) + dot(
            jnp.concatenate(lows, axis=1), sides
        )
    mixed[...] = total
    column_sums[...] = gathered.T[:HEADS]


def owner_columns(owner, rows):
    place = owner * ROWS + iota((ROWS, TOKENS), 0)
    chosen = (lax.shift_right_logical(place, 6) == iota((ROWS, TOKENS), 1)).astype(F32)
    return dot_t(chosen, rows, HIGHEST)


def spread(columns, at):
    return jnp.broadcast_to(columns[:, at : at + 1], (ROWS, TOKENS))


def group_kernel(owner, received, group):
    reply_totals = [received[c, 3 * ROWS : 3 * ROWS + 1, :] for c in range(SLICES)]
    prompt_totals = [received[c, 3 * ROWS + 1 : 3 * ROWS + 2, :] for c in range(SLICES)]
    before, after = [], []
    sum_before = jnp.zeros((1, TOKENS), F32)
    sum_after = jnp.zeros((1, TOKENS), F32)
    for c in range(SLICES):
        before.append(sum_before)
        sum_before = sum_before + reply_totals[c]
        after.append(sum_after)
        sum_after = sum_after + prompt_totals[SLICES - 1 - c]
    pad = jnp.zeros((TOKENS - 2 * SLICES - 1, TOKENS), F32)
    logs = owner_columns(
        owner[0, 0], jnp.concatenate(before + after[::-1] + [sum_after, pad], axis=0)
    )
    factors = jnp.exp(logs)
    states = jnp.zeros((ROWS, TOKENS), F32)
    pulls = jnp.zeros((ROWS, TOKENS), F32)
    for c in range(SLICES):
        states = states + spread(factors, SLICES + c) * received[c, 2 * ROWS : 3 * ROWS, :]
        pulls = pulls + spread(factors, c) * received[c, ROWS : 2 * ROWS, :]
    group[0:ROWS, :] = states
    group[ROWS : 2 * ROWS, :] = pulls
    group[2 * ROWS : 3 * ROWS, :] = spread(logs, 2 * SLICES)
    group[3 * ROWS :, :] = jnp.broadcast_to(sum_after, (8, TOKENS))


def carry_kernel(owner, received, combined, later_groups, sent, later):
    totals = jnp.concatenate(
        [received[c, 3 * ROWS : 3 * ROWS + 1, :] for c in range(SLICES)]
        + [jnp.zeros((TOKENS - SLICES, TOKENS), F32)],
        axis=0,
    )
    factors = jnp.exp(owner_columns(owner[0, 0], totals))
    state = combined[0:ROWS, :]
    for c in range(SLICES):
        sent[c, 0:ROWS, :] = state
        state = spread(factors, c) * state + received[c, 0:ROWS, :]
    pulled = jnp.zeros((ROWS, TOKENS), F32)
    for c in range(SLICES - 1, -1, -1):
        sent[c, ROWS : 2 * ROWS, :] = pulled
        pulled = spread(factors, c) * pulled + received[c, ROWS : 2 * ROWS, :]
        sent[c, 2 * ROWS :, :] = combined[ROWS : 2 * ROWS, :]
    after = later_groups[...]
    for c in range(1, SLICES):
        row = received[c, 3 * ROWS + 1 : 3 * ROWS + 2, :]
        after = after + jnp.where(c > owner[0, 0], row, 0.0)
    later[...] = jnp.broadcast_to(after, (8, TOKENS))


def closing_kernel(
    prompt_inputs, prompt_keys, prompt_steps, reply_inputs, reply_keys, reply_queries,
    reply_steps, rate, upstream, mask_column, weight, prompt_logs, reply_logs, received, later,
    near, mixed, row_sums, column_sums,
    prompt_inputs_out, prompt_keys_out, prompt_steps_out, reply_inputs_out, reply_keys_out,
    reply_queries_out, reply_steps_out, summary,
):
    scale = weight[0, 0]
    first_half = iota((TOKENS, TOKENS), 1) < HEAD_DIM
    lanes = iota((TOKENS, TOKENS), 1)
    zero = jnp.zeros((), BF16)
    mask = mask_column[...]
    rates = rate[...]
    reply_running = reply_logs[...]
    prompt_running = prompt_logs[...]
    later_rows = jnp.broadcast_to(later[0:1, :], (TOKENS, TOKENS)).T[:HEADS]
    reply_ends = jnp.exp(reply_running[:, TOKENS - 1 :] - reply_running) * reply_steps[...]
    prompt_ends = (
        jnp.exp(prompt_running[:, TOKENS - 1 :] - prompt_running + later_rows) * prompt_steps[...]
    )
    reach = transposed(jnp.exp(reply_running) * scale)
    ends = transposed(reply_ends)
    prompt_columns = transposed(prompt_ends)

    keys = reply_keys[...]
    queries = reply_queries[...]
    own_keys = prompt_keys[...]
    keys_wide = keys.astype(F32)
    queries_wide = queries.astype(F32)
    own_wide = own_keys.astype(F32)
    keys_twice = jnp.concatenate([keys, keys], axis=1)
    own_twice = jnp.concatenate([own_keys, own_keys], axis=1)

    mixed_high, mixed_low = halves(mixed[...] * scale)
    key_total = dot(mixed_high, queries) + dot(mixed_low, queries)
    turned = (mixed[...] * scale).T
    mixed_high, mixed_low = halves(turned)
    query_total = dot(mixed_high, keys) + dot(mixed_low, keys)
    own_total = jnp.zeros((TOKENS, TOKENS), F32)
    reached = jnp.zeros((TOKENS, TOKENS), F32)
    ended = jnp.zeros((TOKENS, TOKENS), F32)
    owned = jnp.zeros((TOKENS, TOKENS), F32)
    overlaps = []

    def split(block):
        once = jnp.concatenate(
            [jnp.where(first_half, block, zero), jnp.where(first_half, zero, block)], axis=0
        )
        return jnp.concatenate([once, once], axis=1)

    def gather(base, pair):
        return jnp.concatenate(
            [
                received[owner, base + offset : base + offset + PIECE, :]
                for at, owner, offset in pieces(pair)
            ],
            axis=0,
        )

    for pair in range(PAIRS):
        span = slice(pair * TOKENS, (pair + 1) * TOKENS)
        state = gather(0, pair)
        pull = gather(ROWS, pair)
        end_pull = gather(2 * ROWS, pair)
        state_pair = halves(state)
        pull_pair = halves(pull)
        end_pair = halves(end_pull)
        shared = state * pull
        overlaps.append(jnp.sum(shared[:HEAD_DIM], axis=0, keepdims=True))
        overlaps.append(jnp.sum(shared[HEAD_DIM:], axis=0, keepdims=True))
        pulled = upstream[:, span] * mask
        block = reply_inputs[:, span]
        own = prompt_inputs[:, span]
        forward = dot(split(pulled), jnp.concatenate(state_pair, axis=0))
        backward = dot(split(block), jnp.concatenate(pull_pair, axis=0))
        own_backward = dot(split(own), jnp.concatenate(end_pair, axis=0))
        keyed = dot_t(keys_twice, jnp.concatenate(pull_pair, axis=1))
        own_keyed = dot_t(own_twice, jnp.concatenate(end_pair, axis=1))
        end_columns, own_columns = [], []
        for side in range(2):
            head = 2 * pair + side
            rows = slice(side * TOKENS, (side + 1) * TOKENS)
            part = column(reach, head) * forward[rows]
            query_total = query_total + part
            reached = jnp.where(
                lanes == head, jnp.sum(part * queries_wide, axis=1, keepdims=True), reached
            )
            end_columns.append(column(ends, head))
            part = end_columns[side] * backward[rows]
            key_total = key_total + part
            ended = jnp.where(
                lanes == head, jnp.sum(part * keys_wide, axis=1, keepdims=True), ended
            )
            own_columns.append(column(prompt_columns, head))
            part = own_columns[side] * own_backward[rows]
            own_total = own_total + part
            owned = jnp.where(
                lanes == head, jnp.sum(part * own_wide, axis=1, keepdims=True), owned
            )
        factor = jnp.where(first_half, end_columns[0], end_columns[1])
        reply_inputs_out[:, span] = (near[:, span] * scale + factor * keyed).astype(BF16)
        factor = jnp.where(first_half, own_columns[0], own_columns[1])
        prompt_inputs_out[:, span] = (factor * own_keyed).astype(BF16)

    reply_keys_out[...] = key_total.astype(BF16)
    reply_queries_out[...] = query_total.astype(BF16)
    prompt_keys_out[...] = own_total.astype(BF16)

    reached = reached.T[:HEADS]
    ended = ended.T[:HEADS]
    owned = owned.T[:HEADS]
    upper = iota((TOKENS, TOKENS), 0) >= iota((TOKENS, TOKENS), 1)
    lower = (iota((TOKENS, TOKENS), 0) < iota((TOKENS, TOKENS), 1)).astype(F32)
    carried = jnp.sum(jnp.concatenate(overlaps, axis=0), axis=1, keepdims=True)
    carried = carried * jnp.exp(reply_running[:, TOKENS - 1 :])
    closer = column_sums[...] * scale
    log_pull = (
        exact_dot(row_sums[...] * scale - closer + reached, upper.astype(F32))
        + exact_dot(ended, lower)
        + carried
    )
    steps = reply_steps[...]
    reply_steps_out[...] = (closer + ended) / steps - rates * log_pull
    decay_local = jnp.sum(-steps * rates * log_pull, axis=1, keepdims=True)
    steps = prompt_steps[...]
    log_pull = exact_dot(owned, lower)
    prompt_steps_out[...] = owned / steps - rates * log_pull
    decay_local = decay_local + jnp.sum(-steps * rates * log_pull, axis=1, keepdims=True)
    own_sum = jnp.sum(owned, axis=1, keepdims=True)
    log_sum = jnp.sum(-steps * rates, axis=1, keepdims=True)
    side_by_side = jnp.where(
        lanes[:HEADS] == 0, decay_local, jnp.where(lanes[:HEADS] == 1, own_sum, log_sum)
    )
    summary[...] = transposed(side_by_side)[0:8]


def on_device(kernel, out_shapes, smem, flops, *operands):
    spaces = [
        pl.BlockSpec(memory_space=pltpu.SMEM if at in smem else pltpu.VMEM)
        for at in range(len(operands))
    ]
    moved = sum(x.size * x.dtype.itemsize for x in operands + tuple(out_shapes))
    return pl.pallas_call(
        kernel,
        out_shape=out_shapes,
        in_specs=spaces,
        out_specs=[pl.BlockSpec(memory_space=pltpu.VMEM) for _ in out_shapes],
        compiler_params=pltpu.CompilerParams(vmem_limit_bytes=VMEM_LIMIT),
        cost_estimate=pl.CostEstimate(flops=flops, bytes_accessed=moved, transcendentals=0),
    )(*operands)


def shape(*dims, dtype=F32):
    return jax.ShapeDtypeStruct(dims, dtype)


def everywhere(block, axis):
    copies = jnp.broadcast_to(block[None], (SLICES,) + block.shape)
    return lax.all_to_all(copies, axis, 0, 0)


def per_device(
    prompt_inputs, prompt_keys, prompt_steps, reply_inputs, reply_keys, reply_queries,
    reply_steps, decay_log, upstream, loss_mask, advantage_index, advantage_table,
):
    reply_inputs, reply_keys, reply_queries = reply_inputs[0], reply_keys[0], reply_queries[0]
    reply_steps, upstream = reply_steps[0], upstream[0]
    levels = lax.broadcasted_iota(jnp.int32, advantage_table.shape, 0)
    weight = jnp.sum(jnp.where(levels == advantage_index[0], advantage_table, 0.0)).reshape(1, 1)
    rate = jnp.exp(decay_log)[:, None]
    mask_column = jnp.broadcast_to(loss_mask[0][:, None], (TOKENS, TOKENS)).astype(BF16)
    mine = lax.axis_index("ctx")
    row = lax.axis_index("rollout")
    owner = mine.astype(jnp.int32).reshape(1, 1)

    pack, prompt_logs, reply_logs = on_device(
        local_states_kernel,
        [shape(SLICES, PACK, STATE), shape(HEADS, TOKENS), shape(HEADS, TOKENS)],
        (10,),
        2 * 10**9,
        prompt_inputs, prompt_keys, prompt_steps, reply_inputs, reply_keys, reply_queries,
        reply_steps, rate, upstream, loss_mask, weight,
    )
    received = lax.all_to_all(pack, "ctx", 0, 0)
    near, mixed, row_sums, column_sums = on_device(
        within_kernel,
        [
            shape(TOKENS, CHANNELS), shape(TOKENS, TOKENS), shape(HEADS, TOKENS),
            shape(HEADS, TOKENS),
        ],
        (),
        4 * 10**9,
        reply_inputs, reply_keys, reply_queries, reply_steps, upstream, mask_column, reply_logs,
    )
    (group,) = on_device(group_kernel, [shape(PACK, STATE)], (0,), 10**8, owner, received)
    later_groups = jnp.zeros((1, STATE), F32)
    for bit in (1, 2, 4, 8):
        other = lax.ppermute(group, "rollout", [(at, at ^ bit) for at in range(SLICES)])
        early = (row & bit) == 0
        logs, other_logs = group[2 * ROWS : 3 * ROWS], other[2 * ROWS : 3 * ROWS]
        states, other_states = group[:ROWS], other[:ROWS]
        joined = jnp.where(
            early,
            jnp.exp(other_logs) * states + other_states,
            jnp.exp(logs) * other_states + states,
        )
        later_groups = later_groups + jnp.where(early, other[3 * ROWS : 3 * ROWS + 1], 0.0)
        group = jnp.concatenate([joined, group[ROWS:] + other[ROWS:]], axis=0)
    sent, later = on_device(
        carry_kernel,
        [shape(SLICES, 3 * ROWS, STATE), shape(8, STATE)],
        (0,),
        10**8,
        owner, received, group, later_groups,
    )
    returned = lax.all_to_all(sent, "ctx", 0, 0)
    results = on_device(
        closing_kernel,
        [
            shape(TOKENS, CHANNELS, dtype=BF16), shape(TOKENS, STATE, dtype=BF16),
            shape(HEADS, TOKENS), shape(TOKENS, CHANNELS, dtype=BF16),
            shape(TOKENS, STATE, dtype=BF16), shape(TOKENS, STATE, dtype=BF16),
            shape(HEADS, TOKENS), shape(8, TOKENS),
        ],
        (10,),
        4 * 10**9,
        prompt_inputs, prompt_keys, prompt_steps, reply_inputs, reply_keys, reply_queries,
        reply_steps, rate, upstream, mask_column, weight, prompt_logs, reply_logs, returned,
        later, near, mixed, row_sums, column_sums,
    )
    places = jnp.arange(SLICES)
    strictly = (places[None, :] < places[:, None]).astype(F32)

    def joined_summaries(parts):
        decays, sums, logs = parts[:, 0], parts[:, 1], parts[:, 2]
        before = jnp.sum(strictly[:, :, None] * sums[None], axis=1)
        return jnp.sum(decays + logs * before, axis=0), jnp.sum(sums, axis=0), jnp.sum(logs, axis=0), before

    decays, sums, logs, before = joined_summaries(everywhere(results[7], "ctx"))
    own_before = jnp.sum(jnp.where((places == mine)[:, None], before, 0.0), axis=0)
    block = jnp.stack([decays, sums, logs] + [jnp.zeros_like(sums)] * 5)
    decays, sums, logs, before = joined_summaries(everywhere(block, "rollout"))
    own_before = own_before + jnp.sum(jnp.where((places == row)[:, None], before, 0.0), axis=0)
    prompt_steps_out = results[2] - rate * own_before[:HEADS, None]
    return (
        results[0], results[1], prompt_steps_out, results[3][None], results[4][None],
        results[5][None], results[6][None], decays[:HEADS],
    )


def solution(mesh):
    in_specs = (
        P(("rollout", "ctx"), None),
        P(("rollout", "ctx"), None),
        P(None, ("rollout", "ctx")),
        P("rollout", "ctx", None),
        P("rollout", "ctx", None),
        P("rollout", "ctx", None),
        P("rollout", None, "ctx"),
        P(),
        P("rollout", "ctx", None),
        P("rollout", "ctx"),
        P("rollout"),
        P(),
    )
    out_specs = (
        P(("rollout", "ctx"), None),
        P(("rollout", "ctx"), None),
        P(None, ("rollout", "ctx")),
        P("rollout", "ctx", None),
        P("rollout", "ctx", None),
        P("rollout", "ctx", None),
        P("rollout", None, "ctx"),
        P(),
    )
    return jax.shard_map(
        per_device, mesh=mesh, in_specs=in_specs, out_specs=out_specs, check_vma=False
    )
```

```python
import jax
import jax.numpy as jnp
from jax import lax
from jax.experimental import pallas as pl
from jax.experimental.pallas import tpu as pltpu
from jax.sharding import PartitionSpec as P

HEADS = 40
HEAD_DIM = 64
STATE = 128
TOKENS = 128
CHANNELS = HEADS * HEAD_DIM
PAIRS = HEADS // 2
SLICES = 16
DEVICES = SLICES * SLICES
GO = 328
ROWS = CHANNELS // SLICES
PIECE = 32
PER_SLICE = ROWS // PIECE
F32 = jnp.float32
BF16 = jnp.bfloat16
HIGHEST = lax.Precision.HIGHEST
VMEM_BYTES = 56 * 1024 * 1024
BOTH = ("rollout", "ctx")


def iota(shape, axis):
    return lax.broadcasted_iota(jnp.int32, shape, axis)


def halves(value):
    high = value.astype(BF16)
    return high, (value - high.astype(F32)).astype(BF16)


def dot(left, right):
    return jnp.dot(left, right, preferred_element_type=F32)


def dot_t(left, right, precision=None):
    return lax.dot_general(
        left, right, (((1,), (1,)), ((), ())), preferred_element_type=F32, precision=precision
    )


def exact_dot(left, right):
    return jnp.dot(left, right, preferred_element_type=F32, precision=HIGHEST)


def running_logs(steps, rate):
    earlier = (iota((TOKENS, TOKENS), 0) <= iota((TOKENS, TOKENS), 1)).astype(F32)
    return exact_dot(-steps * rate, earlier)


def transposed(rows, before=0):
    parts = [rows, jnp.zeros((TOKENS - before - rows.shape[0], TOKENS), F32)]
    if before:
        parts = [jnp.zeros((before, TOKENS), F32)] + parts
    return jnp.concatenate(parts, axis=0).T


def as_columns(row):
    return jnp.broadcast_to(row, (TOKENS, TOKENS)).T


def pair_rows(rows, pair):
    first = jnp.broadcast_to(rows[2 * pair : 2 * pair + 1], (HEAD_DIM, TOKENS))
    second = jnp.broadcast_to(rows[2 * pair + 1 : 2 * pair + 2], (HEAD_DIM, TOKENS))
    return jnp.concatenate([first, second], axis=0)


def column(columns, head):
    return jnp.broadcast_to(columns[:, head : head + 1], (TOKENS, TOKENS))


def pieces(pair):
    for part in range(4):
        place = 4 * pair + part
        yield part * PIECE, place // PER_SLICE, (place % PER_SLICE) * PIECE


def first_lanes():
    return iota((TOKENS, TOKENS), 1) < HEAD_DIM


def sides(block):
    zero = jnp.zeros((), BF16)
    half = first_lanes()
    return jnp.concatenate([jnp.where(half, block, zero), jnp.where(half, zero, block)], axis=0)


def span(pair):
    return slice(pair * TOKENS, (pair + 1) * TOKENS)


def gather(received, pair):
    return jnp.concatenate(
        [received[owner, offset : offset + PIECE, :] for at, owner, offset in pieces(pair)], axis=0
    )


def pack_states(pack, base, tokens, rows, keys):
    twice = jnp.concatenate([keys, keys], axis=0)
    for pair in range(PAIRS):
        block = tokens[:, span(pair)].astype(F32).T
        high, low = halves(block * pair_rows(rows, pair))
        states = dot(jnp.concatenate([high, low], axis=1), twice)
        for at, owner, offset in pieces(pair):
            pack[owner, base + offset : base + offset + PIECE, :] = states[at : at + PIECE]


def first_kernel(
    weight, prompt_inputs, prompt_keys, prompt_steps, queries, reply_steps, rate, upstream, mask,
    pack, reply_logs, prompt_logs,
):
    reply_running = running_logs(reply_steps[...], rate[...])
    prompt_running = running_logs(prompt_steps[...], rate[...])
    reply_logs[...] = reply_running
    prompt_logs[...] = prompt_running
    reply_last = jnp.broadcast_to(reply_running[:, TOKENS - 1 :], (HEADS, TOKENS))
    prompt_last = jnp.broadcast_to(prompt_running[:, TOKENS - 1 :], (HEADS, TOKENS))
    totals = jnp.concatenate(
        [transposed(reply_last)[0:1], transposed(prompt_last)[0:1], jnp.zeros((6, TOKENS), F32)],
        axis=0,
    )
    for owner in range(SLICES):
        pack[owner, 2 * ROWS :, :] = totals
    rows = jnp.exp(reply_running) * (mask[...].astype(F32) * weight[0, 0])
    pack_states(pack, 0, upstream, rows, queries[...])
    rows = jnp.exp(prompt_last - prompt_running) * prompt_steps[...]
    pack_states(pack, ROWS, prompt_inputs, rows, prompt_keys[...])


def second_kernel(inputs, keys, steps, logs, pack):
    running = logs[...]
    rows = jnp.exp(running[:, TOKENS - 1 :] - running) * steps[...]
    pack_states(pack, 0, inputs, rows, keys[...])


def within_kernel(
    inputs, keys, queries, steps, upstream, mask_row, logs, near, mixed, row_sums, column_sums
):
    running = logs[...]
    columns = transposed(jnp.log(steps[...]) - running)
    causal = iota((TOKENS, TOKENS), 1) >= iota((TOKENS, TOKENS), 0)
    lanes = iota((TOKENS, TOKENS), 1)
    scores = dot_t(keys[...], queries[...])
    mask = as_columns(mask_row[...].astype(F32)).astype(BF16)
    total = jnp.zeros((TOKENS, TOKENS), F32)
    gathered = jnp.zeros((TOKENS, TOKENS), F32)
    for pair in range(PAIRS):
        pulled = upstream[:, span(pair)] * mask
        products = dot_t(sides(inputs[:, span(pair)]), pulled)
        highs, lows = [], []
        for side in range(2):
            head = 2 * pair + side
            gaps = running[head : head + 1] + column(columns, head)
            mixing = jnp.where(causal, jnp.exp(gaps), 0.0)
            weighted = mixing * products[side * TOKENS : (side + 1) * TOKENS]
            total = total + weighted
            terms = weighted * scores
            row_sums[head : head + 1, :] = jnp.sum(terms, axis=0, keepdims=True)
            gathered = jnp.where(lanes == head, jnp.sum(terms, axis=1, keepdims=True), gathered)
            high, low = halves(mixing * scores)
            highs.append(high)
            lows.append(low)
        both = sides(pulled)
        near[:, span(pair)] = dot(jnp.concatenate(highs, axis=1), both) + dot(
            jnp.concatenate(lows, axis=1), both
        )
    mixed[...] = total
    column_sums[...] = gathered.T[:HEADS]


def spread(columns, at):
    return jnp.broadcast_to(columns[:, at : at + 1], (ROWS, TOKENS))


def owner_columns(owner, rows):
    place = owner * ROWS + iota((ROWS, TOKENS), 0)
    chosen = (lax.shift_right_logical(place, 6) == iota((ROWS, TOKENS), 1)).astype(F32)
    pad = jnp.zeros((TOKENS - rows.shape[0], TOKENS), F32)
    return dot_t(chosen, jnp.concatenate([rows, pad], axis=0), HIGHEST)


def group_kernel(owner, received, after, joint, totals):
    reply = jnp.concatenate(
        [received[c, 2 * ROWS : 2 * ROWS + 1, :] for c in range(SLICES)], axis=0
    )
    prompt = jnp.concatenate(
        [received[c, 2 * ROWS + 1 : 2 * ROWS + 2, :] for c in range(SLICES)], axis=0
    )
    totals[0:SLICES, :] = reply
    totals[SLICES:, :] = prompt
    group = jnp.sum(prompt, axis=0, keepdims=True)
    logs = owner_columns(owner[0, 0], jnp.concatenate([reply, prompt, group], axis=0))
    factors = jnp.exp(logs)
    pulled = jnp.zeros((ROWS, TOKENS), F32)
    state = jnp.zeros((ROWS, TOKENS), F32)
    for c in range(SLICES):
        back = SLICES - 1 - c
        after[back] = pulled
        pulled = spread(factors, back) * pulled + received[back, 0:ROWS, :]
        state = spread(factors, SLICES + c) * state + received[c, ROWS : 2 * ROWS, :]
    joint[0:ROWS, :] = state
    joint[ROWS : 2 * ROWS, :] = pulled
    joint[2 * ROWS : 3 * ROWS, :] = spread(logs, 2 * SLICES)
    joint[3 * ROWS :, :] = jnp.broadcast_to(group, (8, TOKENS))


def carry_kernel(owner, totals, received, joint, starts):
    factors = jnp.exp(owner_columns(owner[0, 0], totals[0:SLICES, :]))
    state = joint[0:ROWS, :]
    for c in range(SLICES):
        starts[c] = state
        if c < SLICES - 1:
            state = spread(factors, c) * state + received[c]


def backward_parts(inputs, pulls, ends, keys, near, scale, inputs_out):
    twice = jnp.concatenate([keys, keys], axis=1)
    wide = keys.astype(F32)
    lanes = iota((TOKENS, TOKENS), 1)
    half = first_lanes()
    total = jnp.zeros((TOKENS, TOKENS), F32)
    gathered = jnp.zeros((TOKENS, TOKENS), F32)
    columns = transposed(ends)
    for pair in range(PAIRS):
        high, low = halves(gather(pulls, pair))
        once = sides(inputs[:, span(pair)])
        backward = dot(
            jnp.concatenate([once, once], axis=1), jnp.concatenate([high, low], axis=0)
        )
        keyed = dot_t(twice, jnp.concatenate([high, low], axis=1))
        factors = []
        for side in range(2):
            head = 2 * pair + side
            factors.append(column(columns, head))
            part = factors[side] * backward[side * TOKENS : (side + 1) * TOKENS]
            total = total + part
            gathered = jnp.where(
                lanes == head, jnp.sum(part * wide, axis=1, keepdims=True), gathered
            )
        own = jnp.where(half, factors[0], factors[1]) * keyed
        if near is not None:
            own = near[:, span(pair)] * scale + own
        inputs_out[:, span(pair)] = own.astype(BF16)
    return total, gathered.T[:HEADS]


def reply_backward_kernel(
    weight, inputs, keys, queries, steps, logs, pulls, near, mixed, inputs_out, keys_out, ended_out
):
    scale = weight[0, 0]
    running = logs[...]
    ends = jnp.exp(running[:, TOKENS - 1 :] - running) * steps[...]
    total, ended = backward_parts(inputs, pulls, ends, keys[...], near, scale, inputs_out)
    high, low = halves(mixed[...] * scale)
    total = total + dot(high, queries[...]) + dot(low, queries[...])
    keys_out[...] = total.astype(BF16)
    ended_out[...] = ended


def log_sums(rows):
    lower = (iota((TOKENS, TOKENS), 0) < iota((TOKENS, TOKENS), 1)).astype(F32)
    return exact_dot(rows, lower)


def prompt_backward_kernel(
    owner, inputs, keys, steps, rate, logs, totals, later_groups, pulls,
    inputs_out, keys_out, owned_out, decay,
):
    later = later_groups[...]
    for c in range(1, SLICES):
        row = totals[SLICES + c : SLICES + c + 1, :]
        later = later + jnp.where(c > owner[0, 0], row, 0.0)
    running = logs[...]
    ends = jnp.exp(running[:, TOKENS - 1 :] - running + as_columns(later)[:HEADS]) * steps[...]
    total, owned = backward_parts(inputs, pulls, ends, keys[...], None, None, inputs_out)
    keys_out[...] = total.astype(BF16)
    owned_out[...] = owned
    inside = jnp.sum(-steps[...] * rate[...] * log_sums(owned), axis=1, keepdims=True)
    sums = jnp.sum(owned, axis=1, keepdims=True)
    logs_whole = running[:, TOKENS - 1 :]
    stacked = jnp.broadcast_to(
        jnp.concatenate([inside, sums, logs_whole], axis=0), (3 * HEADS, TOKENS)
    )
    decay[...] = transposed(stacked)[0:8]


def reply_forward_kernel(
    weight, keys, queries, steps, rate, upstream, mask_row, logs, starts, pulls, mixed,
    row_sums, column_sums, ended, prompt_decay, queries_out, steps_out, summary,
):
    scale = weight[0, 0]
    running = logs[...]
    reach = transposed(jnp.exp(running) * scale)
    mask = as_columns(mask_row[...].astype(F32)).astype(BF16)
    lanes = iota((TOKENS, TOKENS), 1)
    wide = queries[...].astype(F32)
    total = jnp.zeros((TOKENS, TOKENS), F32)
    reached = jnp.zeros((TOKENS, TOKENS), F32)
    overlaps = []
    for pair in range(PAIRS):
        state = gather(starts, pair)
        shared = state * gather(pulls, pair)
        overlaps.append(jnp.sum(shared[:HEAD_DIM], axis=0, keepdims=True))
        overlaps.append(jnp.sum(shared[HEAD_DIM:], axis=0, keepdims=True))
        high, low = halves(state)
        once = sides(upstream[:, span(pair)] * mask)
        forward = dot(
            jnp.concatenate([once, once], axis=1), jnp.concatenate([high, low], axis=0)
        )
        for side in range(2):
            head = 2 * pair + side
            part = column(reach, head) * forward[side * TOKENS : (side + 1) * TOKENS]
            total = total + part
            reached = jnp.where(
                lanes == head, jnp.sum(part * wide, axis=1, keepdims=True), reached
            )
    high, low = halves((mixed[...] * scale).T)
    total = total + dot(high, keys[...]) + dot(low, keys[...])
    queries_out[...] = total.astype(BF16)
    reached = reached.T[:HEADS]
    later = (iota((TOKENS, TOKENS), 0) >= iota((TOKENS, TOKENS), 1)).astype(F32)
    carried = jnp.sum(jnp.concatenate(overlaps, axis=0), axis=1, keepdims=True)
    carried = carried * jnp.exp(running[:, TOKENS - 1 :])
    closer = column_sums[...] * scale
    log_pull = (
        exact_dot(row_sums[...] * scale - closer + reached, later) + log_sums(ended[...]) + carried
    )
    steps_out[...] = (closer + ended[...]) / steps[...] - rate[...] * log_pull
    local = jnp.sum(-steps[...] * rate[...] * log_pull, axis=1, keepdims=True)
    row = transposed(jnp.broadcast_to(local, (HEADS, TOKENS)))[0:1] + prompt_decay[0:1]
    summary[...] = jnp.broadcast_to(row, (DEVICES, TOKENS))


def moved_lanes(rows, by):
    shift = (iota((TOKENS, TOKENS), 0) == iota((TOKENS, TOKENS), 1) + by).astype(F32)
    return exact_dot(rows, shift)


def finish_kernel(place, received, owned, steps, rate, steps_out, decay):
    rows = received[...]
    below = (iota((DEVICES, DEVICES), 0) > iota((DEVICES, DEVICES), 1)).astype(F32)
    before = exact_dot(below, moved_lanes(rows, HEADS))
    decay_rows = rows + before * moved_lanes(rows, 2 * HEADS)
    decay[...] = jnp.broadcast_to(jnp.sum(decay_rows, axis=0, keepdims=True), (8, TOKENS))
    mine = jnp.where(iota((DEVICES, TOKENS), 0) < place[0, 0], rows, 0.0)
    mine = as_columns(jnp.sum(mine, axis=0, keepdims=True))[HEADS : 2 * HEADS]
    steps_out[...] = owned[...] / steps[...] - rate[...] * (log_sums(owned[...]) + mine)


def whole(dims):
    return pl.BlockSpec(dims, lambda step: (0,) * len(dims))


def on_device(kernel, out_shapes, scalars, flops, *operands):
    specs = [pl.BlockSpec(memory_space=pltpu.SMEM) for _ in range(scalars)]
    specs += [whole(x.shape) for x in operands[scalars:]]
    moved = sum(x.size * x.dtype.itemsize for x in operands + tuple(out_shapes))
    return pl.pallas_call(
        kernel,
        grid=(1,),
        out_shape=out_shapes,
        in_specs=specs,
        out_specs=[whole(x.shape) for x in out_shapes],
        compiler_params=pltpu.CompilerParams(vmem_limit_bytes=VMEM_BYTES),
        cost_estimate=pl.CostEstimate(flops=flops, bytes_accessed=moved, transcendentals=0),
    )(*operands)


def shape(*dims, dtype=F32):
    return jax.ShapeDtypeStruct(dims, dtype)


def swap(value, axis):
    return lax.all_to_all(value, axis, 0, 0, tiled=True)


def turn(block):
    pairs = [(a * SLICES + b, b * SLICES + a) for a in range(SLICES) for b in range(SLICES)]
    return lax.ppermute(block, BOTH, pairs)


def per_device(
    prompt_inputs, prompt_keys, prompt_steps, reply_inputs, reply_keys, reply_queries,
    reply_steps, decay_log, upstream, loss_mask, advantage_index, advantage_table,
):
    reply_inputs, reply_keys, reply_queries = reply_inputs[0], reply_keys[0], reply_queries[0]
    reply_steps, upstream = reply_steps[0], upstream[0]
    levels = lax.broadcasted_iota(jnp.int32, advantage_table.shape, 0)
    weight = jnp.sum(jnp.where(levels == advantage_index[0], advantage_table, 0.0)).reshape(1, 1)
    rate = jnp.exp(decay_log)[:, None]
    row, mine = lax.axis_index("rollout"), lax.axis_index("ctx")
    place = (row * SLICES + mine).astype(jnp.int32).reshape(1, 1)
    owner = mine.astype(jnp.int32).reshape(1, 1)
    slices = shape(SLICES, ROWS, STATE)
    heads = shape(HEADS, TOKENS)
    square = shape(TOKENS, TOKENS)
    wide = shape(TOKENS, CHANNELS, dtype=BF16)
    narrow = shape(TOKENS, STATE, dtype=BF16)

    pack, reply_logs, prompt_logs = on_device(
        first_kernel, [shape(SLICES, GO, STATE), heads, heads], 1, 4 * 10**9,
        weight, prompt_inputs, prompt_keys, prompt_steps, reply_queries, reply_steps, rate,
        upstream, loss_mask,
    )
    received = swap(pack, "ctx")
    (states,) = on_device(
        second_kernel, [slices], 0, 2 * 10**9, reply_inputs, reply_keys, reply_steps, reply_logs
    )
    states = swap(states, "ctx")
    near, mixed, row_sums, column_sums = on_device(
        within_kernel, [shape(TOKENS, CHANNELS), square, heads, heads], 0, 6 * 10**9,
        reply_inputs, reply_keys, reply_queries, reply_steps, upstream, loss_mask, reply_logs,
    )
    after, joint, totals = on_device(
        group_kernel, [slices, shape(3 * ROWS + 8, STATE), shape(2 * SLICES, STATE)], 1,
        3 * 10**9, owner, received,
    )
    after = swap(after, "ctx")
    later_groups = jnp.zeros((1, STATE), F32)
    for bit in (1, 2, 4, 8):
        other = lax.ppermute(joint, "rollout", [(at, at ^ bit) for at in range(SLICES)])
        early = (row & bit) == 0
        logs, other_logs = joint[2 * ROWS : 3 * ROWS], other[2 * ROWS : 3 * ROWS]
        ours, others = joint[:ROWS], other[:ROWS]
        joined = jnp.where(
            early, jnp.exp(other_logs) * ours + others, jnp.exp(logs) * others + ours
        )
        later_groups = later_groups + jnp.where(early, other[3 * ROWS : 3 * ROWS + 1], 0.0)
        joint = jnp.concatenate([joined, joint[ROWS:] + other[ROWS:]], axis=0)
    (starts,) = on_device(
        carry_kernel, [slices], 1, 3 * 10**9, owner, totals, states, joint
    )
    starts = swap(starts, "ctx")
    end_pull = lax.all_gather(turn(joint[ROWS : 2 * ROWS]), "rollout")
    reply_inputs_out, reply_keys_out, ended = on_device(
        reply_backward_kernel, [wide, narrow, heads], 1, 6 * 10**9,
        weight, reply_inputs, reply_keys, reply_queries, reply_steps, reply_logs, after, near,
        mixed,
    )
    prompt_inputs_out, prompt_keys_out, owned, prompt_decay = on_device(
        prompt_backward_kernel, [wide, narrow, heads, shape(8, TOKENS)], 1, 6 * 10**9,
        owner, prompt_inputs, prompt_keys, prompt_steps, rate, prompt_logs, totals, later_groups,
        end_pull,
    )
    reply_queries_out, reply_steps_out, summary = on_device(
        reply_forward_kernel, [narrow, heads, shape(DEVICES, TOKENS)], 1, 6 * 10**9,
        weight, reply_keys, reply_queries, reply_steps, rate, upstream, loss_mask, reply_logs,
        starts, after, mixed, row_sums, column_sums, ended, prompt_decay,
    )
    prompt_steps_out, decay = on_device(
        finish_kernel, [heads, shape(8, TOKENS)], 1, 10**8,
        place, swap(summary, BOTH), owned, prompt_steps, rate,
    )
    return (
        prompt_inputs_out, prompt_keys_out, prompt_steps_out, reply_inputs_out[None],
        reply_keys_out[None], reply_queries_out[None], reply_steps_out[None], decay[0, :HEADS],
    )


def solution(mesh):
    in_specs = (
        P(("rollout", "ctx"), None),
        P(("rollout", "ctx"), None),
        P(None, ("rollout", "ctx")),
        P("rollout", "ctx", None),
        P("rollout", "ctx", None),
        P("rollout", "ctx", None),
        P("rollout", None, "ctx"),
        P(),
        P("rollout", "ctx", None),
        P("rollout", "ctx"),
        P("rollout"),
        P(),
    )
    out_specs = (
        P(("rollout", "ctx"), None),
        P(("rollout", "ctx"), None),
        P(None, ("rollout", "ctx")),
        P("rollout", "ctx", None),
        P("rollout", "ctx", None),
        P("rollout", "ctx", None),
        P("rollout", None, "ctx"),
        P(),
    )
    return jax.shard_map(
        per_device, mesh=mesh, in_specs=in_specs, out_specs=out_specs, check_vma=False
    )
```

```python
import jax
import jax.numpy as jnp
from jax import lax
from jax.experimental import pallas as pl
from jax.experimental.pallas import tpu as pltpu
from jax.sharding import PartitionSpec as P

HEADS = 40
HEAD_DIM = 64
STATE = 128
TOKENS = 128
CHANNELS = HEADS * HEAD_DIM
PAIRS = HEADS // 2
SLICES = 16
DEVICES = SLICES * SLICES
GO = 328
ROWS = CHANNELS // SLICES
PIECE = 32
PER_SLICE = ROWS // PIECE
F32 = jnp.float32
BF16 = jnp.bfloat16
HIGHEST = lax.Precision.HIGHEST
VMEM_BYTES = 56 * 1024 * 1024
BOTH = ("rollout", "ctx")


def iota(shape, axis):
    return lax.broadcasted_iota(jnp.int32, shape, axis)


def halves(value):
    high = value.astype(BF16)
    return high, (value - high.astype(F32)).astype(BF16)


def dot(left, right):
    return jnp.dot(left, right, preferred_element_type=F32)


def dot_t(left, right, precision=None):
    return lax.dot_general(
        left, right, (((1,), (1,)), ((), ())), preferred_element_type=F32, precision=precision
    )


def exact_dot(left, right):
    return jnp.dot(left, right, preferred_element_type=F32, precision=HIGHEST)


def running_logs(steps, rate):
    earlier = (iota((TOKENS, TOKENS), 0) <= iota((TOKENS, TOKENS), 1)).astype(F32)
    return exact_dot(-steps * rate, earlier)


def transposed(rows, before=0):
    parts = [rows, jnp.zeros((TOKENS - before - rows.shape[0], TOKENS), F32)]
    if before:
        parts = [jnp.zeros((before, TOKENS), F32)] + parts
    return jnp.concatenate(parts, axis=0).T


def as_columns(row):
    return jnp.broadcast_to(row, (TOKENS, TOKENS)).T


def pair_rows(rows, pair):
    first = jnp.broadcast_to(rows[2 * pair : 2 * pair + 1], (HEAD_DIM, TOKENS))
    second = jnp.broadcast_to(rows[2 * pair + 1 : 2 * pair + 2], (HEAD_DIM, TOKENS))
    return jnp.concatenate([first, second], axis=0)


def column(columns, head):
    return jnp.broadcast_to(columns[:, head : head + 1], (TOKENS, TOKENS))


def pieces(pair):
    for part in range(4):
        place = 4 * pair + part
        yield part * PIECE, place // PER_SLICE, (place % PER_SLICE) * PIECE


def first_lanes():
    return iota((TOKENS, TOKENS), 1) < HEAD_DIM


def sides(block):
    zero = jnp.zeros((), BF16)
    half = first_lanes()
    return jnp.concatenate([jnp.where(half, block, zero), jnp.where(half, zero, block)], axis=0)


def span(pair):
    return slice(pair * TOKENS, (pair + 1) * TOKENS)


def gather(received, pair):
    return jnp.concatenate(
        [received[owner, offset : offset + PIECE, :] for at, owner, offset in pieces(pair)], axis=0
    )


def pack_states(pack, base, tokens, rows, keys):
    twice = jnp.concatenate([keys, keys], axis=0)
    for pair in range(PAIRS):
        block = tokens[:, span(pair)].astype(F32).T
        high, low = halves(block * pair_rows(rows, pair))
        states = dot(jnp.concatenate([high, low], axis=1), twice)
        for at, owner, offset in pieces(pair):
            pack[owner, base + offset : base + offset + PIECE, :] = states[at : at + PIECE]


def rates(decay_log):
    heads = iota((HEADS, TOKENS), 0)
    logs = jnp.zeros((HEADS, TOKENS), F32)
    for head in range(HEADS):
        logs = jnp.where(heads == head, decay_log[head], logs)
    return jnp.exp(logs)


def first_kernel(
    decay_log, index, table, prompt_steps, inputs, keys, queries, steps, upstream, mask,
    pack, reply_logs, prompt_logs, prompt_total,
):
    rate = rates(decay_log)
    running = running_logs(steps[...], rate)
    reply_logs[...] = running
    prompt_running = running_logs(prompt_steps[...], rate)
    prompt_logs[...] = prompt_running
    last = jnp.broadcast_to(prompt_running[:, TOKENS - 1 :], (HEADS, TOKENS))
    prompt_total[...] = transposed(last)[0:8]
    last = jnp.broadcast_to(running[:, TOKENS - 1 :], (HEADS, TOKENS))
    total = transposed(last)[0:8]
    for owner in range(SLICES):
        pack[owner, 2 * ROWS :, :] = total
    rows = jnp.exp(running) * (mask[...].astype(F32) * table[index[0]])
    pack_states(pack, 0, upstream, rows, queries[...])
    rows = jnp.exp(last - running) * steps[...]
    pack_states(pack, ROWS, inputs, rows, keys[...])


def prompt_states_kernel(inputs, keys, steps, logs, later, pack, ends):
    running = logs[...]
    after = as_columns(later[0:1, :])[:HEADS]
    rows = jnp.exp(running[:, TOKENS - 1 :] - running + after) * steps[...]
    ends[...] = rows
    pack_states(pack, 0, inputs, rows, keys[...])


def within_kernel(
    inputs, keys, queries, steps, upstream, mask_row, logs, near, mixed, row_sums, column_sums
):
    running = logs[...]
    columns = transposed(jnp.log(steps[...]) - running)
    causal = iota((TOKENS, TOKENS), 1) >= iota((TOKENS, TOKENS), 0)
    lanes = iota((TOKENS, TOKENS), 1)
    scores = dot_t(keys[...], queries[...])
    mask = as_columns(mask_row[...].astype(F32)).astype(BF16)
    total = jnp.zeros((TOKENS, TOKENS), F32)
    gathered = jnp.zeros((TOKENS, TOKENS), F32)
    for pair in range(PAIRS):
        pulled = upstream[:, span(pair)] * mask
        products = dot_t(sides(inputs[:, span(pair)]), pulled)
        highs, lows = [], []
        for side in range(2):
            head = 2 * pair + side
            gaps = running[head : head + 1] + column(columns, head)
            mixing = jnp.where(causal, jnp.exp(gaps), 0.0)
            weighted = mixing * products[side * TOKENS : (side + 1) * TOKENS]
            total = total + weighted
            terms = weighted * scores
            row_sums[head : head + 1, :] = jnp.sum(terms, axis=0, keepdims=True)
            gathered = jnp.where(lanes == head, jnp.sum(terms, axis=1, keepdims=True), gathered)
            high, low = halves(mixing * scores)
            highs.append(high)
            lows.append(low)
        both = sides(pulled)
        near[:, span(pair)] = dot(jnp.concatenate(highs, axis=1), both) + dot(
            jnp.concatenate(lows, axis=1), both
        )
    mixed[...] = total
    column_sums[...] = gathered.T[:HEADS]


def spread(columns, at):
    return jnp.broadcast_to(columns[:, at : at + 1], (ROWS, TOKENS))


def owner_columns(owner, rows):
    place = owner * ROWS + iota((ROWS, TOKENS), 0)
    chosen = (lax.shift_right_logical(place, 6) == iota((ROWS, TOKENS), 1)).astype(F32)
    pad = jnp.zeros((TOKENS - rows.shape[0], TOKENS), F32)
    return dot_t(chosen, jnp.concatenate([rows, pad], axis=0), HIGHEST)


def group_kernel(owner, received, after, start, totals):
    reply = jnp.concatenate(
        [received[c, 2 * ROWS : 2 * ROWS + 1, :] for c in range(SLICES)], axis=0
    )
    totals[...] = reply
    factors = jnp.exp(owner_columns(owner[0, 0], reply))
    pulled = jnp.zeros((ROWS, TOKENS), F32)
    for c in range(SLICES - 1, -1, -1):
        after[c] = pulled
        pulled = spread(factors, c) * pulled + received[c, 0:ROWS, :]
    start[...] = pulled


def carry_kernel(owner, totals, received, end_state, starts):
    factors = jnp.exp(owner_columns(owner[0, 0], totals[...]))
    state = end_state[...]
    for c in range(SLICES):
        starts[c] = state
        if c < SLICES - 1:
            state = spread(factors, c) * state + received[c, ROWS : 2 * ROWS, :]


def backward_parts(inputs, pulls, ends, keys, near, scale, inputs_out):
    twice = jnp.concatenate([keys, keys], axis=1)
    wide = keys.astype(F32)
    lanes = iota((TOKENS, TOKENS), 1)
    half = first_lanes()
    total = jnp.zeros((TOKENS, TOKENS), F32)
    gathered = jnp.zeros((TOKENS, TOKENS), F32)
    columns = transposed(ends)
    for pair in range(PAIRS):
        high, low = halves(gather(pulls, pair))
        once = sides(inputs[:, span(pair)])
        backward = dot(
            jnp.concatenate([once, once], axis=1), jnp.concatenate([high, low], axis=0)
        )
        keyed = dot_t(twice, jnp.concatenate([high, low], axis=1))
        factors = []
        for side in range(2):
            head = 2 * pair + side
            factors.append(column(columns, head))
            part = factors[side] * backward[side * TOKENS : (side + 1) * TOKENS]
            total = total + part
            gathered = jnp.where(
                lanes == head, jnp.sum(part * wide, axis=1, keepdims=True), gathered
            )
        own = jnp.where(half, factors[0], factors[1]) * keyed
        if near is not None:
            own = near[:, span(pair)] * scale + own
        inputs_out[:, span(pair)] = own.astype(BF16)
    return total, gathered.T[:HEADS]


def reply_backward_kernel(
    index, table, inputs, keys, queries, steps, logs, pulls, near, mixed, inputs_out, keys_out, ended_out
):
    scale = table[index[0]]
    running = logs[...]
    ends = jnp.exp(running[:, TOKENS - 1 :] - running) * steps[...]
    total, ended = backward_parts(inputs, pulls, ends, keys[...], near, scale, inputs_out)
    high, low = halves(mixed[...] * scale)
    total = total + dot(high, queries[...]) + dot(low, queries[...])
    keys_out[...] = total.astype(BF16)
    ended_out[...] = ended


def log_sums(rows):
    lower = (iota((TOKENS, TOKENS), 0) < iota((TOKENS, TOKENS), 1)).astype(F32)
    return exact_dot(rows, lower)


def prompt_backward_kernel(
    decay_log, inputs, keys, steps, logs, ends, pulls, inputs_out, keys_out, owned_out, decay
):
    rate = rates(decay_log)
    total, owned = backward_parts(inputs, pulls, ends[...], keys[...], None, None, inputs_out)
    keys_out[...] = total.astype(BF16)
    owned_out[...] = owned
    inside = jnp.sum(-steps[...] * rate * log_sums(owned), axis=1, keepdims=True)
    sums = jnp.sum(owned, axis=1, keepdims=True)
    stacked = jnp.broadcast_to(
        jnp.concatenate([inside, sums, logs[:, TOKENS - 1 :]], axis=0), (3 * HEADS, TOKENS)
    )
    decay[...] = transposed(stacked)[0:8]


def reply_forward_kernel(
    decay_log, index, table, keys, queries, steps, upstream, mask_row, logs, starts, pulls, mixed,
    row_sums, column_sums, ended, prompt_decay, queries_out, steps_out, summary,
):
    scale = table[index[0]]
    running = logs[...]
    rate = rates(decay_log)
    reach = transposed(jnp.exp(running) * scale)
    mask = as_columns(mask_row[...].astype(F32)).astype(BF16)
    lanes = iota((TOKENS, TOKENS), 1)
    wide = queries[...].astype(F32)
    total = jnp.zeros((TOKENS, TOKENS), F32)
    reached = jnp.zeros((TOKENS, TOKENS), F32)
    overlaps = []
    for pair in range(PAIRS):
        state = gather(starts, pair)
        shared = state * gather(pulls, pair)
        overlaps.append(jnp.sum(shared[:HEAD_DIM], axis=0, keepdims=True))
        overlaps.append(jnp.sum(shared[HEAD_DIM:], axis=0, keepdims=True))
        high, low = halves(state)
        once = sides(upstream[:, span(pair)] * mask)
        forward = dot(
            jnp.concatenate([once, once], axis=1), jnp.concatenate([high, low], axis=0)
        )
        for side in range(2):
            head = 2 * pair + side
            part = column(reach, head) * forward[side * TOKENS : (side + 1) * TOKENS]
            total = total + part
            reached = jnp.where(
                lanes == head, jnp.sum(part * wide, axis=1, keepdims=True), reached
            )
    high, low = halves((mixed[...] * scale).T)
    total = total + dot(high, keys[...]) + dot(low, keys[...])
    queries_out[...] = total.astype(BF16)
    reached = reached.T[:HEADS]
    later = (iota((TOKENS, TOKENS), 0) >= iota((TOKENS, TOKENS), 1)).astype(F32)
    carried = jnp.sum(jnp.concatenate(overlaps, axis=0), axis=1, keepdims=True)
    carried = carried * jnp.exp(running[:, TOKENS - 1 :])
    closer = column_sums[...] * scale
    log_pull = (
        exact_dot(row_sums[...] * scale - closer + reached, later) + log_sums(ended[...]) + carried
    )
    steps_out[...] = (closer + ended[...]) / steps[...] - rate * log_pull
    local = jnp.sum(-steps[...] * rate * log_pull, axis=1, keepdims=True)
    row = transposed(jnp.broadcast_to(local, (HEADS, TOKENS)))[0:1] + prompt_decay[0:1]
    summary[...] = jnp.broadcast_to(row, (DEVICES, TOKENS))


def moved_lanes(rows, by):
    shift = (iota((TOKENS, TOKENS), 0) == iota((TOKENS, TOKENS), 1) + by).astype(F32)
    return exact_dot(rows, shift)


def finish_kernel(place, decay_log, received, owned, steps, steps_out, decay):
    rows = received[...]
    below = (iota((DEVICES, DEVICES), 0) > iota((DEVICES, DEVICES), 1)).astype(F32)
    before = exact_dot(below, moved_lanes(rows, HEADS))
    decay_rows = rows + before * moved_lanes(rows, 2 * HEADS)
    decay[...] = jnp.broadcast_to(jnp.sum(decay_rows, axis=0, keepdims=True), (8, TOKENS))
    mine = jnp.where(iota((DEVICES, TOKENS), 0) < place[0, 0], rows, 0.0)
    mine = as_columns(jnp.sum(mine, axis=0, keepdims=True))[HEADS : 2 * HEADS]
    steps_out[...] = owned[...] / steps[...] - rates(decay_log) * (log_sums(owned[...]) + mine)


def whole(dims):
    return pl.BlockSpec(dims, lambda step: (0,) * len(dims))


def on_device(kernel, out_shapes, scalars, flops, *operands):
    specs = [pl.BlockSpec(memory_space=pltpu.SMEM) for _ in range(scalars)]
    specs += [whole(x.shape) for x in operands[scalars:]]
    moved = sum(x.size * x.dtype.itemsize for x in operands + tuple(out_shapes))
    return pl.pallas_call(
        kernel,
        grid=(1,),
        out_shape=out_shapes,
        in_specs=specs,
        out_specs=[whole(x.shape) for x in out_shapes],
        compiler_params=pltpu.CompilerParams(vmem_limit_bytes=VMEM_BYTES),
        cost_estimate=pl.CostEstimate(flops=flops, bytes_accessed=moved, transcendentals=0),
    )(*operands)


def shape(*dims, dtype=F32):
    return jax.ShapeDtypeStruct(dims, dtype)


def swap(value, axis):
    return lax.all_to_all(value, axis, 0, 0, tiled=True)


def turn(block):
    pairs = [(a * SLICES + b, b * SLICES + a) for a in range(SLICES) for b in range(SLICES)]
    return lax.ppermute(block, BOTH, pairs)


def traded(value, axis, bit):
    return lax.ppermute(value, axis, [(at, at ^ bit) for at in range(SLICES)])


def later_sums(total, row, mine):
    later = jnp.zeros_like(total)
    for axis, place in (("ctx", mine), ("rollout", row)):
        for bit in (1, 2, 4, 8):
            other = traded(total, axis, bit)
            later = later + jnp.where((place & bit) == 0, other, 0.0)
            total = total + other
    return later


def reduced_over_rows(states, row):
    for bit in (1, 2, 4, 8):
        side = ((row & bit) != 0).astype(jnp.int32)
        split = states.reshape((states.shape[0] // 2, 2) + states.shape[1:])
        given = lax.dynamic_index_in_dim(split, 1 - side, 1, keepdims=False)
        kept = lax.dynamic_index_in_dim(split, side, 1, keepdims=False)
        states = kept + traded(given, "rollout", bit)
    return states[0]


def gathered_over_rows(block, row):
    parts = block[None]
    for bit in (8, 4, 2, 1):
        other = traded(parts, "rollout", bit)
        low = (row & bit) == 0
        first, second = jnp.where(low, parts, other), jnp.where(low, other, parts)
        parts = jnp.stack([first, second], axis=1).reshape((-1,) + block.shape)
    return parts


def per_device(
    prompt_inputs, prompt_keys, prompt_steps, reply_inputs, reply_keys, reply_queries,
    reply_steps, decay_log, upstream, loss_mask, advantage_index, advantage_table,
):
    reply_inputs, reply_keys, reply_queries = reply_inputs[0], reply_keys[0], reply_queries[0]
    reply_steps, upstream = reply_steps[0], upstream[0]
    scale = (advantage_index, advantage_table)
    row, mine = lax.axis_index("rollout"), lax.axis_index("ctx")
    place = (row * SLICES + mine).astype(jnp.int32).reshape(1, 1)
    owner = mine.astype(jnp.int32).reshape(1, 1)
    slices = shape(SLICES, ROWS, STATE)
    heads = shape(HEADS, TOKENS)
    square = shape(TOKENS, TOKENS)
    wide = shape(TOKENS, CHANNELS, dtype=BF16)
    narrow = shape(TOKENS, STATE, dtype=BF16)

    pack, reply_logs, prompt_logs, prompt_total = on_device(
        first_kernel, [shape(SLICES, GO, STATE), heads, heads, shape(8, TOKENS)], 3, 5 * 10**9,
        decay_log, *scale, prompt_steps, reply_inputs, reply_keys, reply_queries, reply_steps,
        upstream, loss_mask,
    )
    received = swap(pack, "ctx")
    later = later_sums(prompt_total, row, mine)
    prompt_states, prompt_ends = on_device(
        prompt_states_kernel, [slices, heads], 0, 3 * 10**9,
        prompt_inputs, prompt_keys, prompt_steps, prompt_logs, later,
    )
    prompt_states = turn(reduced_over_rows(prompt_states, row))
    near, mixed, row_sums, column_sums = on_device(
        within_kernel, [shape(TOKENS, CHANNELS), square, heads, heads], 0, 6 * 10**9,
        reply_inputs, reply_keys, reply_queries, reply_steps, upstream, loss_mask, reply_logs,
    )
    after, row_pulls, totals = on_device(
        group_kernel, [slices, shape(ROWS, STATE), shape(SLICES, STATE)], 1, 3 * 10**9,
        owner, received,
    )
    after = swap(after, "ctx")
    joint = jnp.concatenate([prompt_states, row_pulls], axis=0)
    for bit in (1, 2, 4, 8):
        joint = joint + traded(joint, "rollout", bit)
    (starts,) = on_device(
        carry_kernel, [slices], 1, 3 * 10**9, owner, totals, received, joint[:ROWS]
    )
    starts = swap(starts, "ctx")
    end_pull = gathered_over_rows(turn(joint[ROWS:]), row)
    reply_inputs_out, reply_keys_out, ended = on_device(
        reply_backward_kernel, [wide, narrow, heads], 2, 6 * 10**9,
        *scale, reply_inputs, reply_keys, reply_queries, reply_steps, reply_logs, after, near,
        mixed,
    )
    prompt_inputs_out, prompt_keys_out, owned, prompt_decay = on_device(
        prompt_backward_kernel, [wide, narrow, heads, shape(8, TOKENS)], 1, 6 * 10**9,
        decay_log, prompt_inputs, prompt_keys, prompt_steps, prompt_logs, prompt_ends, end_pull,
    )
    reply_queries_out, reply_steps_out, summary = on_device(
        reply_forward_kernel, [narrow, heads, shape(DEVICES, TOKENS)], 3, 6 * 10**9,
        decay_log, *scale, reply_keys, reply_queries, reply_steps, upstream, loss_mask,
        reply_logs, starts, after, mixed, row_sums, column_sums, ended, prompt_decay,
    )
    prompt_steps_out, decay = on_device(
        finish_kernel, [heads, shape(8, TOKENS)], 2, 10**8,
        place, decay_log, swap(summary, BOTH), owned, prompt_steps,
    )
    return (
        prompt_inputs_out, prompt_keys_out, prompt_steps_out, reply_inputs_out[None],
        reply_keys_out[None], reply_queries_out[None], reply_steps_out[None], decay[0, :HEADS],
    )


def solution(mesh):
    in_specs = (
        P(("rollout", "ctx"), None),
        P(("rollout", "ctx"), None),
        P(None, ("rollout", "ctx")),
        P("rollout", "ctx", None),
        P("rollout", "ctx", None),
        P("rollout", "ctx", None),
        P("rollout", None, "ctx"),
        P(),
        P("rollout", "ctx", None),
        P("rollout", "ctx"),
        P("rollout"),
        P(),
    )
    out_specs = (
        P(("rollout", "ctx"), None),
        P(("rollout", "ctx"), None),
        P(None, ("rollout", "ctx")),
        P("rollout", "ctx", None),
        P("rollout", "ctx", None),
        P("rollout", "ctx", None),
        P("rollout", None, "ctx"),
        P(),
    )
    return jax.shard_map(
        per_device, mesh=mesh, in_specs=in_specs, out_specs=out_specs, check_vma=False
    )
```

```python
import jax
import jax.numpy as jnp
from jax import lax
from jax.experimental import pallas as pl
from jax.experimental.pallas import tpu as pltpu
from jax.sharding import PartitionSpec as P

HEADS = 40
HEAD_DIM = 64
STATE = 128
TOKENS = 128
CHANNELS = HEADS * HEAD_DIM
PAIRS = HEADS // 2
SLICES = 16
DEVICES = SLICES * SLICES
GO = 328
ROWS = CHANNELS // SLICES
PIECE = 32
PER_SLICE = ROWS // PIECE
F32 = jnp.float32
BF16 = jnp.bfloat16
HIGHEST = lax.Precision.HIGHEST
VMEM_BYTES = 56 * 1024 * 1024
BOTH = ("rollout", "ctx")


def iota(shape, axis):
    return lax.broadcasted_iota(jnp.int32, shape, axis)


def halves(value):
    high = value.astype(BF16)
    return high, (value - high.astype(F32)).astype(BF16)


def dot(left, right):
    return jnp.dot(left, right, preferred_element_type=F32)


def dot_t(left, right, precision=None):
    return lax.dot_general(
        left, right, (((1,), (1,)), ((), ())), preferred_element_type=F32, precision=precision
    )


def exact_dot(left, right):
    return jnp.dot(left, right, preferred_element_type=F32, precision=HIGHEST)


def running_logs(steps, rate):
    earlier = (iota((TOKENS, TOKENS), 0) <= iota((TOKENS, TOKENS), 1)).astype(F32)
    return exact_dot(-steps * rate, earlier)


def transposed(rows, before=0):
    parts = [rows, jnp.zeros((TOKENS - before - rows.shape[0], TOKENS), F32)]
    if before:
        parts = [jnp.zeros((before, TOKENS), F32)] + parts
    return jnp.concatenate(parts, axis=0).T


def as_columns(row):
    return jnp.broadcast_to(row, (TOKENS, TOKENS)).T


def pair_rows(rows, pair):
    first = jnp.broadcast_to(rows[2 * pair : 2 * pair + 1], (HEAD_DIM, TOKENS))
    second = jnp.broadcast_to(rows[2 * pair + 1 : 2 * pair + 2], (HEAD_DIM, TOKENS))
    return jnp.concatenate([first, second], axis=0)


def column(columns, head):
    return jnp.broadcast_to(columns[:, head : head + 1], (TOKENS, TOKENS))


def pieces(pair):
    for part in range(4):
        place = 4 * pair + part
        yield part * PIECE, place // PER_SLICE, (place % PER_SLICE) * PIECE


def first_lanes():
    return iota((TOKENS, TOKENS), 1) < HEAD_DIM


def sides(block):
    zero = jnp.zeros((), BF16)
    half = first_lanes()
    return jnp.concatenate([jnp.where(half, block, zero), jnp.where(half, zero, block)], axis=0)


def span(pair):
    return slice(pair * TOKENS, (pair + 1) * TOKENS)


def gather(received, pair):
    return jnp.concatenate(
        [received[owner, offset : offset + PIECE, :] for at, owner, offset in pieces(pair)], axis=0
    )


def pack_states(pack, base, tokens, rows, keys):
    twice = jnp.concatenate([keys, keys], axis=0)
    for pair in range(PAIRS):
        block = tokens[:, span(pair)].astype(F32).T
        high, low = halves(block * pair_rows(rows, pair))
        states = dot(jnp.concatenate([high, low], axis=1), twice)
        for at, owner, offset in pieces(pair):
            pack[owner, base + offset : base + offset + PIECE, :] = states[at : at + PIECE]


def rates(decay_log):
    heads = iota((HEADS, TOKENS), 0)
    logs = jnp.zeros((HEADS, TOKENS), F32)
    for head in range(HEADS):
        logs = jnp.where(heads == head, decay_log[head], logs)
    return jnp.exp(logs)


def prompt_logs_kernel(decay_log, steps, logs, total):
    running = running_logs(steps[...], rates(decay_log))
    logs[...] = running
    last = jnp.broadcast_to(running[:, TOKENS - 1 :], (HEADS, TOKENS))
    total[...] = transposed(last)[0:8]


def first_kernel(
    decay_log, index, table, inputs, keys, queries, steps, upstream, mask, pack, reply_logs
):
    running = running_logs(steps[...], rates(decay_log))
    reply_logs[...] = running
    last = jnp.broadcast_to(running[:, TOKENS - 1 :], (HEADS, TOKENS))
    total = transposed(last)[0:8]
    for owner in range(SLICES):
        pack[owner, 2 * ROWS :, :] = total
    rows = jnp.exp(running) * (mask[...].astype(F32) * table[index[0]])
    pack_states(pack, 0, upstream, rows, queries[...])
    rows = jnp.exp(last - running) * steps[...]
    pack_states(pack, ROWS, inputs, rows, keys[...])


def prompt_states_kernel(inputs, keys, steps, logs, later, pack, ends):
    running = logs[...]
    after = as_columns(later[0:1, :])[:HEADS]
    rows = jnp.exp(running[:, TOKENS - 1 :] - running + after) * steps[...]
    ends[...] = rows
    pack_states(pack, 0, inputs, rows, keys[...])


def within_kernel(
    inputs, keys, queries, steps, upstream, mask_row, logs, near, mixed, row_sums, column_sums
):
    running = logs[...]
    columns = transposed(jnp.log(steps[...]) - running)
    causal = iota((TOKENS, TOKENS), 1) >= iota((TOKENS, TOKENS), 0)
    lanes = iota((TOKENS, TOKENS), 1)
    scores = dot_t(keys[...], queries[...])
    mask = as_columns(mask_row[...].astype(F32)).astype(BF16)
    total = jnp.zeros((TOKENS, TOKENS), F32)
    gathered = jnp.zeros((TOKENS, TOKENS), F32)
    for pair in range(PAIRS):
        pulled = upstream[:, span(pair)] * mask
        products = dot_t(sides(inputs[:, span(pair)]), pulled)
        highs, lows = [], []
        for side in range(2):
            head = 2 * pair + side
            gaps = running[head : head + 1] + column(columns, head)
            mixing = jnp.where(causal, jnp.exp(gaps), 0.0)
            weighted = mixing * products[side * TOKENS : (side + 1) * TOKENS]
            total = total + weighted
            terms = weighted * scores
            row_sums[head : head + 1, :] = jnp.sum(terms, axis=0, keepdims=True)
            gathered = jnp.where(lanes == head, jnp.sum(terms, axis=1, keepdims=True), gathered)
            high, low = halves(mixing * scores)
            highs.append(high)
            lows.append(low)
        both = sides(pulled)
        near[:, span(pair)] = dot(jnp.concatenate(highs, axis=1), both) + dot(
            jnp.concatenate(lows, axis=1), both
        )
    mixed[...] = total
    column_sums[...] = gathered.T[:HEADS]


def spread(columns, at):
    return jnp.broadcast_to(columns[:, at : at + 1], (ROWS, TOKENS))


def owner_columns(owner, rows):
    place = owner * ROWS + iota((ROWS, TOKENS), 0)
    chosen = (lax.shift_right_logical(place, 6) == iota((ROWS, TOKENS), 1)).astype(F32)
    pad = jnp.zeros((TOKENS - rows.shape[0], TOKENS), F32)
    return dot_t(chosen, jnp.concatenate([rows, pad], axis=0), HIGHEST)


def group_kernel(owner, received, after, start, totals):
    reply = jnp.concatenate(
        [received[c, 2 * ROWS : 2 * ROWS + 1, :] for c in range(SLICES)], axis=0
    )
    totals[...] = reply
    factors = jnp.exp(owner_columns(owner[0, 0], reply))
    pulled = jnp.zeros((ROWS, TOKENS), F32)
    for c in range(SLICES - 1, -1, -1):
        after[c] = pulled
        pulled = spread(factors, c) * pulled + received[c, 0:ROWS, :]
    start[...] = pulled


def carry_kernel(owner, totals, received, end_state, starts):
    factors = jnp.exp(owner_columns(owner[0, 0], totals[...]))
    state = end_state[...]
    for c in range(SLICES):
        starts[c] = state
        if c < SLICES - 1:
            state = spread(factors, c) * state + received[c, ROWS : 2 * ROWS, :]


def backward_parts(inputs, pulls, ends, keys, near, scale, inputs_out):
    twice = jnp.concatenate([keys, keys], axis=1)
    wide = keys.astype(F32)
    lanes = iota((TOKENS, TOKENS), 1)
    half = first_lanes()
    total = jnp.zeros((TOKENS, TOKENS), F32)
    gathered = jnp.zeros((TOKENS, TOKENS), F32)
    columns = transposed(ends)
    for pair in range(PAIRS):
        high, low = halves(gather(pulls, pair))
        once = sides(inputs[:, span(pair)])
        backward = dot(
            jnp.concatenate([once, once], axis=1), jnp.concatenate([high, low], axis=0)
        )
        keyed = dot_t(twice, jnp.concatenate([high, low], axis=1))
        factors = []
        for side in range(2):
            head = 2 * pair + side
            factors.append(column(columns, head))
            part = factors[side] * backward[side * TOKENS : (side + 1) * TOKENS]
            total = total + part
            gathered = jnp.where(
                lanes == head, jnp.sum(part * wide, axis=1, keepdims=True), gathered
            )
        own = jnp.where(half, factors[0], factors[1]) * keyed
        if near is not None:
            own = near[:, span(pair)] * scale + own
        inputs_out[:, span(pair)] = own.astype(BF16)
    return total, gathered.T[:HEADS]


def reply_backward_kernel(
    index, table, inputs, keys, queries, steps, logs, pulls, near, mixed, inputs_out, keys_out, ended_out
):
    scale = table[index[0]]
    running = logs[...]
    ends = jnp.exp(running[:, TOKENS - 1 :] - running) * steps[...]
    total, ended = backward_parts(inputs, pulls, ends, keys[...], near, scale, inputs_out)
    high, low = halves(mixed[...] * scale)
    total = total + dot(high, queries[...]) + dot(low, queries[...])
    keys_out[...] = total.astype(BF16)
    ended_out[...] = ended


def log_sums(rows):
    lower = (iota((TOKENS, TOKENS), 0) < iota((TOKENS, TOKENS), 1)).astype(F32)
    return exact_dot(rows, lower)


def prompt_backward_kernel(
    decay_log, inputs, keys, steps, logs, ends, pulls, inputs_out, keys_out, owned_out, decay
):
    rate = rates(decay_log)
    total, owned = backward_parts(inputs, pulls, ends[...], keys[...], None, None, inputs_out)
    keys_out[...] = total.astype(BF16)
    owned_out[...] = owned
    inside = jnp.sum(-steps[...] * rate * log_sums(owned), axis=1, keepdims=True)
    sums = jnp.sum(owned, axis=1, keepdims=True)
    stacked = jnp.broadcast_to(
        jnp.concatenate([inside, sums, logs[:, TOKENS - 1 :]], axis=0), (3 * HEADS, TOKENS)
    )
    decay[...] = transposed(stacked)[0:8]


def reply_forward_kernel(
    decay_log, index, table, keys, queries, steps, upstream, mask_row, logs, starts, pulls, mixed,
    row_sums, column_sums, ended, prompt_decay, queries_out, steps_out, summary,
):
    scale = table[index[0]]
    running = logs[...]
    rate = rates(decay_log)
    reach = transposed(jnp.exp(running) * scale)
    mask = as_columns(mask_row[...].astype(F32)).astype(BF16)
    lanes = iota((TOKENS, TOKENS), 1)
    wide = queries[...].astype(F32)
    total = jnp.zeros((TOKENS, TOKENS), F32)
    reached = jnp.zeros((TOKENS, TOKENS), F32)
    overlaps = []
    for pair in range(PAIRS):
        state = gather(starts, pair)
        shared = state * gather(pulls, pair)
        overlaps.append(jnp.sum(shared[:HEAD_DIM], axis=0, keepdims=True))
        overlaps.append(jnp.sum(shared[HEAD_DIM:], axis=0, keepdims=True))
        high, low = halves(state)
        once = sides(upstream[:, span(pair)] * mask)
        forward = dot(
            jnp.concatenate([once, once], axis=1), jnp.concatenate([high, low], axis=0)
        )
        for side in range(2):
            head = 2 * pair + side
            part = column(reach, head) * forward[side * TOKENS : (side + 1) * TOKENS]
            total = total + part
            reached = jnp.where(
                lanes == head, jnp.sum(part * wide, axis=1, keepdims=True), reached
            )
    high, low = halves((mixed[...] * scale).T)
    total = total + dot(high, keys[...]) + dot(low, keys[...])
    queries_out[...] = total.astype(BF16)
    reached = reached.T[:HEADS]
    later = (iota((TOKENS, TOKENS), 0) >= iota((TOKENS, TOKENS), 1)).astype(F32)
    carried = jnp.sum(jnp.concatenate(overlaps, axis=0), axis=1, keepdims=True)
    carried = carried * jnp.exp(running[:, TOKENS - 1 :])
    closer = column_sums[...] * scale
    log_pull = (
        exact_dot(row_sums[...] * scale - closer + reached, later) + log_sums(ended[...]) + carried
    )
    steps_out[...] = (closer + ended[...]) / steps[...] - rate * log_pull
    local = jnp.sum(-steps[...] * rate * log_pull, axis=1, keepdims=True)
    row = transposed(jnp.broadcast_to(local, (HEADS, TOKENS)))[0:1] + prompt_decay[0:1]
    summary[...] = jnp.broadcast_to(row, (DEVICES, TOKENS))


def moved_lanes(rows, by):
    shift = (iota((TOKENS, TOKENS), 0) == iota((TOKENS, TOKENS), 1) + by).astype(F32)
    return exact_dot(rows, shift)


def finish_kernel(place, decay_log, received, owned, steps, steps_out, decay):
    rows = received[...]
    below = (iota((DEVICES, DEVICES), 0) > iota((DEVICES, DEVICES), 1)).astype(F32)
    before = exact_dot(below, moved_lanes(rows, HEADS))
    decay_rows = rows + before * moved_lanes(rows, 2 * HEADS)
    decay[...] = jnp.broadcast_to(jnp.sum(decay_rows, axis=0, keepdims=True), (8, TOKENS))
    mine = jnp.where(iota((DEVICES, TOKENS), 0) < place[0, 0], rows, 0.0)
    mine = as_columns(jnp.sum(mine, axis=0, keepdims=True))[HEADS : 2 * HEADS]
    steps_out[...] = owned[...] / steps[...] - rates(decay_log) * (log_sums(owned[...]) + mine)


def whole(dims):
    return pl.BlockSpec(dims, lambda step: (0,) * len(dims))


def on_device(kernel, out_shapes, scalars, flops, *operands):
    specs = [pl.BlockSpec(memory_space=pltpu.SMEM) for _ in range(scalars)]
    specs += [whole(x.shape) for x in operands[scalars:]]
    return pl.pallas_call(
        kernel,
        grid=(1,),
        out_shape=out_shapes,
        in_specs=specs,
        out_specs=[whole(x.shape) for x in out_shapes],
        compiler_params=pltpu.CompilerParams(vmem_limit_bytes=VMEM_BYTES),
        cost_estimate=pl.CostEstimate(flops=flops, bytes_accessed=1024, transcendentals=0),
    )(*operands)


def shape(*dims, dtype=F32):
    return jax.ShapeDtypeStruct(dims, dtype)


def swap(value, axis):
    return lax.all_to_all(value, axis, 0, 0, tiled=True)


def turn(block):
    pairs = [(a * SLICES + b, b * SLICES + a) for a in range(SLICES) for b in range(SLICES)]
    return lax.ppermute(block, BOTH, pairs)


def traded(value, axis, bit):
    return lax.ppermute(value, axis, [(at, at ^ bit) for at in range(SLICES)])


def later_sums(later, total, axis, place):
    for bit in (1, 2, 4, 8):
        other = traded(total, axis, bit)
        later = later + jnp.where((place & bit) == 0, other, 0.0)
        total = total + other
    return later, total


def reduced_over_rows(states, row):
    for bit in (1, 2, 4, 8):
        side = ((row & bit) != 0).astype(jnp.int32)
        split = states.reshape((states.shape[0] // 2, 2) + states.shape[1:])
        given = lax.dynamic_index_in_dim(split, 1 - side, 1, keepdims=False)
        kept = lax.dynamic_index_in_dim(split, side, 1, keepdims=False)
        states = kept + traded(given, "rollout", bit)
    return states[0]


def gathered_over_rows(block, row):
    parts = block[None]
    for bit in (8, 4, 2, 1):
        other = traded(parts, "rollout", bit)
        low = (row & bit) == 0
        first, second = jnp.where(low, parts, other), jnp.where(low, other, parts)
        parts = jnp.stack([first, second], axis=1).reshape((-1,) + block.shape)
    return parts


def per_device(
    prompt_inputs, prompt_keys, prompt_steps, reply_inputs, reply_keys, reply_queries,
    reply_steps, decay_log, upstream, loss_mask, advantage_index, advantage_table,
):
    reply_inputs, reply_keys, reply_queries = reply_inputs[0], reply_keys[0], reply_queries[0]
    reply_steps, upstream = reply_steps[0], upstream[0]
    scale = (advantage_index, advantage_table)
    row, mine = lax.axis_index("rollout"), lax.axis_index("ctx")
    place = (row * SLICES + mine).astype(jnp.int32).reshape(1, 1)
    owner = mine.astype(jnp.int32).reshape(1, 1)
    slices = shape(SLICES, ROWS, STATE)
    heads = shape(HEADS, TOKENS)
    square = shape(TOKENS, TOKENS)
    wide = shape(TOKENS, CHANNELS, dtype=BF16)
    narrow = shape(TOKENS, STATE, dtype=BF16)

    prompt_logs, prompt_total = on_device(
        prompt_logs_kernel, [heads, shape(8, TOKENS)], 1, 10**8, decay_log, prompt_steps
    )
    pack, reply_logs = on_device(
        first_kernel, [shape(SLICES, GO, STATE), heads], 3, 5 * 10**9,
        decay_log, *scale, reply_inputs, reply_keys, reply_queries, reply_steps, upstream,
        loss_mask,
    )
    near, mixed, row_sums, column_sums = on_device(
        within_kernel, [shape(TOKENS, CHANNELS), square, heads, heads], 0, 6 * 10**9,
        reply_inputs, reply_keys, reply_queries, reply_steps, upstream, loss_mask, reply_logs,
    )
    sums = later_sums(jnp.zeros_like(prompt_total), prompt_total, "ctx", mine)
    pack, sums, row_sums = lax.optimization_barrier((pack, sums, row_sums))
    received = swap(pack, "ctx")
    later, _ = later_sums(*sums, "rollout", row)
    prompt_states, prompt_ends = on_device(
        prompt_states_kernel, [slices, heads], 0, 3 * 10**6,
        prompt_inputs, prompt_keys, prompt_steps, prompt_logs, later,
    )
    received, prompt_states = lax.optimization_barrier(
        (received, reduced_over_rows(prompt_states, row))
    )
    after, row_pulls, totals = on_device(
        group_kernel, [slices, shape(ROWS, STATE), shape(SLICES, STATE)], 1, 3 * 10**6,
        owner, received,
    )
    after, prompt_states = lax.optimization_barrier((after, turn(prompt_states)))
    after = swap(after, "ctx")
    joint = jnp.concatenate([prompt_states, row_pulls], axis=0)
    for bit in (1, 2, 4, 8):
        joint = joint + traded(joint, "rollout", bit)
    (starts,) = on_device(
        carry_kernel, [slices], 1, 3 * 10**6, owner, totals, received, joint[:ROWS]
    )
    starts, after = lax.optimization_barrier((starts, after))
    starts = swap(starts, "ctx")
    end_pull = gathered_over_rows(turn(joint[ROWS:]), row)
    end_pull, after = lax.optimization_barrier((end_pull, after))
    reply_inputs_out, reply_keys_out, ended = on_device(
        reply_backward_kernel, [wide, narrow, heads], 2, 6 * 10**6,
        *scale, reply_inputs, reply_keys, reply_queries, reply_steps, reply_logs, after, near,
        mixed,
    )
    prompt_inputs_out, prompt_keys_out, owned, prompt_decay = on_device(
        prompt_backward_kernel, [wide, narrow, heads, shape(8, TOKENS)], 1, 6 * 10**6,
        decay_log, prompt_inputs, prompt_keys, prompt_steps, prompt_logs, prompt_ends, end_pull,
    )
    reply_queries_out, reply_steps_out, summary = on_device(
        reply_forward_kernel, [narrow, heads, shape(DEVICES, TOKENS)], 3, 6 * 10**6,
        decay_log, *scale, reply_keys, reply_queries, reply_steps, upstream, loss_mask,
        reply_logs, starts, after, mixed, row_sums, column_sums, ended, prompt_decay,
    )
    prompt_steps_out, decay = on_device(
        finish_kernel, [heads, shape(8, TOKENS)], 2, 10**8,
        place, decay_log, swap(summary, BOTH), owned, prompt_steps,
    )
    return (
        prompt_inputs_out, prompt_keys_out, prompt_steps_out, reply_inputs_out[None],
        reply_keys_out[None], reply_queries_out[None], reply_steps_out[None], decay[0, :HEADS],
    )


def solution(mesh):
    in_specs = (
        P(("rollout", "ctx"), None),
        P(("rollout", "ctx"), None),
        P(None, ("rollout", "ctx")),
        P("rollout", "ctx", None),
        P("rollout", "ctx", None),
        P("rollout", "ctx", None),
        P("rollout", None, "ctx"),
        P(),
        P("rollout", "ctx", None),
        P("rollout", "ctx"),
        P("rollout"),
        P(),
    )
    out_specs = (
        P(("rollout", "ctx"), None),
        P(("rollout", "ctx"), None),
        P(None, ("rollout", "ctx")),
        P("rollout", "ctx", None),
        P("rollout", "ctx", None),
        P("rollout", "ctx", None),
        P("rollout", None, "ctx"),
        P(),
    )
    return jax.shard_map(
        per_device, mesh=mesh, in_specs=in_specs, out_specs=out_specs, check_vma=False
    )
```

```python
import jax
import jax.numpy as jnp
from jax import lax
from jax.experimental import pallas as pl
from jax.experimental.pallas import tpu as pltpu
from jax.sharding import PartitionSpec as P

HEADS = 40
HEAD_DIM = 64
STATE = 128
TOKENS = 128
CHANNELS = HEADS * HEAD_DIM
PAIRS = HEADS // 2
SLICES = 16
DEVICES = SLICES * SLICES
ROWS = CHANNELS // SLICES
GO = 3 * ROWS + 8
PIECE = 32
PER_SLICE = ROWS // PIECE
F32 = jnp.float32
BF16 = jnp.bfloat16
HIGHEST = lax.Precision.HIGHEST
VMEM_BYTES = 56 * 1024 * 1024
BOTH = ("rollout", "ctx")


def iota(shape, axis):
    return lax.broadcasted_iota(jnp.int32, shape, axis)


def halves(value):
    high = value.astype(BF16)
    return high, (value - high.astype(F32)).astype(BF16)


def dot(left, right):
    return jnp.dot(left, right, preferred_element_type=F32)


def dot_t(left, right, precision=None):
    return lax.dot_general(
        left, right, (((1,), (1,)), ((), ())), preferred_element_type=F32, precision=precision
    )


def exact_dot(left, right):
    return jnp.dot(left, right, preferred_element_type=F32, precision=HIGHEST)


def running_logs(steps, rate):
    earlier = (iota((TOKENS, TOKENS), 0) <= iota((TOKENS, TOKENS), 1)).astype(F32)
    return exact_dot(-steps * rate, earlier)


def transposed(rows, before=0):
    parts = [rows, jnp.zeros((TOKENS - before - rows.shape[0], TOKENS), F32)]
    if before:
        parts = [jnp.zeros((before, TOKENS), F32)] + parts
    return jnp.concatenate(parts, axis=0).T


def as_columns(row):
    return jnp.broadcast_to(row, (TOKENS, TOKENS)).T


def pair_rows(rows, pair):
    first = jnp.broadcast_to(rows[2 * pair : 2 * pair + 1], (HEAD_DIM, TOKENS))
    second = jnp.broadcast_to(rows[2 * pair + 1 : 2 * pair + 2], (HEAD_DIM, TOKENS))
    return jnp.concatenate([first, second], axis=0)


def column(columns, head):
    return jnp.broadcast_to(columns[:, head : head + 1], (TOKENS, TOKENS))


def pieces(pair):
    for part in range(4):
        place = 4 * pair + part
        yield part * PIECE, place // PER_SLICE, (place % PER_SLICE) * PIECE


def first_lanes():
    return iota((TOKENS, TOKENS), 1) < HEAD_DIM


def sides(block):
    zero = jnp.zeros((), BF16)
    half = first_lanes()
    return jnp.concatenate([jnp.where(half, block, zero), jnp.where(half, zero, block)], axis=0)


def span(pair):
    return slice(pair * TOKENS, (pair + 1) * TOKENS)


def gather(received, pair):
    return jnp.concatenate(
        [received[owner, offset : offset + PIECE, :] for at, owner, offset in pieces(pair)], axis=0
    )


def pack_states(pack, base, tokens, rows, keys):
    twice = jnp.concatenate([keys, keys], axis=0)
    for pair in range(PAIRS):
        block = tokens[:, span(pair)].astype(F32).T
        high, low = halves(block * pair_rows(rows, pair))
        states = dot(jnp.concatenate([high, low], axis=1), twice)
        for at, owner, offset in pieces(pair):
            pack[owner, base + offset : base + offset + PIECE, :] = states[at : at + PIECE]


def rates(decay_log):
    heads = iota((HEADS, TOKENS), 0)
    logs = jnp.zeros((HEADS, TOKENS), F32)
    for head in range(HEADS):
        logs = jnp.where(heads == head, decay_log[head], logs)
    return jnp.exp(logs)


def first_kernel(
    decay_log, index, table, prompt_inputs, prompt_keys, prompt_steps, inputs, keys, queries,
    steps, upstream, mask, pack, reply_logs, prompt_logs,
):
    rate = rates(decay_log)
    running = running_logs(steps[...], rate)
    prompt_running = running_logs(prompt_steps[...], rate)
    reply_logs[...] = running
    prompt_logs[...] = prompt_running
    last = jnp.broadcast_to(running[:, TOKENS - 1 :], (HEADS, TOKENS))
    prompt_last = jnp.broadcast_to(prompt_running[:, TOKENS - 1 :], (HEADS, TOKENS))
    totals = jnp.concatenate(
        [transposed(last)[0:1], transposed(prompt_last)[0:1], jnp.zeros((6, TOKENS), F32)], axis=0
    )
    for owner in range(SLICES):
        pack[owner, 3 * ROWS :, :] = totals
    rows = jnp.exp(running) * (mask[...].astype(F32) * table[index[0]])
    pack_states(pack, 0, upstream, rows, queries[...])
    rows = jnp.exp(last - running) * steps[...]
    pack_states(pack, ROWS, inputs, rows, keys[...])
    rows = jnp.exp(prompt_last - prompt_running) * prompt_steps[...]
    pack_states(pack, 2 * ROWS, prompt_inputs, rows, prompt_keys[...])


def within_kernel(
    inputs, keys, queries, steps, upstream, mask_row, logs, near, mixed, row_sums, column_sums
):
    running = logs[...]
    columns = transposed(jnp.log(steps[...]) - running)
    causal = iota((TOKENS, TOKENS), 1) >= iota((TOKENS, TOKENS), 0)
    lanes = iota((TOKENS, TOKENS), 1)
    scores = dot_t(keys[...], queries[...])
    mask = as_columns(mask_row[...].astype(F32)).astype(BF16)
    total = jnp.zeros((TOKENS, TOKENS), F32)
    gathered = jnp.zeros((TOKENS, TOKENS), F32)
    for pair in range(PAIRS):
        pulled = upstream[:, span(pair)] * mask
        products = dot_t(sides(inputs[:, span(pair)]), pulled)
        highs, lows = [], []
        for side in range(2):
            head = 2 * pair + side
            gaps = running[head : head + 1] + column(columns, head)
            mixing = jnp.where(causal, jnp.exp(gaps), 0.0)
            weighted = mixing * products[side * TOKENS : (side + 1) * TOKENS]
            total = total + weighted
            terms = weighted * scores
            row_sums[head : head + 1, :] = jnp.sum(terms, axis=0, keepdims=True)
            gathered = jnp.where(lanes == head, jnp.sum(terms, axis=1, keepdims=True), gathered)
            high, low = halves(mixing * scores)
            highs.append(high)
            lows.append(low)
        both = sides(pulled)
        near[:, span(pair)] = dot(jnp.concatenate(highs, axis=1), both) + dot(
            jnp.concatenate(lows, axis=1), both
        )
    mixed[...] = total
    column_sums[...] = gathered.T[:HEADS]


def spread(columns, at):
    return jnp.broadcast_to(columns[:, at : at + 1], (ROWS, TOKENS))


def owner_columns(owner, rows):
    place = owner * ROWS + iota((ROWS, TOKENS), 0)
    chosen = (lax.shift_right_logical(place, 6) == iota((ROWS, TOKENS), 1)).astype(F32)
    pad = jnp.zeros((TOKENS - rows.shape[0], TOKENS), F32)
    return dot_t(chosen, jnp.concatenate([rows, pad], axis=0), HIGHEST)


def group_kernel(owner, received, after, joint, totals):
    reply = jnp.concatenate(
        [received[c, 3 * ROWS : 3 * ROWS + 1, :] for c in range(SLICES)], axis=0
    )
    prompt = jnp.concatenate(
        [received[c, 3 * ROWS + 1 : 3 * ROWS + 2, :] for c in range(SLICES)], axis=0
    )
    totals[0:SLICES, :] = reply
    totals[SLICES:, :] = prompt
    group = jnp.sum(prompt, axis=0, keepdims=True)
    logs = owner_columns(owner[0, 0], jnp.concatenate([reply, prompt, group], axis=0))
    factors = jnp.exp(logs)
    pulled = jnp.zeros((ROWS, TOKENS), F32)
    state = jnp.zeros((ROWS, TOKENS), F32)
    for c in range(SLICES):
        back = SLICES - 1 - c
        after[back] = pulled
        pulled = spread(factors, back) * pulled + received[back, 0:ROWS, :]
        state = spread(factors, SLICES + c) * state + received[c, 2 * ROWS : 3 * ROWS, :]
    joint[0:ROWS, :] = state
    joint[ROWS : 2 * ROWS, :] = pulled
    joint[2 * ROWS : 3 * ROWS, :] = spread(logs, 2 * SLICES)
    joint[3 * ROWS :, :] = jnp.broadcast_to(group, (8, TOKENS))


def carry_kernel(owner, totals, received, joint, starts):
    factors = jnp.exp(owner_columns(owner[0, 0], totals[0:SLICES, :]))
    state = joint[0:ROWS, :]
    for c in range(SLICES):
        starts[c] = state
        if c < SLICES - 1:
            state = spread(factors, c) * state + received[c, ROWS : 2 * ROWS, :]


def backward_parts(inputs, pulls, ends, keys, near, scale, inputs_out):
    twice = jnp.concatenate([keys, keys], axis=1)
    wide = keys.astype(F32)
    lanes = iota((TOKENS, TOKENS), 1)
    half = first_lanes()
    total = jnp.zeros((TOKENS, TOKENS), F32)
    gathered = jnp.zeros((TOKENS, TOKENS), F32)
    columns = transposed(ends)
    for pair in range(PAIRS):
        high, low = halves(gather(pulls, pair))
        once = sides(inputs[:, span(pair)])
        backward = dot(
            jnp.concatenate([once, once], axis=1), jnp.concatenate([high, low], axis=0)
        )
        keyed = dot_t(twice, jnp.concatenate([high, low], axis=1))
        factors = []
        for side in range(2):
            head = 2 * pair + side
            factors.append(column(columns, head))
            part = factors[side] * backward[side * TOKENS : (side + 1) * TOKENS]
            total = total + part
            gathered = jnp.where(
                lanes == head, jnp.sum(part * wide, axis=1, keepdims=True), gathered
            )
        own = jnp.where(half, factors[0], factors[1]) * keyed
        if near is not None:
            own = near[:, span(pair)] * scale + own
        inputs_out[:, span(pair)] = own.astype(BF16)
    return total, gathered.T[:HEADS]


def reply_backward_kernel(
    index, table, inputs, keys, queries, steps, logs, pulls, near, mixed, inputs_out, keys_out, ended_out
):
    scale = table[index[0]]
    running = logs[...]
    ends = jnp.exp(running[:, TOKENS - 1 :] - running) * steps[...]
    total, ended = backward_parts(inputs, pulls, ends, keys[...], near, scale, inputs_out)
    high, low = halves(mixed[...] * scale)
    total = total + dot(high, queries[...]) + dot(low, queries[...])
    keys_out[...] = total.astype(BF16)
    ended_out[...] = ended


def log_sums(rows):
    lower = (iota((TOKENS, TOKENS), 0) < iota((TOKENS, TOKENS), 1)).astype(F32)
    return exact_dot(rows, lower)


def prompt_backward_kernel(
    owner, decay_log, inputs, keys, steps, logs, totals, later_groups, pulls,
    inputs_out, keys_out, owned_out, decay,
):
    rate = rates(decay_log)
    later = later_groups[...]
    for c in range(1, SLICES):
        row = totals[SLICES + c : SLICES + c + 1, :]
        later = later + jnp.where(c > owner[0, 0], row, 0.0)
    running = logs[...]
    ends = jnp.exp(running[:, TOKENS - 1 :] - running + as_columns(later)[:HEADS]) * steps[...]
    total, owned = backward_parts(inputs, pulls, ends, keys[...], None, None, inputs_out)
    keys_out[...] = total.astype(BF16)
    owned_out[...] = owned
    inside = jnp.sum(-steps[...] * rate * log_sums(owned), axis=1, keepdims=True)
    sums = jnp.sum(owned, axis=1, keepdims=True)
    logs_whole = running[:, TOKENS - 1 :]
    stacked = jnp.broadcast_to(
        jnp.concatenate([inside, sums, logs_whole], axis=0), (3 * HEADS, TOKENS)
    )
    decay[...] = transposed(stacked)[0:8]


def reply_forward_kernel(
    decay_log, index, table, keys, queries, steps, upstream, mask_row, logs, starts, pulls, mixed,
    row_sums, column_sums, ended, prompt_decay, queries_out, steps_out, summary,
):
    scale = table[index[0]]
    running = logs[...]
    rate = rates(decay_log)
    reach = transposed(jnp.exp(running) * scale)
    mask = as_columns(mask_row[...].astype(F32)).astype(BF16)
    lanes = iota((TOKENS, TOKENS), 1)
    wide = queries[...].astype(F32)
    total = jnp.zeros((TOKENS, TOKENS), F32)
    reached = jnp.zeros((TOKENS, TOKENS), F32)
    overlaps = []
    for pair in range(PAIRS):
        state = gather(starts, pair)
        shared = state * gather(pulls, pair)
        overlaps.append(jnp.sum(shared[:HEAD_DIM], axis=0, keepdims=True))
        overlaps.append(jnp.sum(shared[HEAD_DIM:], axis=0, keepdims=True))
        high, low = halves(state)
        once = sides(upstream[:, span(pair)] * mask)
        forward = dot(
            jnp.concatenate([once, once], axis=1), jnp.concatenate([high, low], axis=0)
        )
        for side in range(2):
            head = 2 * pair + side
            part = column(reach, head) * forward[side * TOKENS : (side + 1) * TOKENS]
            total = total + part
            reached = jnp.where(
                lanes == head, jnp.sum(part * wide, axis=1, keepdims=True), reached
            )
    high, low = halves((mixed[...] * scale).T)
    total = total + dot(high, keys[...]) + dot(low, keys[...])
    queries_out[...] = total.astype(BF16)
    reached = reached.T[:HEADS]
    later = (iota((TOKENS, TOKENS), 0) >= iota((TOKENS, TOKENS), 1)).astype(F32)
    carried = jnp.sum(jnp.concatenate(overlaps, axis=0), axis=1, keepdims=True)
    carried = carried * jnp.exp(running[:, TOKENS - 1 :])
    closer = column_sums[...] * scale
    log_pull = (
        exact_dot(row_sums[...] * scale - closer + reached, later) + log_sums(ended[...]) + carried
    )
    steps_out[...] = (closer + ended[...]) / steps[...] - rate * log_pull
    local = jnp.sum(-steps[...] * rate * log_pull, axis=1, keepdims=True)
    row = transposed(jnp.broadcast_to(local, (HEADS, TOKENS)))[0:1] + prompt_decay[0:1]
    summary[...] = jnp.broadcast_to(row, (DEVICES, TOKENS))


def moved_lanes(rows, by):
    shift = (iota((TOKENS, TOKENS), 0) == iota((TOKENS, TOKENS), 1) + by).astype(F32)
    return exact_dot(rows, shift)


def finish_kernel(place, decay_log, received, owned, steps, steps_out, decay):
    rows = received[...]
    below = (iota((DEVICES, DEVICES), 0) > iota((DEVICES, DEVICES), 1)).astype(F32)
    before = exact_dot(below, moved_lanes(rows, HEADS))
    decay_rows = rows + before * moved_lanes(rows, 2 * HEADS)
    decay[...] = jnp.broadcast_to(jnp.sum(decay_rows, axis=0, keepdims=True), (8, TOKENS))
    mine = jnp.where(iota((DEVICES, TOKENS), 0) < place[0, 0], rows, 0.0)
    mine = as_columns(jnp.sum(mine, axis=0, keepdims=True))[HEADS : 2 * HEADS]
    steps_out[...] = owned[...] / steps[...] - rates(decay_log) * (log_sums(owned[...]) + mine)


def whole(dims):
    return pl.BlockSpec(dims, lambda step: (0,) * len(dims))


def on_device(kernel, out_shapes, scalars, flops, *operands):
    specs = [pl.BlockSpec(memory_space=pltpu.SMEM) for _ in range(scalars)]
    specs += [whole(x.shape) for x in operands[scalars:]]
    return pl.pallas_call(
        kernel,
        grid=(1,),
        out_shape=out_shapes,
        in_specs=specs,
        out_specs=[whole(x.shape) for x in out_shapes],
        compiler_params=pltpu.CompilerParams(vmem_limit_bytes=VMEM_BYTES),
        cost_estimate=pl.CostEstimate(flops=flops, bytes_accessed=1024, transcendentals=0),
    )(*operands)


def shape(*dims, dtype=F32):
    return jax.ShapeDtypeStruct(dims, dtype)


def swap(value, axis):
    return lax.all_to_all(value, axis, 0, 0, tiled=True)


def turn(block):
    pairs = [(a * SLICES + b, b * SLICES + a) for a in range(SLICES) for b in range(SLICES)]
    return lax.ppermute(block, BOTH, pairs)


def traded(value, axis, bit):
    return lax.ppermute(value, axis, [(at, at ^ bit) for at in range(SLICES)])


def gathered_over_rows(block, row):
    parts = block[None]
    for bit in (8, 4, 2, 1):
        other = traded(parts, "rollout", bit)
        low = (row & bit) == 0
        first, second = jnp.where(low, parts, other), jnp.where(low, other, parts)
        parts = jnp.stack([first, second], axis=1).reshape((-1,) + block.shape)
    return parts


def per_device(
    prompt_inputs, prompt_keys, prompt_steps, reply_inputs, reply_keys, reply_queries,
    reply_steps, decay_log, upstream, loss_mask, advantage_index, advantage_table,
):
    reply_inputs, reply_keys, reply_queries = reply_inputs[0], reply_keys[0], reply_queries[0]
    reply_steps, upstream = reply_steps[0], upstream[0]
    scale = (advantage_index, advantage_table)
    row, mine = lax.axis_index("rollout"), lax.axis_index("ctx")
    place = (row * SLICES + mine).astype(jnp.int32).reshape(1, 1)
    owner = mine.astype(jnp.int32).reshape(1, 1)
    slices = shape(SLICES, ROWS, STATE)
    heads = shape(HEADS, TOKENS)
    square = shape(TOKENS, TOKENS)
    wide = shape(TOKENS, CHANNELS, dtype=BF16)
    narrow = shape(TOKENS, STATE, dtype=BF16)

    pack, reply_logs, prompt_logs = on_device(
        first_kernel, [shape(SLICES, GO, STATE), heads, heads], 3, 6 * 10**9,
        decay_log, *scale, prompt_inputs, prompt_keys, prompt_steps, reply_inputs, reply_keys,
        reply_queries, reply_steps, upstream, loss_mask,
    )
    received = swap(pack, "ctx")
    after, joint, totals = on_device(
        group_kernel, [slices, shape(GO, STATE), shape(2 * SLICES, STATE)], 1, 3 * 10**6,
        owner, received,
    )
    after, joint, reply_logs = lax.optimization_barrier((after, joint, reply_logs))
    after = swap(after, "ctx")
    near, mixed, row_sums, column_sums = on_device(
        within_kernel, [shape(TOKENS, CHANNELS), square, heads, heads], 0, 6 * 10**6,
        reply_inputs, reply_keys, reply_queries, reply_steps, upstream, loss_mask, reply_logs,
    )
    later_groups = jnp.zeros((1, STATE), F32)
    for bit in (1, 2, 4, 8):
        other = traded(joint, "rollout", bit)
        early = (row & bit) == 0
        logs, other_logs = joint[2 * ROWS : 3 * ROWS], other[2 * ROWS : 3 * ROWS]
        ours, others = joint[:ROWS], other[:ROWS]
        joined = jnp.where(
            early, jnp.exp(other_logs) * ours + others, jnp.exp(logs) * others + ours
        )
        later_groups = later_groups + jnp.where(early, other[3 * ROWS : 3 * ROWS + 1], 0.0)
        joint = jnp.concatenate([joined, joint[ROWS:] + other[ROWS:]], axis=0)
    (starts,) = on_device(
        carry_kernel, [slices], 1, 3 * 10**6, owner, totals, received, joint
    )
    starts, after, near = lax.optimization_barrier((starts, after, near))
    starts = swap(starts, "ctx")
    end_pull = gathered_over_rows(turn(joint[ROWS : 2 * ROWS]), row)
    end_pull, after = lax.optimization_barrier((end_pull, after))
    reply_inputs_out, reply_keys_out, ended = on_device(
        reply_backward_kernel, [wide, narrow, heads], 2, 6 * 10**6,
        *scale, reply_inputs, reply_keys, reply_queries, reply_steps, reply_logs, after, near,
        mixed,
    )
    prompt_inputs_out, prompt_keys_out, owned, prompt_decay = on_device(
        prompt_backward_kernel, [wide, narrow, heads, shape(8, TOKENS)], 2, 6 * 10**6,
        owner, decay_log, prompt_inputs, prompt_keys, prompt_steps, prompt_logs, totals,
        later_groups, end_pull,
    )
    reply_queries_out, reply_steps_out, summary = on_device(
        reply_forward_kernel, [narrow, heads, shape(DEVICES, TOKENS)], 3, 6 * 10**6,
        decay_log, *scale, reply_keys, reply_queries, reply_steps, upstream, loss_mask,
        reply_logs, starts, after, mixed, row_sums, column_sums, ended, prompt_decay,
    )
    prompt_steps_out, decay = on_device(
        finish_kernel, [heads, shape(8, TOKENS)], 2, 10**8,
        place, decay_log, swap(summary, BOTH), owned, prompt_steps,
    )
    return (
        prompt_inputs_out, prompt_keys_out, prompt_steps_out, reply_inputs_out[None],
        reply_keys_out[None], reply_queries_out[None], reply_steps_out[None], decay[0, :HEADS],
    )


def solution(mesh):
    in_specs = (
        P(("rollout", "ctx"), None),
        P(("rollout", "ctx"), None),
        P(None, ("rollout", "ctx")),
        P("rollout", "ctx", None),
        P("rollout", "ctx", None),
        P("rollout", "ctx", None),
        P("rollout", None, "ctx"),
        P(),
        P("rollout", "ctx", None),
        P("rollout", "ctx"),
        P("rollout"),
        P(),
    )
    out_specs = (
        P(("rollout", "ctx"), None),
        P(("rollout", "ctx"), None),
        P(None, ("rollout", "ctx")),
        P("rollout", "ctx", None),
        P("rollout", "ctx", None),
        P("rollout", "ctx", None),
        P("rollout", None, "ctx"),
        P(),
    )
    return jax.shard_map(
        per_device, mesh=mesh, in_specs=in_specs, out_specs=out_specs, check_vma=False
    )
```

```python
import jax
import jax.numpy as jnp
from jax import lax
from jax.experimental import pallas as pl
from jax.experimental.pallas import tpu as pltpu
from jax.sharding import PartitionSpec as P

HEADS = 40
HEAD_DIM = 64
STATE = 128
TOKENS = 128
CHANNELS = HEADS * HEAD_DIM
PAIRS = HEADS // 2
SLICES = 16
DEVICES = SLICES * SLICES
ROWS = CHANNELS // SLICES
GO = 3 * ROWS + 8
PIECE = 32
PER_SLICE = ROWS // PIECE
F32 = jnp.float32
BF16 = jnp.bfloat16
HIGHEST = lax.Precision.HIGHEST
VMEM_BYTES = 56 * 1024 * 1024
BOTH = ("rollout", "ctx")


def iota(shape, axis):
    return lax.broadcasted_iota(jnp.int32, shape, axis)


def halves(value):
    high = value.astype(BF16)
    return high, (value - high.astype(F32)).astype(BF16)


def dot(left, right):
    return jnp.dot(left, right, preferred_element_type=F32)


def dot_t(left, right, precision=None):
    return lax.dot_general(
        left, right, (((1,), (1,)), ((), ())), preferred_element_type=F32, precision=precision
    )


def exact_dot(left, right):
    return jnp.dot(left, right, preferred_element_type=F32, precision=HIGHEST)


def running_logs(steps, rate):
    earlier = (iota((TOKENS, TOKENS), 0) <= iota((TOKENS, TOKENS), 1)).astype(F32)
    return exact_dot(-steps * rate, earlier)


def transposed(rows, before=0):
    parts = [rows, jnp.zeros((TOKENS - before - rows.shape[0], TOKENS), F32)]
    if before:
        parts = [jnp.zeros((before, TOKENS), F32)] + parts
    return jnp.concatenate(parts, axis=0).T


def as_columns(row):
    return jnp.broadcast_to(row, (TOKENS, TOKENS)).T


def pair_rows(rows, pair):
    first = jnp.broadcast_to(rows[2 * pair : 2 * pair + 1], (HEAD_DIM, TOKENS))
    second = jnp.broadcast_to(rows[2 * pair + 1 : 2 * pair + 2], (HEAD_DIM, TOKENS))
    return jnp.concatenate([first, second], axis=0)


def column(columns, head):
    return jnp.broadcast_to(columns[:, head : head + 1], (TOKENS, TOKENS))


def pieces(pair):
    for part in range(4):
        place = 4 * pair + part
        yield part * PIECE, place // PER_SLICE, (place % PER_SLICE) * PIECE


def first_lanes():
    return iota((TOKENS, TOKENS), 1) < HEAD_DIM


def sides(block):
    zero = jnp.zeros((), BF16)
    half = first_lanes()
    return jnp.concatenate([jnp.where(half, block, zero), jnp.where(half, zero, block)], axis=0)


def span(pair):
    return slice(pair * TOKENS, (pair + 1) * TOKENS)


def gather(received, pair):
    return jnp.concatenate(
        [received[owner, offset : offset + PIECE, :] for at, owner, offset in pieces(pair)], axis=0
    )


def pack_states(pack, base, tokens, rows, keys):
    twice = jnp.concatenate([keys, keys], axis=0)
    for pair in range(PAIRS):
        block = tokens[:, span(pair)].astype(F32).T
        high, low = halves(block * pair_rows(rows, pair))
        states = dot(jnp.concatenate([high, low], axis=1), twice)
        for at, owner, offset in pieces(pair):
            pack[owner, base + offset : base + offset + PIECE, :] = states[at : at + PIECE]


def rates(decay_log):
    heads = iota((HEADS, TOKENS), 0)
    logs = jnp.zeros((HEADS, TOKENS), F32)
    for head in range(HEADS):
        logs = jnp.where(heads == head, decay_log[head], logs)
    return jnp.exp(logs)


def first_kernel(
    decay_log, index, table, prompt_inputs, prompt_keys, prompt_steps, inputs, keys, queries,
    steps, upstream, mask, pack, reply_logs, prompt_logs,
):
    rate = rates(decay_log)
    running = running_logs(steps[...], rate)
    prompt_running = running_logs(prompt_steps[...], rate)
    reply_logs[...] = running
    prompt_logs[...] = prompt_running
    last = jnp.broadcast_to(running[:, TOKENS - 1 :], (HEADS, TOKENS))
    prompt_last = jnp.broadcast_to(prompt_running[:, TOKENS - 1 :], (HEADS, TOKENS))
    totals = jnp.concatenate(
        [transposed(last)[0:1], transposed(prompt_last)[0:1], jnp.zeros((6, TOKENS), F32)], axis=0
    )
    for owner in range(SLICES):
        pack[owner, 3 * ROWS :, :] = totals
    rows = jnp.exp(running) * (mask[...].astype(F32) * table[index[0]])
    pack_states(pack, 0, upstream, rows, queries[...])
    rows = jnp.exp(last - running) * steps[...]
    pack_states(pack, ROWS, inputs, rows, keys[...])
    rows = jnp.exp(prompt_last - prompt_running) * prompt_steps[...]
    pack_states(pack, 2 * ROWS, prompt_inputs, rows, prompt_keys[...])


def within_kernel(
    inputs, keys, queries, steps, upstream, mask_row, logs, near, mixed, row_sums, column_sums
):
    running = logs[...]
    columns = transposed(jnp.log(steps[...]) - running)
    causal = iota((TOKENS, TOKENS), 1) >= iota((TOKENS, TOKENS), 0)
    lanes = iota((TOKENS, TOKENS), 1)
    scores = dot_t(keys[...], queries[...])
    mask = as_columns(mask_row[...].astype(F32)).astype(BF16)
    total = jnp.zeros((TOKENS, TOKENS), F32)
    gathered = jnp.zeros((TOKENS, TOKENS), F32)
    for pair in range(PAIRS):
        pulled = upstream[:, span(pair)] * mask
        products = dot_t(sides(inputs[:, span(pair)]), pulled)
        highs, lows = [], []
        for side in range(2):
            head = 2 * pair + side
            gaps = running[head : head + 1] + column(columns, head)
            mixing = jnp.where(causal, jnp.exp(gaps), 0.0)
            weighted = mixing * products[side * TOKENS : (side + 1) * TOKENS]
            total = total + weighted
            terms = weighted * scores
            row_sums[head : head + 1, :] = jnp.sum(terms, axis=0, keepdims=True)
            gathered = jnp.where(lanes == head, jnp.sum(terms, axis=1, keepdims=True), gathered)
            high, low = halves(mixing * scores)
            highs.append(high)
            lows.append(low)
        both = sides(pulled)
        near[:, span(pair)] = dot(jnp.concatenate(highs, axis=1), both) + dot(
            jnp.concatenate(lows, axis=1), both
        )
    mixed[...] = total
    column_sums[...] = gathered.T[:HEADS]


def spread(columns, at):
    return jnp.broadcast_to(columns[:, at : at + 1], (ROWS, TOKENS))


def owner_columns(owner, rows):
    place = owner * ROWS + iota((ROWS, TOKENS), 0)
    chosen = (lax.shift_right_logical(place, 6) == iota((ROWS, TOKENS), 1)).astype(F32)
    pad = jnp.zeros((TOKENS - rows.shape[0], TOKENS), F32)
    return dot_t(chosen, jnp.concatenate([rows, pad], axis=0), HIGHEST)


def group_kernel(owner, received, after, joint, totals):
    reply = jnp.concatenate(
        [received[c, 3 * ROWS : 3 * ROWS + 1, :] for c in range(SLICES)], axis=0
    )
    prompt = jnp.concatenate(
        [received[c, 3 * ROWS + 1 : 3 * ROWS + 2, :] for c in range(SLICES)], axis=0
    )
    totals[0:SLICES, :] = reply
    totals[SLICES:, :] = prompt
    group = jnp.sum(prompt, axis=0, keepdims=True)
    logs = owner_columns(owner[0, 0], jnp.concatenate([reply, prompt, group], axis=0))
    factors = jnp.exp(logs)
    pulled = jnp.zeros((ROWS, TOKENS), F32)
    state = jnp.zeros((ROWS, TOKENS), F32)
    for c in range(SLICES):
        back = SLICES - 1 - c
        after[back] = pulled
        pulled = spread(factors, back) * pulled + received[back, 0:ROWS, :]
        state = spread(factors, SLICES + c) * state + received[c, 2 * ROWS : 3 * ROWS, :]
    joint[0:ROWS, :] = state
    joint[ROWS : 2 * ROWS, :] = pulled
    joint[2 * ROWS : 3 * ROWS, :] = spread(logs, 2 * SLICES)
    joint[3 * ROWS :, :] = jnp.broadcast_to(group, (8, TOKENS))


def carry_kernel(owner, totals, received, joint, starts, flag):
    flag[...] = joint[3 * ROWS :, :]
    factors = jnp.exp(owner_columns(owner[0, 0], totals[0:SLICES, :]))
    state = joint[0:ROWS, :]
    for c in range(SLICES):
        starts[c] = state
        if c < SLICES - 1:
            state = spread(factors, c) * state + received[c, ROWS : 2 * ROWS, :]


def backward_parts(inputs, pulls, ends, keys, near, scale, inputs_out):
    twice = jnp.concatenate([keys, keys], axis=1)
    wide = keys.astype(F32)
    lanes = iota((TOKENS, TOKENS), 1)
    half = first_lanes()
    total = jnp.zeros((TOKENS, TOKENS), F32)
    gathered = jnp.zeros((TOKENS, TOKENS), F32)
    columns = transposed(ends)
    for pair in range(PAIRS):
        high, low = halves(gather(pulls, pair))
        once = sides(inputs[:, span(pair)])
        backward = dot(
            jnp.concatenate([once, once], axis=1), jnp.concatenate([high, low], axis=0)
        )
        keyed = dot_t(twice, jnp.concatenate([high, low], axis=1))
        factors = []
        for side in range(2):
            head = 2 * pair + side
            factors.append(column(columns, head))
            part = factors[side] * backward[side * TOKENS : (side + 1) * TOKENS]
            total = total + part
            gathered = jnp.where(
                lanes == head, jnp.sum(part * wide, axis=1, keepdims=True), gathered
            )
        own = jnp.where(half, factors[0], factors[1]) * keyed
        if near is not None:
            own = near[:, span(pair)] * scale + own
        inputs_out[:, span(pair)] = own.astype(BF16)
    return total, gathered.T[:HEADS]


def reply_backward_kernel(
    index, table, inputs, keys, queries, steps, logs, pulls, near, mixed, inputs_out, keys_out, ended_out
):
    scale = table[index[0]]
    running = logs[...]
    ends = jnp.exp(running[:, TOKENS - 1 :] - running) * steps[...]
    total, ended = backward_parts(inputs, pulls, ends, keys[...], near, scale, inputs_out)
    high, low = halves(mixed[...] * scale)
    total = total + dot(high, queries[...]) + dot(low, queries[...])
    keys_out[...] = total.astype(BF16)
    ended_out[...] = ended


def log_sums(rows):
    lower = (iota((TOKENS, TOKENS), 0) < iota((TOKENS, TOKENS), 1)).astype(F32)
    return exact_dot(rows, lower)


def prompt_backward_kernel(
    owner, decay_log, inputs, keys, steps, logs, totals, later_groups, pulls, _,
    inputs_out, keys_out, owned_out, decay,
):
    rate = rates(decay_log)
    later = later_groups[...]
    for c in range(1, SLICES):
        row = totals[SLICES + c : SLICES + c + 1, :]
        later = later + jnp.where(c > owner[0, 0], row, 0.0)
    running = logs[...]
    ends = jnp.exp(running[:, TOKENS - 1 :] - running + as_columns(later)[:HEADS]) * steps[...]
    total, owned = backward_parts(inputs, pulls, ends, keys[...], None, None, inputs_out)
    keys_out[...] = total.astype(BF16)
    owned_out[...] = owned
    inside = jnp.sum(-steps[...] * rate * log_sums(owned), axis=1, keepdims=True)
    sums = jnp.sum(owned, axis=1, keepdims=True)
    logs_whole = running[:, TOKENS - 1 :]
    stacked = jnp.broadcast_to(
        jnp.concatenate([inside, sums, logs_whole], axis=0), (3 * HEADS, TOKENS)
    )
    decay[...] = transposed(stacked)[0:8]


def reply_forward_kernel(
    decay_log, index, table, keys, queries, steps, upstream, mask_row, logs, starts, pulls, mixed,
    row_sums, column_sums, ended, prompt_decay, queries_out, steps_out, summary,
):
    scale = table[index[0]]
    running = logs[...]
    rate = rates(decay_log)
    reach = transposed(jnp.exp(running) * scale)
    mask = as_columns(mask_row[...].astype(F32)).astype(BF16)
    lanes = iota((TOKENS, TOKENS), 1)
    wide = queries[...].astype(F32)
    total = jnp.zeros((TOKENS, TOKENS), F32)
    reached = jnp.zeros((TOKENS, TOKENS), F32)
    overlaps = []
    for pair in range(PAIRS):
        state = gather(starts, pair)
        shared = state * gather(pulls, pair)
        overlaps.append(jnp.sum(shared[:HEAD_DIM], axis=0, keepdims=True))
        overlaps.append(jnp.sum(shared[HEAD_DIM:], axis=0, keepdims=True))
        high, low = halves(state)
        once = sides(upstream[:, span(pair)] * mask)
        forward = dot(
            jnp.concatenate([once, once], axis=1), jnp.concatenate([high, low], axis=0)
        )
        for side in range(2):
            head = 2 * pair + side
            part = column(reach, head) * forward[side * TOKENS : (side + 1) * TOKENS]
            total = total + part
            reached = jnp.where(
                lanes == head, jnp.sum(part * wide, axis=1, keepdims=True), reached
            )
    high, low = halves((mixed[...] * scale).T)
    total = total + dot(high, keys[...]) + dot(low, keys[...])
    queries_out[...] = total.astype(BF16)
    reached = reached.T[:HEADS]
    later = (iota((TOKENS, TOKENS), 0) >= iota((TOKENS, TOKENS), 1)).astype(F32)
    carried = jnp.sum(jnp.concatenate(overlaps, axis=0), axis=1, keepdims=True)
    carried = carried * jnp.exp(running[:, TOKENS - 1 :])
    closer = column_sums[...] * scale
    log_pull = (
        exact_dot(row_sums[...] * scale - closer + reached, later) + log_sums(ended[...]) + carried
    )
    steps_out[...] = (closer + ended[...]) / steps[...] - rate * log_pull
    local = jnp.sum(-steps[...] * rate * log_pull, axis=1, keepdims=True)
    row = transposed(jnp.broadcast_to(local, (HEADS, TOKENS)))[0:1] + prompt_decay[0:1]
    summary[...] = jnp.broadcast_to(row, (DEVICES, TOKENS))


def moved_lanes(rows, by):
    shift = (iota((TOKENS, TOKENS), 0) == iota((TOKENS, TOKENS), 1) + by).astype(F32)
    return exact_dot(rows, shift)


def finish_kernel(place, decay_log, received, owned, steps, steps_out, decay):
    rows = received[...]
    below = (iota((DEVICES, DEVICES), 0) > iota((DEVICES, DEVICES), 1)).astype(F32)
    before = exact_dot(below, moved_lanes(rows, HEADS))
    decay_rows = rows + before * moved_lanes(rows, 2 * HEADS)
    decay[...] = jnp.broadcast_to(jnp.sum(decay_rows, axis=0, keepdims=True), (8, TOKENS))
    mine = jnp.where(iota((DEVICES, TOKENS), 0) < place[0, 0], rows, 0.0)
    mine = as_columns(jnp.sum(mine, axis=0, keepdims=True))[HEADS : 2 * HEADS]
    steps_out[...] = owned[...] / steps[...] - rates(decay_log) * (log_sums(owned[...]) + mine)


def whole(dims):
    return pl.BlockSpec(dims, lambda step: (0,) * len(dims))


def on_device(kernel, out_shapes, scalars, flops, *operands):
    specs = [pl.BlockSpec(memory_space=pltpu.SMEM) for _ in range(scalars)]
    specs += [whole(x.shape) for x in operands[scalars:]]
    return pl.pallas_call(
        kernel,
        grid=(1,),
        out_shape=out_shapes,
        in_specs=specs,
        out_specs=[whole(x.shape) for x in out_shapes],
        compiler_params=pltpu.CompilerParams(vmem_limit_bytes=VMEM_BYTES),
        cost_estimate=pl.CostEstimate(flops=flops, bytes_accessed=1024, transcendentals=0),
    )(*operands)


def shape(*dims, dtype=F32):
    return jax.ShapeDtypeStruct(dims, dtype)


def swap(value, axis):
    return lax.all_to_all(value, axis, 0, 0, tiled=True)


def turn(block):
    pairs = [(a * SLICES + b, b * SLICES + a) for a in range(SLICES) for b in range(SLICES)]
    return lax.ppermute(block, BOTH, pairs)


def traded(value, axis, bit):
    return lax.ppermute(value, axis, [(at, at ^ bit) for at in range(SLICES)])


def gathered_over_rows(parts, earlier, bits):
    for step, bit in bits:
        other = traded(parts, "rollout", bit)
        low = earlier[step] == 1
        first, second = jnp.where(low, parts, other), jnp.where(low, other, parts)
        parts = jnp.stack([first, second], axis=1).reshape((-1,) + parts.shape[1:])
    return parts


def per_device(
    prompt_inputs, prompt_keys, prompt_steps, reply_inputs, reply_keys, reply_queries,
    reply_steps, decay_log, upstream, loss_mask, advantage_index, advantage_table,
):
    reply_inputs, reply_keys, reply_queries = reply_inputs[0], reply_keys[0], reply_queries[0]
    reply_steps, upstream = reply_steps[0], upstream[0]
    scale = (advantage_index, advantage_table)
    row, mine = lax.axis_index("rollout"), lax.axis_index("ctx")
    place = (row * SLICES + mine).astype(jnp.int32).reshape(1, 1)
    owner = mine.astype(jnp.int32).reshape(1, 1)
    slices = shape(SLICES, ROWS, STATE)
    heads = shape(HEADS, TOKENS)
    square = shape(TOKENS, TOKENS)
    wide = shape(TOKENS, CHANNELS, dtype=BF16)
    narrow = shape(TOKENS, STATE, dtype=BF16)

    pack, reply_logs, prompt_logs = on_device(
        first_kernel, [shape(SLICES, GO, STATE), heads, heads], 3, 6 * 10**9,
        decay_log, *scale, prompt_inputs, prompt_keys, prompt_steps, reply_inputs, reply_keys,
        reply_queries, reply_steps, upstream, loss_mask,
    )
    earlier = [((row & bit) == 0).astype(jnp.int32) for bit in (1, 2, 4, 8)]
    pack, owner, place, earlier = lax.optimization_barrier((pack, owner, place, earlier))
    received = swap(pack, "ctx")
    after, joint, totals = on_device(
        group_kernel, [slices, shape(GO, STATE), shape(2 * SLICES, STATE)], 1, 3 * 10**6,
        owner, received,
    )
    after, joint, reply_logs = lax.optimization_barrier((after, joint, reply_logs))
    after = swap(after, "ctx")
    near, mixed, row_sums, column_sums = on_device(
        within_kernel, [shape(TOKENS, CHANNELS), square, heads, heads], 0, 6 * 10**6,
        reply_inputs, reply_keys, reply_queries, reply_steps, upstream, loss_mask, reply_logs,
    )
    later_groups = jnp.zeros((1, STATE), F32)
    for step, bit in enumerate((1, 2, 4, 8)):
        other = traded(joint, "rollout", bit)
        early = earlier[step] == 1
        logs, other_logs = joint[2 * ROWS : 3 * ROWS], other[2 * ROWS : 3 * ROWS]
        ours, others = joint[:ROWS], other[:ROWS]
        joined = jnp.where(
            early, jnp.exp(other_logs) * ours + others, jnp.exp(logs) * others + ours
        )
        later_groups = later_groups + jnp.where(early, other[3 * ROWS : 3 * ROWS + 1], 0.0)
        joint = jnp.concatenate([joined, joint[ROWS:] + other[ROWS:]], axis=0)
    starts, flag = on_device(
        carry_kernel, [slices, shape(8, STATE)], 1, 3 * 10**6, owner, totals, received, joint
    )
    turned = turn(joint[ROWS : 2 * ROWS])
    turned, flag, after, near = lax.optimization_barrier((turned, flag, after, near))
    starts = swap(starts, "ctx")
    end_pull = gathered_over_rows(turned[None], earlier, ((3, 8), (2, 4)))
    end_pull, after = lax.optimization_barrier((end_pull, after))
    end_pull = gathered_over_rows(end_pull, earlier, ((1, 2), (0, 1)))
    reply_inputs_out, reply_keys_out, ended = on_device(
        reply_backward_kernel, [wide, narrow, heads], 2, 6 * 10**9,
        *scale, reply_inputs, reply_keys, reply_queries, reply_steps, reply_logs, after, near,
        mixed,
    )
    prompt_inputs_out, prompt_keys_out, owned, prompt_decay = on_device(
        prompt_backward_kernel, [wide, narrow, heads, shape(8, TOKENS)], 2, 6 * 10**6,
        owner, decay_log, prompt_inputs, prompt_keys, prompt_steps, prompt_logs, totals,
        later_groups, end_pull, flag,
    )
    reply_queries_out, reply_steps_out, summary = on_device(
        reply_forward_kernel, [narrow, heads, shape(DEVICES, TOKENS)], 3, 6 * 10**6,
        decay_log, *scale, reply_keys, reply_queries, reply_steps, upstream, loss_mask,
        reply_logs, starts, after, mixed, row_sums, column_sums, ended, prompt_decay,
    )
    prompt_steps_out, decay = on_device(
        finish_kernel, [heads, shape(8, TOKENS)], 2, 10**8,
        place, decay_log, swap(summary, BOTH), owned, prompt_steps,
    )
    return (
        prompt_inputs_out, prompt_keys_out, prompt_steps_out, reply_inputs_out[None],
        reply_keys_out[None], reply_queries_out[None], reply_steps_out[None], decay[0, :HEADS],
    )


def solution(mesh):
    in_specs = (
        P(("rollout", "ctx"), None),
        P(("rollout", "ctx"), None),
        P(None, ("rollout", "ctx")),
        P("rollout", "ctx", None),
        P("rollout", "ctx", None),
        P("rollout", "ctx", None),
        P("rollout", None, "ctx"),
        P(),
        P("rollout", "ctx", None),
        P("rollout", "ctx"),
        P("rollout"),
        P(),
    )
    out_specs = (
        P(("rollout", "ctx"), None),
        P(("rollout", "ctx"), None),
        P(None, ("rollout", "ctx")),
        P("rollout", "ctx", None),
        P("rollout", "ctx", None),
        P("rollout", "ctx", None),
        P("rollout", None, "ctx"),
        P(),
    )
    return jax.shard_map(
        per_device, mesh=mesh, in_specs=in_specs, out_specs=out_specs, check_vma=False
    )
```

```python
import jax
import jax.numpy as jnp
from jax import lax
from jax.experimental import pallas as pl
from jax.experimental.pallas import tpu as pltpu
from jax.sharding import PartitionSpec as P

HEADS = 40
HEAD_DIM = 64
STATE = 128
TOKENS = 128
CHANNELS = HEADS * HEAD_DIM
PAIRS = HEADS // 2
SLICES = 16
DEVICES = SLICES * SLICES
ROWS = CHANNELS // SLICES
GO = 3 * ROWS + 8
PIECE = 32
PER_SLICE = ROWS // PIECE
F32 = jnp.float32
BF16 = jnp.bfloat16
HIGHEST = lax.Precision.HIGHEST
VMEM_BYTES = 24 * 1024 * 1024
BOTH = ("rollout", "ctx")


def iota(shape, axis):
    return lax.broadcasted_iota(jnp.int32, shape, axis)


def halves(value):
    high = value.astype(BF16)
    return high, (value - high.astype(F32)).astype(BF16)


def dot(left, right):
    return jnp.dot(left, right, preferred_element_type=F32)


def dot_t(left, right, precision=None):
    return lax.dot_general(
        left, right, (((1,), (1,)), ((), ())), preferred_element_type=F32, precision=precision
    )


def exact_dot(left, right):
    return jnp.dot(left, right, preferred_element_type=F32, precision=HIGHEST)


def running_logs(steps, rate):
    earlier = (iota((TOKENS, TOKENS), 0) <= iota((TOKENS, TOKENS), 1)).astype(F32)
    return exact_dot(-steps * rate, earlier)


def transposed(rows, before=0):
    parts = [rows, jnp.zeros((TOKENS - before - rows.shape[0], TOKENS), F32)]
    if before:
        parts = [jnp.zeros((before, TOKENS), F32)] + parts
    return jnp.concatenate(parts, axis=0).T


def as_columns(row):
    return jnp.broadcast_to(row, (TOKENS, TOKENS)).T


def pair_rows(rows, pair):
    first = jnp.broadcast_to(rows[2 * pair : 2 * pair + 1], (HEAD_DIM, TOKENS))
    second = jnp.broadcast_to(rows[2 * pair + 1 : 2 * pair + 2], (HEAD_DIM, TOKENS))
    return jnp.concatenate([first, second], axis=0)


def column(columns, head):
    return jnp.broadcast_to(columns[:, head : head + 1], (TOKENS, TOKENS))


def pieces(pair):
    for part in range(4):
        place = 4 * pair + part
        yield part * PIECE, place // PER_SLICE, (place % PER_SLICE) * PIECE


def first_lanes():
    return iota((TOKENS, TOKENS), 1) < HEAD_DIM


def sides(block):
    zero = jnp.zeros((), BF16)
    half = first_lanes()
    return jnp.concatenate([jnp.where(half, block, zero), jnp.where(half, zero, block)], axis=0)


def span(pair):
    return slice(pair * TOKENS, (pair + 1) * TOKENS)


def gather(received, pair):
    return jnp.concatenate(
        [received[owner, offset : offset + PIECE, :] for at, owner, offset in pieces(pair)], axis=0
    )


def pack_states(pack, base, tokens, rows, keys):
    twice = jnp.concatenate([keys, keys], axis=0)
    for pair in range(PAIRS):
        block = tokens[:, span(pair)].astype(F32).T
        high, low = halves(block * pair_rows(rows, pair))
        states = dot(jnp.concatenate([high, low], axis=1), twice)
        for at, owner, offset in pieces(pair):
            pack[owner, base + offset : base + offset + PIECE, :] = states[at : at + PIECE]


def rates(decay_log):
    heads = iota((HEADS, TOKENS), 0)
    logs = jnp.zeros((HEADS, TOKENS), F32)
    for head in range(HEADS):
        logs = jnp.where(heads == head, decay_log[head], logs)
    return jnp.exp(logs)


def first_kernel(
    decay_log, index, table, prompt_inputs, prompt_keys, prompt_steps, inputs, keys, queries,
    steps, upstream, mask, pack, reply_logs, prompt_logs,
):
    rate = rates(decay_log)
    running = running_logs(steps[...], rate)
    prompt_running = running_logs(prompt_steps[...], rate)
    reply_logs[...] = running
    prompt_logs[...] = prompt_running
    last = jnp.broadcast_to(running[:, TOKENS - 1 :], (HEADS, TOKENS))
    prompt_last = jnp.broadcast_to(prompt_running[:, TOKENS - 1 :], (HEADS, TOKENS))
    totals = jnp.concatenate(
        [transposed(last)[0:1], transposed(prompt_last)[0:1], jnp.zeros((6, TOKENS), F32)], axis=0
    )
    for owner in range(SLICES):
        pack[owner, 3 * ROWS :, :] = totals
    rows = jnp.exp(running) * (mask[...].astype(F32) * table[index[0]])
    pack_states(pack, 0, upstream, rows, queries[...])
    rows = jnp.exp(last - running) * steps[...]
    pack_states(pack, ROWS, inputs, rows, keys[...])
    rows = jnp.exp(prompt_last - prompt_running) * prompt_steps[...]
    pack_states(pack, 2 * ROWS, prompt_inputs, rows, prompt_keys[...])


def within_kernel(
    inputs, keys, queries, steps, upstream, mask_row, logs, near, mixed, row_sums, column_sums
):
    running = logs[...]
    columns = transposed(jnp.log(steps[...]) - running)
    causal = iota((TOKENS, TOKENS), 1) >= iota((TOKENS, TOKENS), 0)
    lanes = iota((TOKENS, TOKENS), 1)
    scores = dot_t(keys[...], queries[...])
    mask = as_columns(mask_row[...].astype(F32)).astype(BF16)
    total = jnp.zeros((TOKENS, TOKENS), F32)
    gathered = jnp.zeros((TOKENS, TOKENS), F32)
    for pair in range(PAIRS):
        pulled = upstream[:, span(pair)] * mask
        products = dot_t(sides(inputs[:, span(pair)]), pulled)
        highs, lows = [], []
        for side in range(2):
            head = 2 * pair + side
            gaps = running[head : head + 1] + column(columns, head)
            mixing = jnp.where(causal, jnp.exp(gaps), 0.0)
            weighted = mixing * products[side * TOKENS : (side + 1) * TOKENS]
            total = total + weighted
            terms = weighted * scores
            row_sums[head : head + 1, :] = jnp.sum(terms, axis=0, keepdims=True)
            gathered = jnp.where(lanes == head, jnp.sum(terms, axis=1, keepdims=True), gathered)
            high, low = halves(mixing * scores)
            highs.append(high)
            lows.append(low)
        both = sides(pulled)
        near[:, span(pair)] = dot(jnp.concatenate(highs, axis=1), both) + dot(
            jnp.concatenate(lows, axis=1), both
        )
    mixed[...] = total
    column_sums[...] = gathered.T[:HEADS]


def spread(columns, at):
    return jnp.broadcast_to(columns[:, at : at + 1], (ROWS, TOKENS))


def owner_columns(owner, rows):
    place = owner * ROWS + iota((ROWS, TOKENS), 0)
    chosen = (lax.shift_right_logical(place, 6) == iota((ROWS, TOKENS), 1)).astype(F32)
    pad = jnp.zeros((TOKENS - rows.shape[0], TOKENS), F32)
    return dot_t(chosen, jnp.concatenate([rows, pad], axis=0), HIGHEST)


def group_kernel(owner, received, after, joint, totals):
    reply = jnp.concatenate(
        [received[c, 3 * ROWS : 3 * ROWS + 1, :] for c in range(SLICES)], axis=0
    )
    prompt = jnp.concatenate(
        [received[c, 3 * ROWS + 1 : 3 * ROWS + 2, :] for c in range(SLICES)], axis=0
    )
    totals[0:SLICES, :] = reply
    totals[SLICES:, :] = prompt
    group = jnp.sum(prompt, axis=0, keepdims=True)
    logs = owner_columns(owner[0, 0], jnp.concatenate([reply, prompt, group], axis=0))
    factors = jnp.exp(logs)
    pulled = jnp.zeros((ROWS, TOKENS), F32)
    state = jnp.zeros((ROWS, TOKENS), F32)
    for c in range(SLICES):
        back = SLICES - 1 - c
        after[back] = pulled
        pulled = spread(factors, back) * pulled + received[back, 0:ROWS, :]
        state = spread(factors, SLICES + c) * state + received[c, 2 * ROWS : 3 * ROWS, :]
    joint[0:ROWS, :] = state
    joint[ROWS : 2 * ROWS, :] = pulled
    joint[2 * ROWS : 3 * ROWS, :] = spread(logs, 2 * SLICES)
    joint[3 * ROWS :, :] = jnp.broadcast_to(group, (8, TOKENS))


def carry_kernel(owner, totals, received, joint, starts, flag):
    flag[...] = joint[3 * ROWS :, :]
    factors = jnp.exp(owner_columns(owner[0, 0], totals[0:SLICES, :]))
    state = joint[0:ROWS, :]
    for c in range(SLICES):
        starts[c] = state
        if c < SLICES - 1:
            state = spread(factors, c) * state + received[c, ROWS : 2 * ROWS, :]


def backward_parts(inputs, pulls, ends, keys, near, scale, inputs_out):
    twice = jnp.concatenate([keys, keys], axis=1)
    wide = keys.astype(F32)
    lanes = iota((TOKENS, TOKENS), 1)
    half = first_lanes()
    total = jnp.zeros((TOKENS, TOKENS), F32)
    gathered = jnp.zeros((TOKENS, TOKENS), F32)
    columns = transposed(ends)
    for pair in range(PAIRS):
        high, low = halves(gather(pulls, pair))
        once = sides(inputs[:, span(pair)])
        backward = dot(
            jnp.concatenate([once, once], axis=1), jnp.concatenate([high, low], axis=0)
        )
        keyed = dot_t(twice, jnp.concatenate([high, low], axis=1))
        factors = []
        for side in range(2):
            head = 2 * pair + side
            factors.append(column(columns, head))
            part = factors[side] * backward[side * TOKENS : (side + 1) * TOKENS]
            total = total + part
            gathered = jnp.where(
                lanes == head, jnp.sum(part * wide, axis=1, keepdims=True), gathered
            )
        own = jnp.where(half, factors[0], factors[1]) * keyed
        if near is not None:
            own = near[:, span(pair)] * scale + own
        inputs_out[:, span(pair)] = own.astype(BF16)
    return total, gathered.T[:HEADS]


def reply_backward_kernel(
    index, table, inputs, keys, queries, steps, logs, pulls, near, mixed, inputs_out, keys_out, ended_out
):
    scale = table[index[0]]
    running = logs[...]
    ends = jnp.exp(running[:, TOKENS - 1 :] - running) * steps[...]
    total, ended = backward_parts(inputs, pulls, ends, keys[...], near, scale, inputs_out)
    high, low = halves(mixed[...] * scale)
    total = total + dot(high, queries[...]) + dot(low, queries[...])
    keys_out[...] = total.astype(BF16)
    ended_out[...] = ended


def log_sums(rows):
    lower = (iota((TOKENS, TOKENS), 0) < iota((TOKENS, TOKENS), 1)).astype(F32)
    return exact_dot(rows, lower)


def prompt_backward_kernel(
    owner, decay_log, inputs, keys, steps, logs, totals, later_groups, pulls, _,
    inputs_out, keys_out, owned_out, decay,
):
    rate = rates(decay_log)
    later = later_groups[...]
    for c in range(1, SLICES):
        row = totals[SLICES + c : SLICES + c + 1, :]
        later = later + jnp.where(c > owner[0, 0], row, 0.0)
    running = logs[...]
    ends = jnp.exp(running[:, TOKENS - 1 :] - running + as_columns(later)[:HEADS]) * steps[...]
    total, owned = backward_parts(inputs, pulls, ends, keys[...], None, None, inputs_out)
    keys_out[...] = total.astype(BF16)
    owned_out[...] = owned
    inside = jnp.sum(-steps[...] * rate * log_sums(owned), axis=1, keepdims=True)
    sums = jnp.sum(owned, axis=1, keepdims=True)
    logs_whole = running[:, TOKENS - 1 :]
    stacked = jnp.broadcast_to(
        jnp.concatenate([inside, sums, logs_whole], axis=0), (3 * HEADS, TOKENS)
    )
    decay[...] = transposed(stacked)[0:8]


def reply_forward_kernel(
    decay_log, index, table, keys, queries, steps, upstream, mask_row, logs, starts, pulls, mixed,
    row_sums, column_sums, ended, prompt_decay, queries_out, steps_out, summary,
):
    scale = table[index[0]]
    running = logs[...]
    rate = rates(decay_log)
    reach = transposed(jnp.exp(running) * scale)
    mask = as_columns(mask_row[...].astype(F32)).astype(BF16)
    lanes = iota((TOKENS, TOKENS), 1)
    wide = queries[...].astype(F32)
    total = jnp.zeros((TOKENS, TOKENS), F32)
    reached = jnp.zeros((TOKENS, TOKENS), F32)
    overlaps = []
    for pair in range(PAIRS):
        state = gather(starts, pair)
        shared = state * gather(pulls, pair)
        overlaps.append(jnp.sum(shared[:HEAD_DIM], axis=0, keepdims=True))
        overlaps.append(jnp.sum(shared[HEAD_DIM:], axis=0, keepdims=True))
        high, low = halves(state)
        once = sides(upstream[:, span(pair)] * mask)
        forward = dot(
            jnp.concatenate([once, once], axis=1), jnp.concatenate([high, low], axis=0)
        )
        for side in range(2):
            head = 2 * pair + side
            part = column(reach, head) * forward[side * TOKENS : (side + 1) * TOKENS]
            total = total + part
            reached = jnp.where(
                lanes == head, jnp.sum(part * wide, axis=1, keepdims=True), reached
            )
    high, low = halves((mixed[...] * scale).T)
    total = total + dot(high, keys[...]) + dot(low, keys[...])
    queries_out[...] = total.astype(BF16)
    reached = reached.T[:HEADS]
    later = (iota((TOKENS, TOKENS), 0) >= iota((TOKENS, TOKENS), 1)).astype(F32)
    carried = jnp.sum(jnp.concatenate(overlaps, axis=0), axis=1, keepdims=True)
    carried = carried * jnp.exp(running[:, TOKENS - 1 :])
    closer = column_sums[...] * scale
    log_pull = (
        exact_dot(row_sums[...] * scale - closer + reached, later) + log_sums(ended[...]) + carried
    )
    steps_out[...] = (closer + ended[...]) / steps[...] - rate * log_pull
    local = jnp.sum(-steps[...] * rate * log_pull, axis=1, keepdims=True)
    row = transposed(jnp.broadcast_to(local, (HEADS, TOKENS)))[0:1] + prompt_decay[0:1]
    summary[...] = jnp.broadcast_to(row, (DEVICES, TOKENS))


def moved_lanes(rows, by):
    shift = (iota((TOKENS, TOKENS), 0) == iota((TOKENS, TOKENS), 1) + by).astype(F32)
    return exact_dot(rows, shift)


def finish_kernel(place, decay_log, received, owned, steps, steps_out, decay):
    rows = received[...]
    below = (iota((DEVICES, DEVICES), 0) > iota((DEVICES, DEVICES), 1)).astype(F32)
    before = exact_dot(below, moved_lanes(rows, HEADS))
    decay_rows = rows + before * moved_lanes(rows, 2 * HEADS)
    decay[...] = jnp.broadcast_to(jnp.sum(decay_rows, axis=0, keepdims=True), (8, TOKENS))
    mine = jnp.where(iota((DEVICES, TOKENS), 0) < place[0, 0], rows, 0.0)
    mine = as_columns(jnp.sum(mine, axis=0, keepdims=True))[HEADS : 2 * HEADS]
    steps_out[...] = owned[...] / steps[...] - rates(decay_log) * (log_sums(owned[...]) + mine)


def whole(dims):
    return pl.BlockSpec(dims, lambda step: (0,) * len(dims))


def on_device(kernel, out_shapes, scalars, flops, *operands):
    specs = [pl.BlockSpec(memory_space=pltpu.SMEM) for _ in range(scalars)]
    specs += [whole(x.shape) for x in operands[scalars:]]
    return pl.pallas_call(
        kernel,
        grid=(1,),
        out_shape=out_shapes,
        in_specs=specs,
        out_specs=[whole(x.shape) for x in out_shapes],
        compiler_params=pltpu.CompilerParams(vmem_limit_bytes=VMEM_BYTES),
        cost_estimate=pl.CostEstimate(flops=flops, bytes_accessed=1024, transcendentals=0),
    )(*operands)


def shape(*dims, dtype=F32):
    return jax.ShapeDtypeStruct(dims, dtype)


def swap(value, axis):
    return lax.all_to_all(value, axis, 0, 0, tiled=True)


def turn(block):
    pairs = [(a * SLICES + b, b * SLICES + a) for a in range(SLICES) for b in range(SLICES)]
    return lax.ppermute(block, BOTH, pairs)


def traded(value, axis, bit):
    return lax.ppermute(value, axis, [(at, at ^ bit) for at in range(SLICES)])


def gathered_over_rows(parts, earlier, bits):
    for step, bit in bits:
        other = traded(parts, "rollout", bit)
        low = earlier[step] == 1
        first, second = jnp.where(low, parts, other), jnp.where(low, other, parts)
        parts = jnp.stack([first, second], axis=1).reshape((-1,) + parts.shape[1:])
    return parts


def per_device(
    prompt_inputs, prompt_keys, prompt_steps, reply_inputs, reply_keys, reply_queries,
    reply_steps, decay_log, upstream, loss_mask, advantage_index, advantage_table,
):
    reply_inputs, reply_keys, reply_queries = reply_inputs[0], reply_keys[0], reply_queries[0]
    reply_steps, upstream = reply_steps[0], upstream[0]
    scale = (advantage_index, advantage_table)
    row, mine = lax.axis_index("rollout"), lax.axis_index("ctx")
    place = (row * SLICES + mine).astype(jnp.int32).reshape(1, 1)
    owner = mine.astype(jnp.int32).reshape(1, 1)
    slices = shape(SLICES, ROWS, STATE)
    heads = shape(HEADS, TOKENS)
    square = shape(TOKENS, TOKENS)
    wide = shape(TOKENS, CHANNELS, dtype=BF16)
    narrow = shape(TOKENS, STATE, dtype=BF16)

    pack, reply_logs, prompt_logs = on_device(
        first_kernel, [shape(SLICES, GO, STATE), heads, heads], 3, 6 * 10**9,
        decay_log, *scale, prompt_inputs, prompt_keys, prompt_steps, reply_inputs, reply_keys,
        reply_queries, reply_steps, upstream, loss_mask,
    )
    earlier = [((row & bit) == 0).astype(jnp.int32) for bit in (1, 2, 4, 8)]
    pack, owner, place, earlier = lax.optimization_barrier((pack, owner, place, earlier))
    received = swap(pack, "ctx")
    after, joint, totals = on_device(
        group_kernel, [slices, shape(GO, STATE), shape(2 * SLICES, STATE)], 1, 3 * 10**6,
        owner, received,
    )
    after, joint, reply_logs = lax.optimization_barrier((after, joint, reply_logs))
    after = swap(after, "ctx")
    near, mixed, row_sums, column_sums = on_device(
        within_kernel, [shape(TOKENS, CHANNELS), square, heads, heads], 0, 6 * 10**6,
        reply_inputs, reply_keys, reply_queries, reply_steps, upstream, loss_mask, reply_logs,
    )
    later_groups = jnp.zeros((1, STATE), F32)
    for step, bit in enumerate((1, 2, 4, 8)):
        other = traded(joint, "rollout", bit)
        early = earlier[step] == 1
        logs, other_logs = joint[2 * ROWS : 3 * ROWS], other[2 * ROWS : 3 * ROWS]
        ours, others = joint[:ROWS], other[:ROWS]
        joined = jnp.where(
            early, jnp.exp(other_logs) * ours + others, jnp.exp(logs) * others + ours
        )
        later_groups = later_groups + jnp.where(early, other[3 * ROWS : 3 * ROWS + 1], 0.0)
        joint = jnp.concatenate([joined, joint[ROWS:] + other[ROWS:]], axis=0)
    starts, flag = on_device(
        carry_kernel, [slices, shape(8, STATE)], 1, 3 * 10**6, owner, totals, received, joint
    )
    turned = turn(joint[ROWS : 2 * ROWS])
    turned, flag, after, near = lax.optimization_barrier((turned, flag, after, near))
    starts = swap(starts, "ctx")
    end_pull = gathered_over_rows(turned[None], earlier, ((3, 8), (2, 4)))
    end_pull, after = lax.optimization_barrier((end_pull, after))
    end_pull = gathered_over_rows(end_pull, earlier, ((1, 2), (0, 1)))
    reply_inputs_out, reply_keys_out, ended = on_device(
        reply_backward_kernel, [wide, narrow, heads], 2, 6 * 10**9,
        *scale, reply_inputs, reply_keys, reply_queries, reply_steps, reply_logs, after, near,
        mixed,
    )
    prompt_inputs_out, prompt_keys_out, owned, prompt_decay = on_device(
        prompt_backward_kernel, [wide, narrow, heads, shape(8, TOKENS)], 2, 6 * 10**6,
        owner, decay_log, prompt_inputs, prompt_keys, prompt_steps, prompt_logs, totals,
        later_groups, end_pull, flag,
    )
    reply_queries_out, reply_steps_out, summary = on_device(
        reply_forward_kernel, [narrow, heads, shape(DEVICES, TOKENS)], 3, 6 * 10**6,
        decay_log, *scale, reply_keys, reply_queries, reply_steps, upstream, loss_mask,
        reply_logs, starts, after, mixed, row_sums, column_sums, ended, prompt_decay,
    )
    prompt_steps_out, decay = on_device(
        finish_kernel, [heads, shape(8, TOKENS)], 2, 10**8,
        place, decay_log, swap(summary, BOTH), owned, prompt_steps,
    )
    return (
        prompt_inputs_out, prompt_keys_out, prompt_steps_out, reply_inputs_out[None],
        reply_keys_out[None], reply_queries_out[None], reply_steps_out[None], decay[0, :HEADS],
    )


def solution(mesh):
    in_specs = (
        P(("rollout", "ctx"), None),
        P(("rollout", "ctx"), None),
        P(None, ("rollout", "ctx")),
        P("rollout", "ctx", None),
        P("rollout", "ctx", None),
        P("rollout", "ctx", None),
        P("rollout", None, "ctx"),
        P(),
        P("rollout", "ctx", None),
        P("rollout", "ctx"),
        P("rollout"),
        P(),
    )
    out_specs = (
        P(("rollout", "ctx"), None),
        P(("rollout", "ctx"), None),
        P(None, ("rollout", "ctx")),
        P("rollout", "ctx", None),
        P("rollout", "ctx", None),
        P("rollout", "ctx", None),
        P("rollout", None, "ctx"),
        P(),
    )
    return jax.shard_map(
        per_device, mesh=mesh, in_specs=in_specs, out_specs=out_specs, check_vma=False
    )
```

```python
import jax
import jax.numpy as jnp
from jax import lax
from jax.experimental import pallas as pl
from jax.experimental.pallas import tpu as pltpu
from jax.sharding import PartitionSpec as P

HEADS = 40
HEAD_DIM = 64
STATE = 128
TOKENS = 128
CHANNELS = HEADS * HEAD_DIM
PAIRS = HEADS // 2
SLICES = 16
DEVICES = SLICES * SLICES
ROWS = CHANNELS // SLICES
GO = 3 * ROWS + 8
PIECE = 32
PER_SLICE = ROWS // PIECE
F32 = jnp.float32
BF16 = jnp.bfloat16
HIGHEST = lax.Precision.HIGHEST
VMEM_BYTES = 24 * 1024 * 1024
VMEM_MOST = 56 * 1024 * 1024
DOUBLING = (2, 8, 4, 1)
BOTH = ("rollout", "ctx")


def iota(shape, axis):
    return lax.broadcasted_iota(jnp.int32, shape, axis)


def halves(value):
    high = value.astype(BF16)
    return high, (value - high.astype(F32)).astype(BF16)


def dot(left, right):
    return jnp.dot(left, right, preferred_element_type=F32)


def dot_t(left, right, precision=None):
    return lax.dot_general(
        left, right, (((1,), (1,)), ((), ())), preferred_element_type=F32, precision=precision
    )


def exact_dot(left, right):
    return jnp.dot(left, right, preferred_element_type=F32, precision=HIGHEST)


def running_logs(steps, rate):
    earlier = (iota((TOKENS, TOKENS), 0) <= iota((TOKENS, TOKENS), 1)).astype(F32)
    return exact_dot(-steps * rate, earlier)


def transposed(rows, before=0):
    parts = [rows, jnp.zeros((TOKENS - before - rows.shape[0], TOKENS), F32)]
    if before:
        parts = [jnp.zeros((before, TOKENS), F32)] + parts
    return jnp.concatenate(parts, axis=0).T


def as_columns(row):
    return jnp.broadcast_to(row, (TOKENS, TOKENS)).T


def pair_rows(rows, pair):
    first = jnp.broadcast_to(rows[2 * pair : 2 * pair + 1], (HEAD_DIM, TOKENS))
    second = jnp.broadcast_to(rows[2 * pair + 1 : 2 * pair + 2], (HEAD_DIM, TOKENS))
    return jnp.concatenate([first, second], axis=0)


def column(columns, head):
    return jnp.broadcast_to(columns[:, head : head + 1], (TOKENS, TOKENS))


def pieces(pair):
    for part in range(4):
        place = 4 * pair + part
        yield part * PIECE, place // PER_SLICE, (place % PER_SLICE) * PIECE


def first_lanes():
    return iota((TOKENS, TOKENS), 1) < HEAD_DIM


def sides(block):
    zero = jnp.zeros((), BF16)
    half = first_lanes()
    return jnp.concatenate([jnp.where(half, block, zero), jnp.where(half, zero, block)], axis=0)


def span(pair):
    return slice(pair * TOKENS, (pair + 1) * TOKENS)


def gather(received, pair, order=None):
    places = order or range(SLICES)
    return jnp.concatenate(
        [
            received[places[owner], offset : offset + PIECE, :]
            for at, owner, offset in pieces(pair)
        ],
        axis=0,
    )


def doubled_order():
    places = []
    for owner in range(SLICES):
        place = 0
        for bit in DOUBLING:
            place = 2 * place + (1 if owner & bit else 0)
        places.append(place)
    return places


def pack_states(pack, base, tokens, rows, keys):
    twice = jnp.concatenate([keys, keys], axis=0)
    for pair in range(PAIRS):
        block = tokens[:, span(pair)].astype(F32).T
        high, low = halves(block * pair_rows(rows, pair))
        states = dot(jnp.concatenate([high, low], axis=1), twice)
        for at, owner, offset in pieces(pair):
            pack[owner, base + offset : base + offset + PIECE, :] = states[at : at + PIECE]


def rates(decay_log):
    heads = iota((HEADS, TOKENS), 0)
    logs = jnp.zeros((HEADS, TOKENS), F32)
    for head in range(HEADS):
        logs = jnp.where(heads == head, decay_log[head], logs)
    return jnp.exp(logs)


def first_kernel(
    decay_log, index, table, prompt_inputs, prompt_keys, prompt_steps, inputs, keys, queries,
    steps, upstream, mask, pack, reply_logs, prompt_logs,
):
    rate = rates(decay_log)
    running = running_logs(steps[...], rate)
    prompt_running = running_logs(prompt_steps[...], rate)
    reply_logs[...] = running
    prompt_logs[...] = prompt_running
    last = jnp.broadcast_to(running[:, TOKENS - 1 :], (HEADS, TOKENS))
    prompt_last = jnp.broadcast_to(prompt_running[:, TOKENS - 1 :], (HEADS, TOKENS))
    totals = jnp.concatenate(
        [transposed(last)[0:1], transposed(prompt_last)[0:1], jnp.zeros((6, TOKENS), F32)], axis=0
    )
    for owner in range(SLICES):
        pack[owner, 3 * ROWS :, :] = totals
    rows = jnp.exp(running) * (mask[...].astype(F32) * table[index[0]])
    pack_states(pack, 0, upstream, rows, queries[...])
    rows = jnp.exp(last - running) * steps[...]
    pack_states(pack, ROWS, inputs, rows, keys[...])
    rows = jnp.exp(prompt_last - prompt_running) * prompt_steps[...]
    pack_states(pack, 2 * ROWS, prompt_inputs, rows, prompt_keys[...])


def within_kernel(
    inputs, keys, queries, steps, upstream, mask_row, logs, near, mixed, row_sums, column_sums
):
    running = logs[...]
    columns = transposed(jnp.log(steps[...]) - running)
    causal = iota((TOKENS, TOKENS), 1) >= iota((TOKENS, TOKENS), 0)
    lanes = iota((TOKENS, TOKENS), 1)
    scores = dot_t(keys[...], queries[...])
    mask = as_columns(mask_row[...].astype(F32)).astype(BF16)
    total = jnp.zeros((TOKENS, TOKENS), F32)
    gathered = jnp.zeros((TOKENS, TOKENS), F32)
    for pair in range(PAIRS):
        pulled = upstream[:, span(pair)] * mask
        products = dot_t(sides(inputs[:, span(pair)]), pulled)
        highs, lows = [], []
        for side in range(2):
            head = 2 * pair + side
            gaps = running[head : head + 1] + column(columns, head)
            mixing = jnp.where(causal, jnp.exp(gaps), 0.0)
            weighted = mixing * products[side * TOKENS : (side + 1) * TOKENS]
            total = total + weighted
            terms = weighted * scores
            row_sums[head : head + 1, :] = jnp.sum(terms, axis=0, keepdims=True)
            gathered = jnp.where(lanes == head, jnp.sum(terms, axis=1, keepdims=True), gathered)
            high, low = halves(mixing * scores)
            highs.append(high)
            lows.append(low)
        both = sides(pulled)
        near[:, span(pair)] = dot(jnp.concatenate(highs, axis=1), both) + dot(
            jnp.concatenate(lows, axis=1), both
        )
    mixed[...] = total
    column_sums[...] = gathered.T[:HEADS]


def spread(columns, at):
    return jnp.broadcast_to(columns[:, at : at + 1], (ROWS, TOKENS))


def owner_columns(owner, rows):
    place = owner * ROWS + iota((ROWS, TOKENS), 0)
    chosen = (lax.shift_right_logical(place, 6) == iota((ROWS, TOKENS), 1)).astype(F32)
    pad = jnp.zeros((TOKENS - rows.shape[0], TOKENS), F32)
    return dot_t(chosen, jnp.concatenate([rows, pad], axis=0), HIGHEST)


def group_kernel(owner, received, after, joint, totals):
    reply = jnp.concatenate(
        [received[c, 3 * ROWS : 3 * ROWS + 1, :] for c in range(SLICES)], axis=0
    )
    prompt = jnp.concatenate(
        [received[c, 3 * ROWS + 1 : 3 * ROWS + 2, :] for c in range(SLICES)], axis=0
    )
    totals[0:SLICES, :] = reply
    totals[SLICES:, :] = prompt
    group = jnp.sum(prompt, axis=0, keepdims=True)
    logs = owner_columns(owner[0, 0], jnp.concatenate([reply, prompt, group], axis=0))
    factors = jnp.exp(logs)
    pulled = jnp.zeros((ROWS, TOKENS), F32)
    state = jnp.zeros((ROWS, TOKENS), F32)
    for c in range(SLICES):
        back = SLICES - 1 - c
        after[back] = pulled
        pulled = spread(factors, back) * pulled + received[back, 0:ROWS, :]
        state = spread(factors, SLICES + c) * state + received[c, 2 * ROWS : 3 * ROWS, :]
    joint[0:ROWS, :] = state
    joint[ROWS : 2 * ROWS, :] = pulled
    joint[2 * ROWS : 3 * ROWS, :] = spread(logs, 2 * SLICES)
    joint[3 * ROWS :, :] = jnp.broadcast_to(group, (8, TOKENS))


def carry_kernel(owner, totals, received, joint, starts, flag):
    flag[...] = joint[3 * ROWS :, :]
    factors = jnp.exp(owner_columns(owner[0, 0], totals[0:SLICES, :]))
    state = joint[0:ROWS, :]
    for c in range(SLICES):
        starts[c] = state
        if c < SLICES - 1:
            state = spread(factors, c) * state + received[c, ROWS : 2 * ROWS, :]


def backward_parts(inputs, pulls, ends, keys, near, scale, inputs_out, order=None):
    twice = jnp.concatenate([keys, keys], axis=1)
    wide = keys.astype(F32)
    lanes = iota((TOKENS, TOKENS), 1)
    half = first_lanes()
    total = jnp.zeros((TOKENS, TOKENS), F32)
    gathered = jnp.zeros((TOKENS, TOKENS), F32)
    columns = transposed(ends)
    for pair in range(PAIRS):
        high, low = halves(gather(pulls, pair, order))
        once = sides(inputs[:, span(pair)])
        backward = dot(
            jnp.concatenate([once, once], axis=1), jnp.concatenate([high, low], axis=0)
        )
        keyed = dot_t(twice, jnp.concatenate([high, low], axis=1))
        factors = []
        for side in range(2):
            head = 2 * pair + side
            factors.append(column(columns, head))
            part = factors[side] * backward[side * TOKENS : (side + 1) * TOKENS]
            total = total + part
            gathered = jnp.where(
                lanes == head, jnp.sum(part * wide, axis=1, keepdims=True), gathered
            )
        own = jnp.where(half, factors[0], factors[1]) * keyed
        if near is not None:
            own = near[:, span(pair)] * scale + own
        inputs_out[:, span(pair)] = own.astype(BF16)
    return total, gathered.T[:HEADS]


def reply_backward_kernel(
    index, table, inputs, keys, queries, steps, logs, pulls, near, mixed, inputs_out, keys_out, ended_out
):
    scale = table[index[0]]
    running = logs[...]
    ends = jnp.exp(running[:, TOKENS - 1 :] - running) * steps[...]
    total, ended = backward_parts(inputs, pulls, ends, keys[...], near, scale, inputs_out)
    high, low = halves(mixed[...] * scale)
    total = total + dot(high, queries[...]) + dot(low, queries[...])
    keys_out[...] = total.astype(BF16)
    ended_out[...] = ended


def log_sums(rows):
    lower = (iota((TOKENS, TOKENS), 0) < iota((TOKENS, TOKENS), 1)).astype(F32)
    return exact_dot(rows, lower)


def prompt_backward_kernel(
    owner, decay_log, inputs, keys, steps, logs, totals, later_groups, pulls, _,
    inputs_out, keys_out, owned_out, decay,
):
    rate = rates(decay_log)
    later = later_groups[...]
    for c in range(1, SLICES):
        row = totals[SLICES + c : SLICES + c + 1, :]
        later = later + jnp.where(c > owner[0, 0], row, 0.0)
    running = logs[...]
    ends = jnp.exp(running[:, TOKENS - 1 :] - running + as_columns(later)[:HEADS]) * steps[...]
    total, owned = backward_parts(
        inputs, pulls, ends, keys[...], None, None, inputs_out, doubled_order()
    )
    keys_out[...] = total.astype(BF16)
    owned_out[...] = owned
    inside = jnp.sum(-steps[...] * rate * log_sums(owned), axis=1, keepdims=True)
    sums = jnp.sum(owned, axis=1, keepdims=True)
    logs_whole = running[:, TOKENS - 1 :]
    stacked = jnp.broadcast_to(
        jnp.concatenate([inside, sums, logs_whole], axis=0), (3 * HEADS, TOKENS)
    )
    decay[...] = transposed(stacked)[0:8]


def reply_forward_kernel(
    decay_log, index, table, keys, queries, steps, upstream, mask_row, logs, starts, pulls, mixed,
    row_sums, column_sums, ended, prompt_decay, queries_out, steps_out, summary,
):
    scale = table[index[0]]
    running = logs[...]
    rate = rates(decay_log)
    reach = transposed(jnp.exp(running) * scale)
    mask = as_columns(mask_row[...].astype(F32)).astype(BF16)
    lanes = iota((TOKENS, TOKENS), 1)
    wide = queries[...].astype(F32)
    total = jnp.zeros((TOKENS, TOKENS), F32)
    reached = jnp.zeros((TOKENS, TOKENS), F32)
    overlaps = []
    for pair in range(PAIRS):
        state = gather(starts, pair)
        shared = state * gather(pulls, pair)
        overlaps.append(jnp.sum(shared[:HEAD_DIM], axis=0, keepdims=True))
        overlaps.append(jnp.sum(shared[HEAD_DIM:], axis=0, keepdims=True))
        high, low = halves(state)
        once = sides(upstream[:, span(pair)] * mask)
        forward = dot(
            jnp.concatenate([once, once], axis=1), jnp.concatenate([high, low], axis=0)
        )
        for side in range(2):
            head = 2 * pair + side
            part = column(reach, head) * forward[side * TOKENS : (side + 1) * TOKENS]
            total = total + part
            reached = jnp.where(
                lanes == head, jnp.sum(part * wide, axis=1, keepdims=True), reached
            )
    high, low = halves((mixed[...] * scale).T)
    total = total + dot(high, keys[...]) + dot(low, keys[...])
    queries_out[...] = total.astype(BF16)
    reached = reached.T[:HEADS]
    later = (iota((TOKENS, TOKENS), 0) >= iota((TOKENS, TOKENS), 1)).astype(F32)
    carried = jnp.sum(jnp.concatenate(overlaps, axis=0), axis=1, keepdims=True)
    carried = carried * jnp.exp(running[:, TOKENS - 1 :])
    closer = column_sums[...] * scale
    log_pull = (
        exact_dot(row_sums[...] * scale - closer + reached, later) + log_sums(ended[...]) + carried
    )
    steps_out[...] = (closer + ended[...]) / steps[...] - rate * log_pull
    local = jnp.sum(-steps[...] * rate * log_pull, axis=1, keepdims=True)
    row = transposed(jnp.broadcast_to(local, (HEADS, TOKENS)))[0:1] + prompt_decay[0:1]
    summary[...] = jnp.broadcast_to(row, (DEVICES, TOKENS))


def moved_lanes(rows, by):
    shift = (iota((TOKENS, TOKENS), 0) == iota((TOKENS, TOKENS), 1) + by).astype(F32)
    return exact_dot(rows, shift)


def finish_kernel(place, decay_log, received, owned, steps, steps_out, decay):
    rows = received[...]
    below = (iota((DEVICES, DEVICES), 0) > iota((DEVICES, DEVICES), 1)).astype(F32)
    before = exact_dot(below, moved_lanes(rows, HEADS))
    decay_rows = rows + before * moved_lanes(rows, 2 * HEADS)
    decay[...] = jnp.broadcast_to(jnp.sum(decay_rows, axis=0, keepdims=True), (8, TOKENS))
    mine = jnp.where(iota((DEVICES, TOKENS), 0) < place[0, 0], rows, 0.0)
    mine = as_columns(jnp.sum(mine, axis=0, keepdims=True))[HEADS : 2 * HEADS]
    steps_out[...] = owned[...] / steps[...] - rates(decay_log) * (log_sums(owned[...]) + mine)


def whole(dims):
    return pl.BlockSpec(dims, lambda step: (0,) * len(dims))


def on_device(kernel, out_shapes, scalars, flops, *operands, vmem=VMEM_BYTES):
    specs = [pl.BlockSpec(memory_space=pltpu.SMEM) for _ in range(scalars)]
    specs += [whole(x.shape) for x in operands[scalars:]]
    return pl.pallas_call(
        kernel,
        grid=(1,),
        out_shape=out_shapes,
        in_specs=specs,
        out_specs=[whole(x.shape) for x in out_shapes],
        compiler_params=pltpu.CompilerParams(vmem_limit_bytes=vmem),
        cost_estimate=pl.CostEstimate(flops=flops, bytes_accessed=1024, transcendentals=0),
    )(*operands)


def shape(*dims, dtype=F32):
    return jax.ShapeDtypeStruct(dims, dtype)


def swap(value, axis):
    return lax.all_to_all(value, axis, 0, 0, tiled=True)


def turn(block):
    pairs = [(a * SLICES + b, b * SLICES + a) for a in range(SLICES) for b in range(SLICES)]
    return lax.ppermute(block, BOTH, pairs)


def traded(value, axis, bit):
    return lax.ppermute(value, axis, [(at, at ^ bit) for at in range(SLICES)])


def doubled(parts, earlier, bits):
    for bit in bits:
        other = traded(parts, "rollout", bit)
        low = earlier[(1, 2, 4, 8).index(bit)] == 1
        first, second = jnp.where(low, parts, other), jnp.where(low, other, parts)
        parts = jnp.stack([first, second], axis=1).reshape((-1,) + parts.shape[1:])
    return parts


def per_device(
    prompt_inputs, prompt_keys, prompt_steps, reply_inputs, reply_keys, reply_queries,
    reply_steps, decay_log, upstream, loss_mask, advantage_index, advantage_table,
):
    reply_inputs, reply_keys, reply_queries = reply_inputs[0], reply_keys[0], reply_queries[0]
    reply_steps, upstream = reply_steps[0], upstream[0]
    scale = (advantage_index, advantage_table)
    row, mine = lax.axis_index("rollout"), lax.axis_index("ctx")
    place = (row * SLICES + mine).astype(jnp.int32).reshape(1, 1)
    owner = mine.astype(jnp.int32).reshape(1, 1)
    slices = shape(SLICES, ROWS, STATE)
    heads = shape(HEADS, TOKENS)
    square = shape(TOKENS, TOKENS)
    wide = shape(TOKENS, CHANNELS, dtype=BF16)
    narrow = shape(TOKENS, STATE, dtype=BF16)

    pack, reply_logs, prompt_logs = on_device(
        first_kernel, [shape(SLICES, GO, STATE), heads, heads], 3, 6 * 10**9,
        decay_log, *scale, prompt_inputs, prompt_keys, prompt_steps, reply_inputs, reply_keys,
        reply_queries, reply_steps, upstream, loss_mask, vmem=VMEM_MOST,
    )
    earlier = [((row & bit) == 0).astype(jnp.int32) for bit in (1, 2, 4, 8)]
    pack, owner, place, earlier = lax.optimization_barrier((pack, owner, place, earlier))
    received = swap(pack, "ctx")
    after, joint, totals = on_device(
        group_kernel, [slices, shape(GO, STATE), shape(2 * SLICES, STATE)], 1, 3 * 10**6,
        owner, received,
    )
    after, joint, reply_logs = lax.optimization_barrier((after, joint, reply_logs))
    after = swap(after, "ctx")
    near, mixed, row_sums, column_sums = on_device(
        within_kernel, [shape(TOKENS, CHANNELS), square, heads, heads], 0, 6 * 10**6,
        reply_inputs, reply_keys, reply_queries, reply_steps, upstream, loss_mask, reply_logs,
    )
    later_groups = jnp.zeros((1, STATE), F32)
    for step, bit in enumerate((1, 2, 4, 8)):
        other = traded(joint, "rollout", bit)
        early = earlier[step] == 1
        logs, other_logs = joint[2 * ROWS : 3 * ROWS], other[2 * ROWS : 3 * ROWS]
        ours, others = joint[:ROWS], other[:ROWS]
        joined = jnp.where(
            early, jnp.exp(other_logs) * ours + others, jnp.exp(logs) * others + ours
        )
        later_groups = later_groups + jnp.where(early, other[3 * ROWS : 3 * ROWS + 1], 0.0)
        joint = jnp.concatenate([joined, joint[ROWS:] + other[ROWS:]], axis=0)
    starts, flag = on_device(
        carry_kernel, [slices, shape(8, STATE)], 1, 3 * 10**6, owner, totals, received, joint
    )
    turned = turn(joint[ROWS : 2 * ROWS])
    turned, flag, after, near = lax.optimization_barrier((turned, flag, after, near))
    starts = swap(starts, "ctx")
    end_pull = doubled(turned[None], earlier, DOUBLING[:2])
    end_pull, after = lax.optimization_barrier((end_pull, after))
    reply_inputs_out, reply_keys_out, ended = on_device(
        reply_backward_kernel, [wide, narrow, heads], 2, 6 * 10**6,
        *scale, reply_inputs, reply_keys, reply_queries, reply_steps, reply_logs, after, near,
        mixed,
    )
    end_pull = doubled(end_pull, earlier, DOUBLING[2:3])
    end_pull, ended = lax.optimization_barrier((end_pull, ended))
    end_pull = doubled(end_pull, earlier, DOUBLING[3:])
    prompt_inputs_out, prompt_keys_out, owned, prompt_decay = on_device(
        prompt_backward_kernel, [wide, narrow, heads, shape(8, TOKENS)], 2, 6 * 10**6,
        owner, decay_log, prompt_inputs, prompt_keys, prompt_steps, prompt_logs, totals,
        later_groups, end_pull, flag,
    )
    reply_queries_out, reply_steps_out, summary = on_device(
        reply_forward_kernel, [narrow, heads, shape(DEVICES, TOKENS)], 3, 6 * 10**6,
        decay_log, *scale, reply_keys, reply_queries, reply_steps, upstream, loss_mask,
        reply_logs, starts, after, mixed, row_sums, column_sums, ended, prompt_decay,
    )
    prompt_steps_out, decay = on_device(
        finish_kernel, [heads, shape(8, TOKENS)], 2, 10**8,
        place, decay_log, swap(summary, BOTH), owned, prompt_steps,
    )
    return (
        prompt_inputs_out, prompt_keys_out, prompt_steps_out, reply_inputs_out[None],
        reply_keys_out[None], reply_queries_out[None], reply_steps_out[None], decay[0, :HEADS],
    )


def solution(mesh):
    in_specs = (
        P(("rollout", "ctx"), None),
        P(("rollout", "ctx"), None),
        P(None, ("rollout", "ctx")),
        P("rollout", "ctx", None),
        P("rollout", "ctx", None),
        P("rollout", "ctx", None),
        P("rollout", None, "ctx"),
        P(),
        P("rollout", "ctx", None),
        P("rollout", "ctx"),
        P("rollout"),
        P(),
    )
    out_specs = (
        P(("rollout", "ctx"), None),
        P(("rollout", "ctx"), None),
        P(None, ("rollout", "ctx")),
        P("rollout", "ctx", None),
        P("rollout", "ctx", None),
        P("rollout", "ctx", None),
        P("rollout", None, "ctx"),
        P(),
    )
    return jax.shard_map(
        per_device, mesh=mesh, in_specs=in_specs, out_specs=out_specs, check_vma=False
    )
```

```python
import jax
import jax.numpy as jnp
from jax import lax
from jax.experimental import pallas as pl
from jax.experimental.pallas import tpu as pltpu
from jax.sharding import PartitionSpec as P

HEADS = 40
HEAD_DIM = 64
STATE = 128
TOKENS = 128
CHANNELS = HEADS * HEAD_DIM
PAIRS = HEADS // 2
SLICES = 16
DEVICES = SLICES * SLICES
ROWS = CHANNELS // SLICES
GO = 2 * ROWS + 8
PIECE = 32
PER_SLICE = ROWS // PIECE
F32 = jnp.float32
BF16 = jnp.bfloat16
HIGHEST = lax.Precision.HIGHEST
VMEM_BYTES = 24 * 1024 * 1024
VMEM_MOST = 56 * 1024 * 1024
DOUBLING = (2, 8, 4, 1)
HALVING = (1, 4, 8, 2)
BOTH = ("rollout", "ctx")


def iota(shape, axis):
    return lax.broadcasted_iota(jnp.int32, shape, axis)


def halves(value):
    high = value.astype(BF16)
    return high, (value - high.astype(F32)).astype(BF16)


def dot(left, right):
    return jnp.dot(left, right, preferred_element_type=F32)


def dot_t(left, right, precision=None):
    return lax.dot_general(
        left, right, (((1,), (1,)), ((), ())), preferred_element_type=F32, precision=precision
    )


def exact_dot(left, right):
    return jnp.dot(left, right, preferred_element_type=F32, precision=HIGHEST)


def running_logs(steps, rate):
    earlier = (iota((TOKENS, TOKENS), 0) <= iota((TOKENS, TOKENS), 1)).astype(F32)
    return exact_dot(-steps * rate, earlier)


def transposed(rows, before=0):
    parts = [rows, jnp.zeros((TOKENS - before - rows.shape[0], TOKENS), F32)]
    if before:
        parts = [jnp.zeros((before, TOKENS), F32)] + parts
    return jnp.concatenate(parts, axis=0).T


def as_columns(row):
    return jnp.broadcast_to(row, (TOKENS, TOKENS)).T


def pair_rows(rows, pair):
    first = jnp.broadcast_to(rows[2 * pair : 2 * pair + 1], (HEAD_DIM, TOKENS))
    second = jnp.broadcast_to(rows[2 * pair + 1 : 2 * pair + 2], (HEAD_DIM, TOKENS))
    return jnp.concatenate([first, second], axis=0)


def column(columns, head):
    return jnp.broadcast_to(columns[:, head : head + 1], (TOKENS, TOKENS))


def pieces(pair):
    for part in range(4):
        place = 4 * pair + part
        yield part * PIECE, place // PER_SLICE, (place % PER_SLICE) * PIECE


def first_lanes():
    return iota((TOKENS, TOKENS), 1) < HEAD_DIM


def sides(block):
    zero = jnp.zeros((), BF16)
    half = first_lanes()
    return jnp.concatenate([jnp.where(half, block, zero), jnp.where(half, zero, block)], axis=0)


def span(pair):
    return slice(pair * TOKENS, (pair + 1) * TOKENS)


def gather(received, pair, order=None):
    places = order or range(SLICES)
    return jnp.concatenate(
        [
            received[places[owner], offset : offset + PIECE, :]
            for at, owner, offset in pieces(pair)
        ],
        axis=0,
    )


def doubled_order():
    places = []
    for owner in range(SLICES):
        place = 0
        for bit in DOUBLING:
            place = 2 * place + (1 if owner & bit else 0)
        places.append(place)
    return places


def pack_states(pack, base, tokens, rows, keys):
    twice = jnp.concatenate([keys, keys], axis=0)
    for pair in range(PAIRS):
        block = tokens[:, span(pair)].astype(F32).T
        high, low = halves(block * pair_rows(rows, pair))
        states = dot(jnp.concatenate([high, low], axis=1), twice)
        for at, owner, offset in pieces(pair):
            pack[owner, base + offset : base + offset + PIECE, :] = states[at : at + PIECE]


def rates(decay_log):
    heads = iota((HEADS, TOKENS), 0)
    logs = jnp.zeros((HEADS, TOKENS), F32)
    for head in range(HEADS):
        logs = jnp.where(heads == head, decay_log[head], logs)
    return jnp.exp(logs)


def prompt_logs_kernel(decay_log, steps, logs, total):
    running = running_logs(steps[...], rates(decay_log))
    logs[...] = running
    last = jnp.broadcast_to(running[:, TOKENS - 1 :], (HEADS, TOKENS))
    total[...] = transposed(last)[0:SLICES]


def first_kernel(
    decay_log, index, table, inputs, keys, queries, steps, upstream, mask, pack, reply_logs
):
    running = running_logs(steps[...], rates(decay_log))
    reply_logs[...] = running
    last = jnp.broadcast_to(running[:, TOKENS - 1 :], (HEADS, TOKENS))
    total = transposed(last)[0:8]
    for owner in range(SLICES):
        pack[owner, 2 * ROWS :, :] = total
    rows = jnp.exp(running) * (mask[...].astype(F32) * table[index[0]])
    pack_states(pack, 0, upstream, rows, queries[...])
    rows = jnp.exp(last - running) * steps[...]
    pack_states(pack, ROWS, inputs, rows, keys[...])


def prompt_states_kernel(inputs, keys, steps, logs, later, pack, ends):
    running = logs[...]
    after = as_columns(later[0:1, :])[:HEADS]
    rows = jnp.exp(running[:, TOKENS - 1 :] - running + after) * steps[...]
    ends[...] = rows
    pack_states(pack, 0, inputs, rows, keys[...])


def within_kernel(
    inputs, keys, queries, steps, upstream, mask_row, logs, near, mixed, row_sums, column_sums
):
    running = logs[...]
    columns = transposed(jnp.log(steps[...]) - running)
    causal = iota((TOKENS, TOKENS), 1) >= iota((TOKENS, TOKENS), 0)
    lanes = iota((TOKENS, TOKENS), 1)
    scores = dot_t(keys[...], queries[...])
    mask = as_columns(mask_row[...].astype(F32)).astype(BF16)
    total = jnp.zeros((TOKENS, TOKENS), F32)
    gathered = jnp.zeros((TOKENS, TOKENS), F32)
    for pair in range(PAIRS):
        pulled = upstream[:, span(pair)] * mask
        products = dot_t(sides(inputs[:, span(pair)]), pulled)
        highs, lows = [], []
        for side in range(2):
            head = 2 * pair + side
            gaps = running[head : head + 1] + column(columns, head)
            mixing = jnp.where(causal, jnp.exp(gaps), 0.0)
            weighted = mixing * products[side * TOKENS : (side + 1) * TOKENS]
            total = total + weighted
            terms = weighted * scores
            row_sums[head : head + 1, :] = jnp.sum(terms, axis=0, keepdims=True)
            gathered = jnp.where(lanes == head, jnp.sum(terms, axis=1, keepdims=True), gathered)
            high, low = halves(mixing * scores)
            highs.append(high)
            lows.append(low)
        both = sides(pulled)
        near[:, span(pair)] = dot(jnp.concatenate(highs, axis=1), both) + dot(
            jnp.concatenate(lows, axis=1), both
        )
    mixed[...] = total
    column_sums[...] = gathered.T[:HEADS]


def spread(columns, at):
    return jnp.broadcast_to(columns[:, at : at + 1], (ROWS, TOKENS))


def owner_columns(owner, rows):
    place = owner * ROWS + iota((ROWS, TOKENS), 0)
    chosen = (lax.shift_right_logical(place, 6) == iota((ROWS, TOKENS), 1)).astype(F32)
    pad = jnp.zeros((TOKENS - rows.shape[0], TOKENS), F32)
    return dot_t(chosen, jnp.concatenate([rows, pad], axis=0), HIGHEST)


def group_kernel(owner, received, after, start, totals):
    reply = jnp.concatenate(
        [received[c, 2 * ROWS : 2 * ROWS + 1, :] for c in range(SLICES)], axis=0
    )
    totals[...] = reply
    factors = jnp.exp(owner_columns(owner[0, 0], reply))
    pulled = jnp.zeros((ROWS, TOKENS), F32)
    for c in range(SLICES - 1, -1, -1):
        after[c] = pulled
        pulled = spread(factors, c) * pulled + received[c, 0:ROWS, :]
    start[...] = pulled


def carry_kernel(owner, totals, received, end_state, starts, flag):
    flag[...] = end_state[0:8, :]
    factors = jnp.exp(owner_columns(owner[0, 0], totals[...]))
    state = end_state[...]
    for c in range(SLICES):
        starts[c] = state
        if c < SLICES - 1:
            state = spread(factors, c) * state + received[c, ROWS : 2 * ROWS, :]


def backward_parts(inputs, pulls, ends, keys, near, scale, inputs_out, order=None):
    twice = jnp.concatenate([keys, keys], axis=1)
    wide = keys.astype(F32)
    lanes = iota((TOKENS, TOKENS), 1)
    half = first_lanes()
    total = jnp.zeros((TOKENS, TOKENS), F32)
    gathered = jnp.zeros((TOKENS, TOKENS), F32)
    columns = transposed(ends)
    for pair in range(PAIRS):
        high, low = halves(gather(pulls, pair, order))
        once = sides(inputs[:, span(pair)])
        backward = dot(
            jnp.concatenate([once, once], axis=1), jnp.concatenate([high, low], axis=0)
        )
        keyed = dot_t(twice, jnp.concatenate([high, low], axis=1))
        factors = []
        for side in range(2):
            head = 2 * pair + side
            factors.append(column(columns, head))
            part = factors[side] * backward[side * TOKENS : (side + 1) * TOKENS]
            total = total + part
            gathered = jnp.where(
                lanes == head, jnp.sum(part * wide, axis=1, keepdims=True), gathered
            )
        own = jnp.where(half, factors[0], factors[1]) * keyed
        if near is not None:
            own = near[:, span(pair)] * scale + own
        inputs_out[:, span(pair)] = own.astype(BF16)
    return total, gathered.T[:HEADS]


def reply_backward_kernel(
    index, table, inputs, keys, queries, steps, logs, pulls, near, mixed, inputs_out, keys_out, ended_out
):
    scale = table[index[0]]
    running = logs[...]
    ends = jnp.exp(running[:, TOKENS - 1 :] - running) * steps[...]
    total, ended = backward_parts(inputs, pulls, ends, keys[...], near, scale, inputs_out)
    high, low = halves(mixed[...] * scale)
    total = total + dot(high, queries[...]) + dot(low, queries[...])
    keys_out[...] = total.astype(BF16)
    ended_out[...] = ended


def log_sums(rows):
    lower = (iota((TOKENS, TOKENS), 0) < iota((TOKENS, TOKENS), 1)).astype(F32)
    return exact_dot(rows, lower)


def prompt_backward_kernel(
    decay_log, inputs, keys, steps, logs, ends, pulls, _,
    inputs_out, keys_out, owned_out, decay,
):
    rate = rates(decay_log)
    total, owned = backward_parts(
        inputs, pulls, ends[...], keys[...], None, None, inputs_out, doubled_order()
    )
    keys_out[...] = total.astype(BF16)
    owned_out[...] = owned
    inside = jnp.sum(-steps[...] * rate * log_sums(owned), axis=1, keepdims=True)
    sums = jnp.sum(owned, axis=1, keepdims=True)
    stacked = jnp.broadcast_to(
        jnp.concatenate([inside, sums, logs[:, TOKENS - 1 :]], axis=0), (3 * HEADS, TOKENS)
    )
    decay[...] = transposed(stacked)[0:8]


def reply_forward_kernel(
    decay_log, index, table, keys, queries, steps, upstream, mask_row, logs, starts, pulls, mixed,
    row_sums, column_sums, ended, prompt_decay, queries_out, steps_out, summary,
):
    scale = table[index[0]]
    running = logs[...]
    rate = rates(decay_log)
    reach = transposed(jnp.exp(running) * scale)
    mask = as_columns(mask_row[...].astype(F32)).astype(BF16)
    lanes = iota((TOKENS, TOKENS), 1)
    wide = queries[...].astype(F32)
    total = jnp.zeros((TOKENS, TOKENS), F32)
    reached = jnp.zeros((TOKENS, TOKENS), F32)
    overlaps = []
    for pair in range(PAIRS):
        state = gather(starts, pair)
        shared = state * gather(pulls, pair)
        overlaps.append(jnp.sum(shared[:HEAD_DIM], axis=0, keepdims=True))
        overlaps.append(jnp.sum(shared[HEAD_DIM:], axis=0, keepdims=True))
        high, low = halves(state)
        once = sides(upstream[:, span(pair)] * mask)
        forward = dot(
            jnp.concatenate([once, once], axis=1), jnp.concatenate([high, low], axis=0)
        )
        for side in range(2):
            head = 2 * pair + side
            part = column(reach, head) * forward[side * TOKENS : (side + 1) * TOKENS]
            total = total + part
            reached = jnp.where(
                lanes == head, jnp.sum(part * wide, axis=1, keepdims=True), reached
            )
    high, low = halves((mixed[...] * scale).T)
    total = total + dot(high, keys[...]) + dot(low, keys[...])
    queries_out[...] = total.astype(BF16)
    reached = reached.T[:HEADS]
    later = (iota((TOKENS, TOKENS), 0) >= iota((TOKENS, TOKENS), 1)).astype(F32)
    carried = jnp.sum(jnp.concatenate(overlaps, axis=0), axis=1, keepdims=True)
    carried = carried * jnp.exp(running[:, TOKENS - 1 :])
    closer = column_sums[...] * scale
    log_pull = (
        exact_dot(row_sums[...] * scale - closer + reached, later) + log_sums(ended[...]) + carried
    )
    steps_out[...] = (closer + ended[...]) / steps[...] - rate * log_pull
    local = jnp.sum(-steps[...] * rate * log_pull, axis=1, keepdims=True)
    row = transposed(jnp.broadcast_to(local, (HEADS, TOKENS)))[0:1] + prompt_decay[0:1]
    summary[...] = jnp.broadcast_to(row, (DEVICES, TOKENS))


def moved_lanes(rows, by):
    shift = (iota((TOKENS, TOKENS), 0) == iota((TOKENS, TOKENS), 1) + by).astype(F32)
    return exact_dot(rows, shift)


def finish_kernel(place, decay_log, received, owned, steps, steps_out, decay):
    rows = received[...]
    below = (iota((DEVICES, DEVICES), 0) > iota((DEVICES, DEVICES), 1)).astype(F32)
    before = exact_dot(below, moved_lanes(rows, HEADS))
    decay_rows = rows + before * moved_lanes(rows, 2 * HEADS)
    decay[...] = jnp.broadcast_to(jnp.sum(decay_rows, axis=0, keepdims=True), (8, TOKENS))
    mine = jnp.where(iota((DEVICES, TOKENS), 0) < place[0, 0], rows, 0.0)
    mine = as_columns(jnp.sum(mine, axis=0, keepdims=True))[HEADS : 2 * HEADS]
    steps_out[...] = owned[...] / steps[...] - rates(decay_log) * (log_sums(owned[...]) + mine)


def whole(dims):
    return pl.BlockSpec(dims, lambda step: (0,) * len(dims))


def on_device(kernel, out_shapes, scalars, flops, *operands, vmem=VMEM_BYTES):
    specs = [pl.BlockSpec(memory_space=pltpu.SMEM) for _ in range(scalars)]
    specs += [whole(x.shape) for x in operands[scalars:]]
    return pl.pallas_call(
        kernel,
        grid=(1,),
        out_shape=out_shapes,
        in_specs=specs,
        out_specs=[whole(x.shape) for x in out_shapes],
        compiler_params=pltpu.CompilerParams(vmem_limit_bytes=vmem),
        cost_estimate=pl.CostEstimate(flops=flops, bytes_accessed=1024, transcendentals=0),
    )(*operands)


def shape(*dims, dtype=F32):
    return jax.ShapeDtypeStruct(dims, dtype)


def swap(value, axis):
    return lax.all_to_all(value, axis, 0, 0, tiled=True)


def turn(block):
    pairs = [(a * SLICES + b, b * SLICES + a) for a in range(SLICES) for b in range(SLICES)]
    return lax.ppermute(block, BOTH, pairs)


def traded(value, axis, bit):
    return lax.ppermute(value, axis, [(at, at ^ bit) for at in range(SLICES)])


def later_sums(later, total, earlier):
    for step, bit in enumerate((1, 2, 4, 8)):
        other = traded(total, "rollout", bit)
        later = later + jnp.where(earlier[step] == 1, other, 0.0)
        total = total + other
    return later


def reduced_over_rows(states, earlier):
    block = states.shape[1:]
    left = [8, 4, 2, 1]
    for bit in HALVING:
        side = 1 - earlier[(1, 2, 4, 8).index(bit)]
        axis = left.index(bit)
        split = states.reshape((2,) * len(left) + block)
        given = lax.dynamic_index_in_dim(split, 1 - side, axis, keepdims=False)
        kept = lax.dynamic_index_in_dim(split, side, axis, keepdims=False)
        left.remove(bit)
        flat = (2 ** len(left),) + block
        states = kept.reshape(flat) + traded(given.reshape(flat), "rollout", bit)
    return states[0]


def doubled(parts, earlier, bits):
    for bit in bits:
        other = traded(parts, "rollout", bit)
        low = earlier[(1, 2, 4, 8).index(bit)] == 1
        first, second = jnp.where(low, parts, other), jnp.where(low, other, parts)
        parts = jnp.stack([first, second], axis=1).reshape((-1,) + parts.shape[1:])
    return parts


def per_device(
    prompt_inputs, prompt_keys, prompt_steps, reply_inputs, reply_keys, reply_queries,
    reply_steps, decay_log, upstream, loss_mask, advantage_index, advantage_table,
):
    reply_inputs, reply_keys, reply_queries = reply_inputs[0], reply_keys[0], reply_queries[0]
    reply_steps, upstream = reply_steps[0], upstream[0]
    scale = (advantage_index, advantage_table)
    row, mine = lax.axis_index("rollout"), lax.axis_index("ctx")
    place = (row * SLICES + mine).astype(jnp.int32).reshape(1, 1)
    owner = mine.astype(jnp.int32).reshape(1, 1)
    slices = shape(SLICES, ROWS, STATE)
    heads = shape(HEADS, TOKENS)
    square = shape(TOKENS, TOKENS)
    wide = shape(TOKENS, CHANNELS, dtype=BF16)
    narrow = shape(TOKENS, STATE, dtype=BF16)

    prompt_logs, prompt_total = on_device(
        prompt_logs_kernel, [heads, shape(SLICES, TOKENS)], 1, 10**6, decay_log, prompt_steps
    )
    earlier = [((row & bit) == 0).astype(jnp.int32) for bit in (1, 2, 4, 8)]
    group_totals = swap(prompt_total, "ctx")
    pack, reply_logs = on_device(
        first_kernel, [shape(SLICES, GO, STATE), heads], 3, 5 * 10**9,
        decay_log, *scale, reply_inputs, reply_keys, reply_queries, reply_steps, upstream,
        loss_mask, vmem=VMEM_MOST,
    )
    later = jnp.sum(
        jnp.where(jnp.arange(SLICES)[:, None] > mine, group_totals, 0.0), axis=0, keepdims=True
    )
    total = jnp.sum(group_totals, axis=0, keepdims=True)
    later, total = (jnp.broadcast_to(x, (8, TOKENS)) for x in (later, total))
    pack, later, total, owner, place, earlier = lax.optimization_barrier(
        (pack, later, total, owner, place, earlier)
    )
    received = swap(pack, "ctx")
    later = later_sums(later, total, earlier)
    prompt_states, prompt_ends = on_device(
        prompt_states_kernel, [slices, heads], 0, 3 * 10**6,
        prompt_inputs, prompt_keys, prompt_steps, prompt_logs, later,
    )
    received, prompt_states = lax.optimization_barrier(
        (received, reduced_over_rows(prompt_states, earlier))
    )
    after, row_pulls, totals = on_device(
        group_kernel, [slices, shape(ROWS, STATE), shape(SLICES, STATE)], 1, 3 * 10**6,
        owner, received,
    )
    after, prompt_states, row_pulls, reply_logs = lax.optimization_barrier(
        (after, turn(prompt_states), row_pulls, reply_logs)
    )
    after = swap(after, "ctx")
    near, mixed, row_sums, column_sums = on_device(
        within_kernel, [shape(TOKENS, CHANNELS), square, heads, heads], 0, 6 * 10**6,
        reply_inputs, reply_keys, reply_queries, reply_steps, upstream, loss_mask, reply_logs,
    )
    joint = jnp.concatenate([prompt_states, row_pulls], axis=0)
    for bit in (1, 2, 4, 8):
        joint = joint + traded(joint, "rollout", bit)
    starts, flag = on_device(
        carry_kernel, [slices, shape(8, STATE)], 1, 3 * 10**6,
        owner, totals, received, joint[:ROWS],
    )
    turned = turn(joint[ROWS:])
    turned, flag, after, near = lax.optimization_barrier((turned, flag, after, near))
    starts = swap(starts, "ctx")
    end_pull = doubled(turned[None], earlier, DOUBLING[:2])
    end_pull, after = lax.optimization_barrier((end_pull, after))
    reply_inputs_out, reply_keys_out, ended = on_device(
        reply_backward_kernel, [wide, narrow, heads], 2, 6 * 10**6,
        *scale, reply_inputs, reply_keys, reply_queries, reply_steps, reply_logs, after, near,
        mixed,
    )
    end_pull = doubled(end_pull, earlier, DOUBLING[2:3])
    end_pull, ended = lax.optimization_barrier((end_pull, ended))
    end_pull = doubled(end_pull, earlier, DOUBLING[3:])
    prompt_inputs_out, prompt_keys_out, owned, prompt_decay = on_device(
        prompt_backward_kernel, [wide, narrow, heads, shape(8, TOKENS)], 1, 6 * 10**6,
        decay_log, prompt_inputs, prompt_keys, prompt_steps, prompt_logs, prompt_ends, end_pull,
        flag,
    )
    reply_queries_out, reply_steps_out, summary = on_device(
        reply_forward_kernel, [narrow, heads, shape(DEVICES, TOKENS)], 3, 6 * 10**6,
        decay_log, *scale, reply_keys, reply_queries, reply_steps, upstream, loss_mask,
        reply_logs, starts, after, mixed, row_sums, column_sums, ended, prompt_decay,
    )
    prompt_steps_out, decay = on_device(
        finish_kernel, [heads, shape(8, TOKENS)], 2, 10**8,
        place, decay_log, swap(summary, BOTH), owned, prompt_steps,
    )
    return (
        prompt_inputs_out, prompt_keys_out, prompt_steps_out, reply_inputs_out[None],
        reply_keys_out[None], reply_queries_out[None], reply_steps_out[None], decay[0, :HEADS],
    )


def solution(mesh):
    in_specs = (
        P(("rollout", "ctx"), None),
        P(("rollout", "ctx"), None),
        P(None, ("rollout", "ctx")),
        P("rollout", "ctx", None),
        P("rollout", "ctx", None),
        P("rollout", "ctx", None),
        P("rollout", None, "ctx"),
        P(),
        P("rollout", "ctx", None),
        P("rollout", "ctx"),
        P("rollout"),
        P(),
    )
    out_specs = (
        P(("rollout", "ctx"), None),
        P(("rollout", "ctx"), None),
        P(None, ("rollout", "ctx")),
        P("rollout", "ctx", None),
        P("rollout", "ctx", None),
        P("rollout", "ctx", None),
        P("rollout", None, "ctx"),
        P(),
    )
    return jax.shard_map(
        per_device, mesh=mesh, in_specs=in_specs, out_specs=out_specs, check_vma=False
    )
```

```python
import jax
import jax.numpy as jnp
from jax import lax
from jax.experimental import pallas as pl
from jax.experimental.pallas import tpu as pltpu
from jax.sharding import PartitionSpec as P

HEADS = 40
HEAD_DIM = 64
STATE = 128
TOKENS = 128
CHANNELS = HEADS * HEAD_DIM
PAIRS = HEADS // 2
SLICES = 16
DEVICES = SLICES * SLICES
ROWS = CHANNELS // SLICES
GO = 2 * ROWS + 8
PIECE = 32
PER_SLICE = ROWS // PIECE
F32 = jnp.float32
BF16 = jnp.bfloat16
HIGHEST = lax.Precision.HIGHEST
VMEM_BYTES = 24 * 1024 * 1024
VMEM_MOST = 56 * 1024 * 1024
DOUBLING = (2, 8, 4, 1)
HALVING = (1, 4, 8, 2)
BOTH = ("rollout", "ctx")


def iota(shape, axis):
    return lax.broadcasted_iota(jnp.int32, shape, axis)


def halves(value):
    high = value.astype(BF16)
    return high, (value - high.astype(F32)).astype(BF16)


def dot(left, right):
    return jnp.dot(left, right, preferred_element_type=F32)


def dot_t(left, right, precision=None):
    return lax.dot_general(
        left, right, (((1,), (1,)), ((), ())), preferred_element_type=F32, precision=precision
    )


def exact_dot(left, right):
    return jnp.dot(left, right, preferred_element_type=F32, precision=HIGHEST)


def running_logs(steps, rate):
    earlier = (iota((TOKENS, TOKENS), 0) <= iota((TOKENS, TOKENS), 1)).astype(F32)
    return exact_dot(-steps * rate, earlier)


def transposed(rows, before=0):
    parts = [rows, jnp.zeros((TOKENS - before - rows.shape[0], TOKENS), F32)]
    if before:
        parts = [jnp.zeros((before, TOKENS), F32)] + parts
    return jnp.concatenate(parts, axis=0).T


def as_columns(row):
    return jnp.broadcast_to(row, (TOKENS, TOKENS)).T


def pair_rows(rows, pair):
    first = jnp.broadcast_to(rows[2 * pair : 2 * pair + 1], (HEAD_DIM, TOKENS))
    second = jnp.broadcast_to(rows[2 * pair + 1 : 2 * pair + 2], (HEAD_DIM, TOKENS))
    return jnp.concatenate([first, second], axis=0)


def column(columns, head):
    return jnp.broadcast_to(columns[:, head : head + 1], (TOKENS, TOKENS))


def pieces(pair):
    for part in range(4):
        place = 4 * pair + part
        yield part * PIECE, place // PER_SLICE, (place % PER_SLICE) * PIECE


def first_lanes():
    return iota((TOKENS, TOKENS), 1) < HEAD_DIM


def sides(block):
    zero = jnp.zeros((), BF16)
    half = first_lanes()
    return jnp.concatenate([jnp.where(half, block, zero), jnp.where(half, zero, block)], axis=0)


def span(pair):
    return slice(pair * TOKENS, (pair + 1) * TOKENS)


def gather(received, pair, order=None):
    places = order or range(SLICES)
    return jnp.concatenate(
        [
            received[places[owner], offset : offset + PIECE, :]
            for at, owner, offset in pieces(pair)
        ],
        axis=0,
    )


def doubled_order():
    places = []
    for owner in range(SLICES):
        place = 0
        for bit in DOUBLING:
            place = 2 * place + (1 if owner & bit else 0)
        places.append(place)
    return places


def pack_states(pack, base, tokens, rows, keys):
    twice = jnp.concatenate([keys, keys], axis=0)
    for pair in range(PAIRS):
        block = tokens[:, span(pair)].astype(F32).T
        high, low = halves(block * pair_rows(rows, pair))
        states = dot(jnp.concatenate([high, low], axis=1), twice)
        for at, owner, offset in pieces(pair):
            pack[owner, base + offset : base + offset + PIECE, :] = states[at : at + PIECE]


def rates(decay_log):
    heads = iota((HEADS, TOKENS), 0)
    logs = jnp.zeros((HEADS, TOKENS), F32)
    for head in range(HEADS):
        logs = jnp.where(heads == head, decay_log[head], logs)
    return jnp.exp(logs)


def prompt_logs_kernel(decay_log, steps, logs, total):
    running = running_logs(steps[...], rates(decay_log))
    logs[...] = running
    last = jnp.broadcast_to(running[:, TOKENS - 1 :], (HEADS, TOKENS))
    total[...] = transposed(last)[0:SLICES]


def first_kernel(
    decay_log, index, table, inputs, keys, queries, steps, upstream, mask, pack, reply_logs
):
    running = running_logs(steps[...], rates(decay_log))
    reply_logs[...] = running
    last = jnp.broadcast_to(running[:, TOKENS - 1 :], (HEADS, TOKENS))
    total = transposed(last)[0:8]
    for owner in range(SLICES):
        pack[owner, 2 * ROWS :, :] = total
    rows = jnp.exp(running) * (mask[...].astype(F32) * table[index[0]])
    pack_states(pack, 0, upstream, rows, queries[...])
    rows = jnp.exp(last - running) * steps[...]
    pack_states(pack, ROWS, inputs, rows, keys[...])


def prompt_states_kernel(inputs, keys, steps, logs, later, pack, ends):
    running = logs[...]
    after = as_columns(later[0:1, :])[:HEADS]
    rows = jnp.exp(running[:, TOKENS - 1 :] - running + after) * steps[...]
    ends[...] = rows
    pack_states(pack, 0, inputs, rows, keys[...])


def within_kernel(
    inputs, keys, queries, steps, upstream, mask_row, logs, near, mixed, row_sums, column_sums
):
    running = logs[...]
    columns = transposed(jnp.log(steps[...]) - running)
    causal = iota((TOKENS, TOKENS), 1) >= iota((TOKENS, TOKENS), 0)
    lanes = iota((TOKENS, TOKENS), 1)
    scores = dot_t(keys[...], queries[...])
    mask = as_columns(mask_row[...].astype(F32)).astype(BF16)
    total = jnp.zeros((TOKENS, TOKENS), F32)
    gathered = jnp.zeros((TOKENS, TOKENS), F32)
    for pair in range(PAIRS):
        pulled = upstream[:, span(pair)] * mask
        products = dot_t(sides(inputs[:, span(pair)]), pulled)
        highs, lows = [], []
        for side in range(2):
            head = 2 * pair + side
            gaps = running[head : head + 1] + column(columns, head)
            mixing = jnp.where(causal, jnp.exp(gaps), 0.0)
            weighted = mixing * products[side * TOKENS : (side + 1) * TOKENS]
            total = total + weighted
            terms = weighted * scores
            row_sums[head : head + 1, :] = jnp.sum(terms, axis=0, keepdims=True)
            gathered = jnp.where(lanes == head, jnp.sum(terms, axis=1, keepdims=True), gathered)
            high, low = halves(mixing * scores)
            highs.append(high)
            lows.append(low)
        both = sides(pulled)
        near[:, span(pair)] = dot(jnp.concatenate(highs, axis=1), both) + dot(
            jnp.concatenate(lows, axis=1), both
        )
    mixed[...] = total
    column_sums[...] = gathered.T[:HEADS]


def spread(columns, at):
    return jnp.broadcast_to(columns[:, at : at + 1], (ROWS, TOKENS))


def owner_columns(owner, rows):
    place = owner * ROWS + iota((ROWS, TOKENS), 0)
    chosen = (lax.shift_right_logical(place, 6) == iota((ROWS, TOKENS), 1)).astype(F32)
    pad = jnp.zeros((TOKENS - rows.shape[0], TOKENS), F32)
    return dot_t(chosen, jnp.concatenate([rows, pad], axis=0), HIGHEST)


def group_kernel(owner, received, after, start, totals):
    reply = jnp.concatenate(
        [received[c, 2 * ROWS : 2 * ROWS + 1, :] for c in range(SLICES)], axis=0
    )
    totals[...] = reply
    factors = jnp.exp(owner_columns(owner[0, 0], reply))
    pulled = jnp.zeros((ROWS, TOKENS), F32)
    for c in range(SLICES - 1, -1, -1):
        after[c] = pulled
        pulled = spread(factors, c) * pulled + received[c, 0:ROWS, :]
    start[...] = pulled


def carry_kernel(owner, totals, received, end_state, starts, flag):
    flag[...] = end_state[0:8, :]
    factors = jnp.exp(owner_columns(owner[0, 0], totals[...]))
    state = end_state[...]
    for c in range(SLICES):
        starts[c] = state
        if c < SLICES - 1:
            state = spread(factors, c) * state + received[c, ROWS : 2 * ROWS, :]


def backward_parts(inputs, pulls, ends, keys, near, scale, inputs_out, order=None):
    twice = jnp.concatenate([keys, keys], axis=1)
    wide = keys.astype(F32)
    lanes = iota((TOKENS, TOKENS), 1)
    half = first_lanes()
    total = jnp.zeros((TOKENS, TOKENS), F32)
    gathered = jnp.zeros((TOKENS, TOKENS), F32)
    columns = transposed(ends)
    for pair in range(PAIRS):
        high, low = halves(gather(pulls, pair, order))
        once = sides(inputs[:, span(pair)])
        backward = dot(
            jnp.concatenate([once, once], axis=1), jnp.concatenate([high, low], axis=0)
        )
        keyed = dot_t(twice, jnp.concatenate([high, low], axis=1))
        factors = []
        for side in range(2):
            head = 2 * pair + side
            factors.append(column(columns, head))
            part = factors[side] * backward[side * TOKENS : (side + 1) * TOKENS]
            total = total + part
            gathered = jnp.where(
                lanes == head, jnp.sum(part * wide, axis=1, keepdims=True), gathered
            )
        own = jnp.where(half, factors[0], factors[1]) * keyed
        if near is not None:
            own = near[:, span(pair)] * scale + own
        inputs_out[:, span(pair)] = own.astype(BF16)
    return total, gathered.T[:HEADS]


def reply_backward_kernel(
    index, table, inputs, keys, queries, steps, logs, pulls, near, mixed, inputs_out, keys_out, ended_out
):
    scale = table[index[0]]
    running = logs[...]
    ends = jnp.exp(running[:, TOKENS - 1 :] - running) * steps[...]
    total, ended = backward_parts(inputs, pulls, ends, keys[...], near, scale, inputs_out)
    high, low = halves(mixed[...] * scale)
    total = total + dot(high, queries[...]) + dot(low, queries[...])
    keys_out[...] = total.astype(BF16)
    ended_out[...] = ended


def log_sums(rows):
    lower = (iota((TOKENS, TOKENS), 0) < iota((TOKENS, TOKENS), 1)).astype(F32)
    return exact_dot(rows, lower)


def prompt_backward_kernel(
    decay_log, inputs, keys, steps, logs, ends, pulls, _,
    inputs_out, keys_out, owned_out, decay,
):
    rate = rates(decay_log)
    total, owned = backward_parts(
        inputs, pulls, ends[...], keys[...], None, None, inputs_out, doubled_order()
    )
    keys_out[...] = total.astype(BF16)
    owned_out[...] = owned
    inside = jnp.sum(-steps[...] * rate * log_sums(owned), axis=1, keepdims=True)
    sums = jnp.sum(owned, axis=1, keepdims=True)
    stacked = jnp.broadcast_to(
        jnp.concatenate([inside, sums, logs[:, TOKENS - 1 :]], axis=0), (3 * HEADS, TOKENS)
    )
    decay[...] = transposed(stacked)[0:8]


def reply_forward_kernel(
    decay_log, index, table, keys, queries, steps, upstream, mask_row, logs, starts, pulls, mixed,
    row_sums, column_sums, ended, prompt_decay, queries_out, steps_out, summary,
):
    scale = table[index[0]]
    running = logs[...]
    rate = rates(decay_log)
    reach = transposed(jnp.exp(running) * scale)
    mask = as_columns(mask_row[...].astype(F32)).astype(BF16)
    lanes = iota((TOKENS, TOKENS), 1)
    wide = queries[...].astype(F32)
    total = jnp.zeros((TOKENS, TOKENS), F32)
    reached = jnp.zeros((TOKENS, TOKENS), F32)
    overlaps = []
    for pair in range(PAIRS):
        state = gather(starts, pair)
        shared = state * gather(pulls, pair)
        overlaps.append(jnp.sum(shared[:HEAD_DIM], axis=0, keepdims=True))
        overlaps.append(jnp.sum(shared[HEAD_DIM:], axis=0, keepdims=True))
        high, low = halves(state)
        once = sides(upstream[:, span(pair)] * mask)
        forward = dot(
            jnp.concatenate([once, once], axis=1), jnp.concatenate([high, low], axis=0)
        )
        for side in range(2):
            head = 2 * pair + side
            part = column(reach, head) * forward[side * TOKENS : (side + 1) * TOKENS]
            total = total + part
            reached = jnp.where(
                lanes == head, jnp.sum(part * wide, axis=1, keepdims=True), reached
            )
    high, low = halves((mixed[...] * scale).T)
    total = total + dot(high, keys[...]) + dot(low, keys[...])
    queries_out[...] = total.astype(BF16)
    reached = reached.T[:HEADS]
    later = (iota((TOKENS, TOKENS), 0) >= iota((TOKENS, TOKENS), 1)).astype(F32)
    carried = jnp.sum(jnp.concatenate(overlaps, axis=0), axis=1, keepdims=True)
    carried = carried * jnp.exp(running[:, TOKENS - 1 :])
    closer = column_sums[...] * scale
    log_pull = (
        exact_dot(row_sums[...] * scale - closer + reached, later) + log_sums(ended[...]) + carried
    )
    steps_out[...] = (closer + ended[...]) / steps[...] - rate * log_pull
    local = jnp.sum(-steps[...] * rate * log_pull, axis=1, keepdims=True)
    row = transposed(jnp.broadcast_to(local, (HEADS, TOKENS)))[0:1] + prompt_decay[0:1]
    summary[...] = jnp.broadcast_to(row, (DEVICES, TOKENS))


def moved_lanes(rows, by):
    shift = (iota((TOKENS, TOKENS), 0) == iota((TOKENS, TOKENS), 1) + by).astype(F32)
    return exact_dot(rows, shift)


def finish_kernel(place, decay_log, received, owned, steps, steps_out, decay):
    rows = received[...]
    below = (iota((DEVICES, DEVICES), 0) > iota((DEVICES, DEVICES), 1)).astype(F32)
    before = exact_dot(below, moved_lanes(rows, HEADS))
    decay_rows = rows + before * moved_lanes(rows, 2 * HEADS)
    decay[...] = jnp.broadcast_to(jnp.sum(decay_rows, axis=0, keepdims=True), (8, TOKENS))
    mine = jnp.where(iota((DEVICES, TOKENS), 0) < place[0, 0], rows, 0.0)
    mine = as_columns(jnp.sum(mine, axis=0, keepdims=True))[HEADS : 2 * HEADS]
    steps_out[...] = owned[...] / steps[...] - rates(decay_log) * (log_sums(owned[...]) + mine)


def whole(dims):
    return pl.BlockSpec(dims, lambda step: (0,) * len(dims))


def on_device(kernel, out_shapes, scalars, flops, *operands, vmem=VMEM_BYTES):
    specs = [pl.BlockSpec(memory_space=pltpu.SMEM) for _ in range(scalars)]
    specs += [whole(x.shape) for x in operands[scalars:]]
    return pl.pallas_call(
        kernel,
        grid=(1,),
        out_shape=out_shapes,
        in_specs=specs,
        out_specs=[whole(x.shape) for x in out_shapes],
        compiler_params=pltpu.CompilerParams(vmem_limit_bytes=vmem),
        cost_estimate=pl.CostEstimate(flops=flops, bytes_accessed=1024, transcendentals=0),
    )(*operands)


def shape(*dims, dtype=F32):
    return jax.ShapeDtypeStruct(dims, dtype)


def swap(value, axis):
    return lax.all_to_all(value, axis, 0, 0, tiled=True)


def turn(block):
    pairs = [(a * SLICES + b, b * SLICES + a) for a in range(SLICES) for b in range(SLICES)]
    return lax.ppermute(block, BOTH, pairs)


def traded(value, axis, bit):
    return lax.ppermute(value, axis, [(at, at ^ bit) for at in range(SLICES)])


def later_sums(later, total, earlier):
    for step, bit in enumerate((1, 2, 4, 8)):
        other = traded(total, "rollout", bit)
        later = later + jnp.where(earlier[step] == 1, other, 0.0)
        total = total + other
    return later


def reduced_over_rows(states, earlier):
    block = states.shape[1:]
    left = [8, 4, 2, 1]
    for bit in HALVING:
        side = 1 - earlier[(1, 2, 4, 8).index(bit)]
        axis = left.index(bit)
        split = states.reshape((2,) * len(left) + block)
        given = lax.dynamic_index_in_dim(split, 1 - side, axis, keepdims=False)
        kept = lax.dynamic_index_in_dim(split, side, axis, keepdims=False)
        left.remove(bit)
        flat = (2 ** len(left),) + block
        states = kept.reshape(flat) + traded(given.reshape(flat), "rollout", bit)
    return states[0]


def doubled(parts, earlier, bits):
    for bit in bits:
        other = traded(parts, "rollout", bit)
        low = earlier[(1, 2, 4, 8).index(bit)] == 1
        first, second = jnp.where(low, parts, other), jnp.where(low, other, parts)
        parts = jnp.stack([first, second], axis=1).reshape((-1,) + parts.shape[1:])
    return parts


def per_device(
    prompt_inputs, prompt_keys, prompt_steps, reply_inputs, reply_keys, reply_queries,
    reply_steps, decay_log, upstream, loss_mask, advantage_index, advantage_table,
):
    reply_inputs, reply_keys, reply_queries = reply_inputs[0], reply_keys[0], reply_queries[0]
    reply_steps, upstream = reply_steps[0], upstream[0]
    scale = (advantage_index, advantage_table)
    row, mine = lax.axis_index("rollout"), lax.axis_index("ctx")
    place = (row * SLICES + mine).astype(jnp.int32).reshape(1, 1)
    owner = mine.astype(jnp.int32).reshape(1, 1)
    slices = shape(SLICES, ROWS, STATE)
    heads = shape(HEADS, TOKENS)
    square = shape(TOKENS, TOKENS)
    wide = shape(TOKENS, CHANNELS, dtype=BF16)
    narrow = shape(TOKENS, STATE, dtype=BF16)

    prompt_logs, prompt_total = on_device(
        prompt_logs_kernel, [heads, shape(SLICES, TOKENS)], 1, 10**6, decay_log, prompt_steps
    )
    earlier = [((row & bit) == 0).astype(jnp.int32) for bit in (1, 2, 4, 8)]
    group_totals = swap(prompt_total, "ctx")
    pack, reply_logs = on_device(
        first_kernel, [shape(SLICES, GO, STATE), heads], 3, 5 * 10**9,
        decay_log, *scale, reply_inputs, reply_keys, reply_queries, reply_steps, upstream,
        loss_mask, vmem=VMEM_MOST,
    )
    later = jnp.sum(
        jnp.where(jnp.arange(SLICES)[:, None] > mine, group_totals, 0.0), axis=0, keepdims=True
    )
    total = jnp.sum(group_totals, axis=0, keepdims=True)
    later, total = (jnp.broadcast_to(x, (8, TOKENS)) for x in (later, total))
    pack, later, total, owner, place, earlier = lax.optimization_barrier(
        (pack, later, total, owner, place, earlier)
    )
    received = swap(pack, "ctx")
    later = later_sums(later, total, earlier)
    prompt_states, prompt_ends = on_device(
        prompt_states_kernel, [slices, heads], 0, 3 * 10**6,
        prompt_inputs, prompt_keys, prompt_steps, prompt_logs, later,
    )
    near, mixed, row_sums, column_sums = on_device(
        within_kernel, [shape(TOKENS, CHANNELS), square, heads, heads], 0, 6 * 10**6,
        reply_inputs, reply_keys, reply_queries, reply_steps, upstream, loss_mask, reply_logs,
    )
    prompt_states = turn(reduced_over_rows(prompt_states, earlier))
    received, prompt_states, row_sums = lax.optimization_barrier(
        (received, prompt_states, row_sums)
    )
    after, row_pulls, totals = on_device(
        group_kernel, [slices, shape(ROWS, STATE), shape(SLICES, STATE)], 1, 3 * 10**6,
        owner, received,
    )
    after = swap(after, "ctx")
    joint = jnp.concatenate([prompt_states, row_pulls], axis=0)
    for bit in (1, 2, 4, 8):
        joint = joint + traded(joint, "rollout", bit)
    starts, flag = on_device(
        carry_kernel, [slices, shape(8, STATE)], 1, 3 * 10**6,
        owner, totals, received, joint[:ROWS],
    )
    turned = turn(joint[ROWS:])
    turned, flag, after, near = lax.optimization_barrier((turned, flag, after, near))
    starts = swap(starts, "ctx")
    end_pull = doubled(turned[None], earlier, DOUBLING[:2])
    end_pull, after = lax.optimization_barrier((end_pull, after))
    reply_inputs_out, reply_keys_out, ended = on_device(
        reply_backward_kernel, [wide, narrow, heads], 2, 6 * 10**6,
        *scale, reply_inputs, reply_keys, reply_queries, reply_steps, reply_logs, after, near,
        mixed,
    )
    end_pull = doubled(end_pull, earlier, DOUBLING[2:3])
    end_pull, ended = lax.optimization_barrier((end_pull, ended))
    end_pull = doubled(end_pull, earlier, DOUBLING[3:])
    prompt_inputs_out, prompt_keys_out, owned, prompt_decay = on_device(
        prompt_backward_kernel, [wide, narrow, heads, shape(8, TOKENS)], 1, 6 * 10**6,
        decay_log, prompt_inputs, prompt_keys, prompt_steps, prompt_logs, prompt_ends, end_pull,
        flag,
    )
    reply_queries_out, reply_steps_out, summary = on_device(
        reply_forward_kernel, [narrow, heads, shape(DEVICES, TOKENS)], 3, 6 * 10**6,
        decay_log, *scale, reply_keys, reply_queries, reply_steps, upstream, loss_mask,
        reply_logs, starts, after, mixed, row_sums, column_sums, ended, prompt_decay,
    )
    prompt_steps_out, decay = on_device(
        finish_kernel, [heads, shape(8, TOKENS)], 2, 10**8,
        place, decay_log, swap(summary, BOTH), owned, prompt_steps,
    )
    return (
        prompt_inputs_out, prompt_keys_out, prompt_steps_out, reply_inputs_out[None],
        reply_keys_out[None], reply_queries_out[None], reply_steps_out[None], decay[0, :HEADS],
    )


def solution(mesh):
    in_specs = (
        P(("rollout", "ctx"), None),
        P(("rollout", "ctx"), None),
        P(None, ("rollout", "ctx")),
        P("rollout", "ctx", None),
        P("rollout", "ctx", None),
        P("rollout", "ctx", None),
        P("rollout", None, "ctx"),
        P(),
        P("rollout", "ctx", None),
        P("rollout", "ctx"),
        P("rollout"),
        P(),
    )
    out_specs = (
        P(("rollout", "ctx"), None),
        P(("rollout", "ctx"), None),
        P(None, ("rollout", "ctx")),
        P("rollout", "ctx", None),
        P("rollout", "ctx", None),
        P("rollout", "ctx", None),
        P("rollout", None, "ctx"),
        P(),
    )
    return jax.shard_map(
        per_device, mesh=mesh, in_specs=in_specs, out_specs=out_specs, check_vma=False
    )
```

```python
import jax
import jax.numpy as jnp
from jax import lax
from jax.experimental import pallas as pl
from jax.experimental.pallas import tpu as pltpu
from jax.sharding import PartitionSpec as P

HEADS = 40
HEAD_DIM = 64
STATE = 128
TOKENS = 128
CHANNELS = HEADS * HEAD_DIM
PAIRS = HEADS // 2
SLICES = 16
DEVICES = SLICES * SLICES
ROWS = CHANNELS // SLICES
GO = 2 * ROWS + 8
PIECE = 32
PER_SLICE = ROWS // PIECE
F32 = jnp.float32
BF16 = jnp.bfloat16
HIGHEST = lax.Precision.HIGHEST
VMEM_BYTES = 24 * 1024 * 1024
VMEM_MOST = 56 * 1024 * 1024
DOUBLING = (2, 8, 4, 1)
HALVING = (1, 4, 8, 2)
BOTH = ("rollout", "ctx")


def iota(shape, axis):
    return lax.broadcasted_iota(jnp.int32, shape, axis)


def halves(value):
    high = value.astype(BF16)
    return high, (value - high.astype(F32)).astype(BF16)


def dot(left, right):
    return jnp.dot(left, right, preferred_element_type=F32)


def dot_t(left, right, precision=None):
    return lax.dot_general(
        left, right, (((1,), (1,)), ((), ())), preferred_element_type=F32, precision=precision
    )


def exact_dot(left, right):
    return jnp.dot(left, right, preferred_element_type=F32, precision=HIGHEST)


def running_logs(steps, rate):
    earlier = (iota((TOKENS, TOKENS), 0) <= iota((TOKENS, TOKENS), 1)).astype(F32)
    return exact_dot(-steps * rate, earlier)


def transposed(rows, before=0):
    parts = [rows, jnp.zeros((TOKENS - before - rows.shape[0], TOKENS), F32)]
    if before:
        parts = [jnp.zeros((before, TOKENS), F32)] + parts
    return jnp.concatenate(parts, axis=0).T


def as_columns(row):
    return jnp.broadcast_to(row, (TOKENS, TOKENS)).T


def pair_rows(rows, pair):
    first = jnp.broadcast_to(rows[2 * pair : 2 * pair + 1], (HEAD_DIM, TOKENS))
    second = jnp.broadcast_to(rows[2 * pair + 1 : 2 * pair + 2], (HEAD_DIM, TOKENS))
    return jnp.concatenate([first, second], axis=0)


def column(columns, head):
    return jnp.broadcast_to(columns[:, head : head + 1], (TOKENS, TOKENS))


def pieces(pair):
    for part in range(4):
        place = 4 * pair + part
        yield part * PIECE, place // PER_SLICE, (place % PER_SLICE) * PIECE


def first_lanes():
    return iota((TOKENS, TOKENS), 1) < HEAD_DIM


def sides(block):
    zero = jnp.zeros((), BF16)
    half = first_lanes()
    return jnp.concatenate([jnp.where(half, block, zero), jnp.where(half, zero, block)], axis=0)


def span(pair):
    return slice(pair * TOKENS, (pair + 1) * TOKENS)


def gather(received, pair, order=None):
    places = order or range(SLICES)
    return jnp.concatenate(
        [
            received[places[owner], offset : offset + PIECE, :]
            for at, owner, offset in pieces(pair)
        ],
        axis=0,
    )


def doubled_order():
    places = []
    for owner in range(SLICES):
        place = 0
        for bit in DOUBLING:
            place = 2 * place + (1 if owner & bit else 0)
        places.append(place)
    return places


def pack_states(pack, base, tokens, rows, keys):
    twice = jnp.concatenate([keys, keys], axis=0)
    for pair in range(PAIRS):
        block = tokens[:, span(pair)].astype(F32).T
        high, low = halves(block * pair_rows(rows, pair))
        states = dot(jnp.concatenate([high, low], axis=1), twice)
        for at, owner, offset in pieces(pair):
            pack[owner, base + offset : base + offset + PIECE, :] = states[at : at + PIECE]


def rates(decay_log):
    heads = iota((HEADS, TOKENS), 0)
    logs = jnp.zeros((HEADS, TOKENS), F32)
    for head in range(HEADS):
        logs = jnp.where(heads == head, decay_log[head], logs)
    return jnp.exp(logs)


def prompt_logs_kernel(decay_log, steps, logs, total):
    running = running_logs(steps[...], rates(decay_log))
    logs[...] = running
    last = jnp.broadcast_to(running[:, TOKENS - 1 :], (HEADS, TOKENS))
    total[...] = transposed(last)[0:SLICES]


def first_kernel(
    decay_log, index, table, inputs, keys, queries, steps, upstream, mask, pack, reply_logs
):
    running = running_logs(steps[...], rates(decay_log))
    reply_logs[...] = running
    last = jnp.broadcast_to(running[:, TOKENS - 1 :], (HEADS, TOKENS))
    total = transposed(last)[0:8]
    for owner in range(SLICES):
        pack[owner, 2 * ROWS :, :] = total
    rows = jnp.exp(running) * (mask[...].astype(F32) * table[index[0]])
    pack_states(pack, 0, upstream, rows, queries[...])
    rows = jnp.exp(last - running) * steps[...]
    pack_states(pack, ROWS, inputs, rows, keys[...])


def prompt_states_kernel(inputs, keys, steps, logs, later, pack, ends):
    running = logs[...]
    after = as_columns(later[0:1, :])[:HEADS]
    rows = jnp.exp(running[:, TOKENS - 1 :] - running + after) * steps[...]
    ends[...] = rows
    pack_states(pack, 0, inputs, rows, keys[...])


def within_kernel(
    inputs, keys, queries, steps, upstream, mask_row, logs, near, mixed, row_sums, column_sums
):
    running = logs[...]
    columns = transposed(jnp.log(steps[...]) - running)
    causal = iota((TOKENS, TOKENS), 1) >= iota((TOKENS, TOKENS), 0)
    lanes = iota((TOKENS, TOKENS), 1)
    scores = dot_t(keys[...], queries[...])
    mask = as_columns(mask_row[...].astype(F32)).astype(BF16)
    total = jnp.zeros((TOKENS, TOKENS), F32)
    gathered = jnp.zeros((TOKENS, TOKENS), F32)
    for pair in range(PAIRS):
        pulled = upstream[:, span(pair)] * mask
        products = dot_t(sides(inputs[:, span(pair)]), pulled)
        highs, lows = [], []
        for side in range(2):
            head = 2 * pair + side
            gaps = running[head : head + 1] + column(columns, head)
            mixing = jnp.where(causal, jnp.exp(gaps), 0.0)
            weighted = mixing * products[side * TOKENS : (side + 1) * TOKENS]
            total = total + weighted
            terms = weighted * scores
            row_sums[head : head + 1, :] = jnp.sum(terms, axis=0, keepdims=True)
            gathered = jnp.where(lanes == head, jnp.sum(terms, axis=1, keepdims=True), gathered)
            high, low = halves(mixing * scores)
            highs.append(high)
            lows.append(low)
        both = sides(pulled)
        near[:, span(pair)] = dot(jnp.concatenate(highs, axis=1), both) + dot(
            jnp.concatenate(lows, axis=1), both
        )
    mixed[...] = total
    column_sums[...] = gathered.T[:HEADS]


def spread(columns, at):
    return jnp.broadcast_to(columns[:, at : at + 1], (ROWS, TOKENS))


def owner_columns(owner, rows):
    place = owner * ROWS + iota((ROWS, TOKENS), 0)
    chosen = (lax.shift_right_logical(place, 6) == iota((ROWS, TOKENS), 1)).astype(F32)
    pad = jnp.zeros((TOKENS - rows.shape[0], TOKENS), F32)
    return dot_t(chosen, jnp.concatenate([rows, pad], axis=0), HIGHEST)


def group_kernel(owner, received, after, start, totals):
    reply = jnp.concatenate(
        [received[c, 2 * ROWS : 2 * ROWS + 1, :] for c in range(SLICES)], axis=0
    )
    totals[...] = reply
    factors = jnp.exp(owner_columns(owner[0, 0], reply))
    pulled = jnp.zeros((ROWS, TOKENS), F32)
    for c in range(SLICES - 1, -1, -1):
        after[c] = pulled
        pulled = spread(factors, c) * pulled + received[c, 0:ROWS, :]
    start[...] = pulled


def carry_kernel(owner, totals, received, end_state, starts, flag):
    flag[...] = end_state[0:8, :]
    factors = jnp.exp(owner_columns(owner[0, 0], totals[...]))
    state = end_state[...]
    for c in range(SLICES):
        starts[c] = state
        if c < SLICES - 1:
            state = spread(factors, c) * state + received[c, ROWS : 2 * ROWS, :]


def backward_parts(inputs, pulls, ends, keys, near, scale, inputs_out, order=None):
    twice = jnp.concatenate([keys, keys], axis=1)
    wide = keys.astype(F32)
    lanes = iota((TOKENS, TOKENS), 1)
    half = first_lanes()
    total = jnp.zeros((TOKENS, TOKENS), F32)
    gathered = jnp.zeros((TOKENS, TOKENS), F32)
    columns = transposed(ends)
    for pair in range(PAIRS):
        high, low = halves(gather(pulls, pair, order))
        once = sides(inputs[:, span(pair)])
        backward = dot(
            jnp.concatenate([once, once], axis=1), jnp.concatenate([high, low], axis=0)
        )
        keyed = dot_t(twice, jnp.concatenate([high, low], axis=1))
        factors = []
        for side in range(2):
            head = 2 * pair + side
            factors.append(column(columns, head))
            part = factors[side] * backward[side * TOKENS : (side + 1) * TOKENS]
            total = total + part
            gathered = jnp.where(
                lanes == head, jnp.sum(part * wide, axis=1, keepdims=True), gathered
            )
        own = jnp.where(half, factors[0], factors[1]) * keyed
        if near is not None:
            own = near[:, span(pair)] * scale + own
        inputs_out[:, span(pair)] = own.astype(BF16)
    return total, gathered.T[:HEADS]


def reply_backward_kernel(
    index, table, inputs, keys, queries, steps, logs, pulls, near, mixed, inputs_out, keys_out, ended_out
):
    scale = table[index[0]]
    running = logs[...]
    ends = jnp.exp(running[:, TOKENS - 1 :] - running) * steps[...]
    total, ended = backward_parts(inputs, pulls, ends, keys[...], near, scale, inputs_out)
    high, low = halves(mixed[...] * scale)
    total = total + dot(high, queries[...]) + dot(low, queries[...])
    keys_out[...] = total.astype(BF16)
    ended_out[...] = ended


def log_sums(rows):
    lower = (iota((TOKENS, TOKENS), 0) < iota((TOKENS, TOKENS), 1)).astype(F32)
    return exact_dot(rows, lower)


def prompt_backward_kernel(
    decay_log, inputs, keys, steps, logs, ends, pulls, _,
    inputs_out, keys_out, owned_out, decay,
):
    rate = rates(decay_log)
    total, owned = backward_parts(
        inputs, pulls, ends[...], keys[...], None, None, inputs_out, doubled_order()
    )
    keys_out[...] = total.astype(BF16)
    owned_out[...] = owned
    inside = jnp.sum(-steps[...] * rate * log_sums(owned), axis=1, keepdims=True)
    sums = jnp.sum(owned, axis=1, keepdims=True)
    stacked = jnp.broadcast_to(
        jnp.concatenate([inside, sums, logs[:, TOKENS - 1 :]], axis=0), (3 * HEADS, TOKENS)
    )
    decay[...] = transposed(stacked)[0:8]


def reply_forward_kernel(
    decay_log, index, table, keys, queries, steps, upstream, mask_row, logs, starts, pulls, mixed,
    row_sums, column_sums, ended, prompt_decay, queries_out, steps_out, summary,
):
    scale = table[index[0]]
    running = logs[...]
    rate = rates(decay_log)
    reach = transposed(jnp.exp(running) * scale)
    mask = as_columns(mask_row[...].astype(F32)).astype(BF16)
    lanes = iota((TOKENS, TOKENS), 1)
    wide = queries[...].astype(F32)
    total = jnp.zeros((TOKENS, TOKENS), F32)
    reached = jnp.zeros((TOKENS, TOKENS), F32)
    overlaps = []
    for pair in range(PAIRS):
        state = gather(starts, pair)
        shared = state * gather(pulls, pair)
        overlaps.append(jnp.sum(shared[:HEAD_DIM], axis=0, keepdims=True))
        overlaps.append(jnp.sum(shared[HEAD_DIM:], axis=0, keepdims=True))
        high, low = halves(state)
        once = sides(upstream[:, span(pair)] * mask)
        forward = dot(
            jnp.concatenate([once, once], axis=1), jnp.concatenate([high, low], axis=0)
        )
        for side in range(2):
            head = 2 * pair + side
            part = column(reach, head) * forward[side * TOKENS : (side + 1) * TOKENS]
            total = total + part
            reached = jnp.where(
                lanes == head, jnp.sum(part * wide, axis=1, keepdims=True), reached
            )
    high, low = halves((mixed[...] * scale).T)
    total = total + dot(high, keys[...]) + dot(low, keys[...])
    queries_out[...] = total.astype(BF16)
    reached = reached.T[:HEADS]
    later = (iota((TOKENS, TOKENS), 0) >= iota((TOKENS, TOKENS), 1)).astype(F32)
    carried = jnp.sum(jnp.concatenate(overlaps, axis=0), axis=1, keepdims=True)
    carried = carried * jnp.exp(running[:, TOKENS - 1 :])
    closer = column_sums[...] * scale
    log_pull = (
        exact_dot(row_sums[...] * scale - closer + reached, later) + log_sums(ended[...]) + carried
    )
    steps_out[...] = (closer + ended[...]) / steps[...] - rate * log_pull
    local = jnp.sum(-steps[...] * rate * log_pull, axis=1, keepdims=True)
    row = transposed(jnp.broadcast_to(local, (HEADS, TOKENS)))[0:1] + prompt_decay[0:1]
    summary[...] = jnp.broadcast_to(row, (DEVICES, TOKENS))


def moved_lanes(rows, by):
    shift = (iota((TOKENS, TOKENS), 0) == iota((TOKENS, TOKENS), 1) + by).astype(F32)
    return exact_dot(rows, shift)


def finish_kernel(place, decay_log, received, owned, steps, steps_out, decay):
    rows = received[...]
    below = (iota((DEVICES, DEVICES), 0) > iota((DEVICES, DEVICES), 1)).astype(F32)
    before = exact_dot(below, moved_lanes(rows, HEADS))
    decay_rows = rows + before * moved_lanes(rows, 2 * HEADS)
    decay[...] = jnp.broadcast_to(jnp.sum(decay_rows, axis=0, keepdims=True), (8, TOKENS))
    mine = jnp.where(iota((DEVICES, TOKENS), 0) < place[0, 0], rows, 0.0)
    mine = as_columns(jnp.sum(mine, axis=0, keepdims=True))[HEADS : 2 * HEADS]
    steps_out[...] = owned[...] / steps[...] - rates(decay_log) * (log_sums(owned[...]) + mine)


def whole(dims):
    return pl.BlockSpec(dims, lambda step: (0,) * len(dims))


def on_device(kernel, out_shapes, scalars, flops, *operands, vmem=VMEM_BYTES):
    specs = [pl.BlockSpec(memory_space=pltpu.SMEM) for _ in range(scalars)]
    specs += [whole(x.shape) for x in operands[scalars:]]
    return pl.pallas_call(
        kernel,
        grid=(1,),
        out_shape=out_shapes,
        in_specs=specs,
        out_specs=[whole(x.shape) for x in out_shapes],
        compiler_params=pltpu.CompilerParams(vmem_limit_bytes=vmem),
        cost_estimate=pl.CostEstimate(flops=flops, bytes_accessed=1024, transcendentals=0),
    )(*operands)


def shape(*dims, dtype=F32):
    return jax.ShapeDtypeStruct(dims, dtype)


def swap(value, axis):
    return lax.all_to_all(value, axis, 0, 0, tiled=True)


def turn(block):
    pairs = [(a * SLICES + b, b * SLICES + a) for a in range(SLICES) for b in range(SLICES)]
    return lax.ppermute(block, BOTH, pairs)


def traded(value, axis, bit):
    return lax.ppermute(value, axis, [(at, at ^ bit) for at in range(SLICES)])


def later_sums(later, total, earlier):
    for step, bit in enumerate((1, 2, 4, 8)):
        other = traded(total, "rollout", bit)
        later = later + jnp.where(earlier[step] == 1, other, 0.0)
        total = total + other
    return later


def reduced_over_rows(states, earlier, beside):
    block = states.shape[1:]
    left = [8, 4, 2, 1]
    for bit in HALVING:
        side = 1 - earlier[(1, 2, 4, 8).index(bit)]
        axis = left.index(bit)
        split = states.reshape((2,) * len(left) + block)
        given = lax.dynamic_index_in_dim(split, 1 - side, axis, keepdims=False)
        kept = lax.dynamic_index_in_dim(split, side, axis, keepdims=False)
        left.remove(bit)
        flat = (2 ** len(left),) + block
        states = kept.reshape(flat) + traded(given.reshape(flat), "rollout", bit)
        if bit == HALVING[1]:
            states, beside = lax.optimization_barrier((states, beside))
    return states[0], beside


def doubled(parts, earlier, bits):
    for bit in bits:
        other = traded(parts, "rollout", bit)
        low = earlier[(1, 2, 4, 8).index(bit)] == 1
        first, second = jnp.where(low, parts, other), jnp.where(low, other, parts)
        parts = jnp.stack([first, second], axis=1).reshape((-1,) + parts.shape[1:])
    return parts


def per_device(
    prompt_inputs, prompt_keys, prompt_steps, reply_inputs, reply_keys, reply_queries,
    reply_steps, decay_log, upstream, loss_mask, advantage_index, advantage_table,
):
    reply_inputs, reply_keys, reply_queries = reply_inputs[0], reply_keys[0], reply_queries[0]
    reply_steps, upstream = reply_steps[0], upstream[0]
    scale = (advantage_index, advantage_table)
    row, mine = lax.axis_index("rollout"), lax.axis_index("ctx")
    place = (row * SLICES + mine).astype(jnp.int32).reshape(1, 1)
    owner = mine.astype(jnp.int32).reshape(1, 1)
    slices = shape(SLICES, ROWS, STATE)
    heads = shape(HEADS, TOKENS)
    square = shape(TOKENS, TOKENS)
    wide = shape(TOKENS, CHANNELS, dtype=BF16)
    narrow = shape(TOKENS, STATE, dtype=BF16)

    prompt_logs, prompt_total = on_device(
        prompt_logs_kernel, [heads, shape(SLICES, TOKENS)], 1, 10**6, decay_log, prompt_steps
    )
    earlier = [((row & bit) == 0).astype(jnp.int32) for bit in (1, 2, 4, 8)]
    group_totals = swap(prompt_total, "ctx")
    pack, reply_logs = on_device(
        first_kernel, [shape(SLICES, GO, STATE), heads], 3, 5 * 10**9,
        decay_log, *scale, reply_inputs, reply_keys, reply_queries, reply_steps, upstream,
        loss_mask, vmem=VMEM_MOST,
    )
    later = jnp.sum(
        jnp.where(jnp.arange(SLICES)[:, None] > mine, group_totals, 0.0), axis=0, keepdims=True
    )
    total = jnp.sum(group_totals, axis=0, keepdims=True)
    later, total = (jnp.broadcast_to(x, (8, TOKENS)) for x in (later, total))
    pack, later, total, owner, place, earlier = lax.optimization_barrier(
        (pack, later, total, owner, place, earlier)
    )
    received = swap(pack, "ctx")
    later = later_sums(later, total, earlier)
    prompt_states, prompt_ends = on_device(
        prompt_states_kernel, [slices, heads], 0, 3 * 10**6,
        prompt_inputs, prompt_keys, prompt_steps, prompt_logs, later,
    )
    near, mixed, row_sums, column_sums = on_device(
        within_kernel, [shape(TOKENS, CHANNELS), square, heads, heads], 0, 6 * 10**6,
        reply_inputs, reply_keys, reply_queries, reply_steps, upstream, loss_mask, reply_logs,
    )
    prompt_states, row_sums = reduced_over_rows(prompt_states, earlier, row_sums)
    received, prompt_states = lax.optimization_barrier((received, turn(prompt_states)))
    after, row_pulls, totals = on_device(
        group_kernel, [slices, shape(ROWS, STATE), shape(SLICES, STATE)], 1, 3 * 10**6,
        owner, received,
    )
    after = swap(after, "ctx")
    joint = jnp.concatenate([prompt_states, row_pulls], axis=0)
    for bit in (1, 2, 4, 8):
        joint = joint + traded(joint, "rollout", bit)
    starts, flag = on_device(
        carry_kernel, [slices, shape(8, STATE)], 1, 3 * 10**6,
        owner, totals, received, joint[:ROWS],
    )
    turned = turn(joint[ROWS:])
    turned, flag, after, near = lax.optimization_barrier((turned, flag, after, near))
    starts = swap(starts, "ctx")
    end_pull = doubled(turned[None], earlier, DOUBLING[:2])
    end_pull, after = lax.optimization_barrier((end_pull, after))
    reply_inputs_out, reply_keys_out, ended = on_device(
        reply_backward_kernel, [wide, narrow, heads], 2, 6 * 10**6,
        *scale, reply_inputs, reply_keys, reply_queries, reply_steps, reply_logs, after, near,
        mixed,
    )
    end_pull = doubled(end_pull, earlier, DOUBLING[2:3])
    end_pull, ended = lax.optimization_barrier((end_pull, ended))
    end_pull = doubled(end_pull, earlier, DOUBLING[3:])
    prompt_inputs_out, prompt_keys_out, owned, prompt_decay = on_device(
        prompt_backward_kernel, [wide, narrow, heads, shape(8, TOKENS)], 1, 6 * 10**6,
        decay_log, prompt_inputs, prompt_keys, prompt_steps, prompt_logs, prompt_ends, end_pull,
        flag,
    )
    reply_queries_out, reply_steps_out, summary = on_device(
        reply_forward_kernel, [narrow, heads, shape(DEVICES, TOKENS)], 3, 6 * 10**6,
        decay_log, *scale, reply_keys, reply_queries, reply_steps, upstream, loss_mask,
        reply_logs, starts, after, mixed, row_sums, column_sums, ended, prompt_decay,
        vmem=VMEM_MOST,
    )
    prompt_steps_out, decay = on_device(
        finish_kernel, [heads, shape(8, TOKENS)], 2, 10**8,
        place, decay_log, swap(summary, BOTH), owned, prompt_steps,
    )
    return (
        prompt_inputs_out, prompt_keys_out, prompt_steps_out, reply_inputs_out[None],
        reply_keys_out[None], reply_queries_out[None], reply_steps_out[None], decay[0, :HEADS],
    )


def solution(mesh):
    in_specs = (
        P(("rollout", "ctx"), None),
        P(("rollout", "ctx"), None),
        P(None, ("rollout", "ctx")),
        P("rollout", "ctx", None),
        P("rollout", "ctx", None),
        P("rollout", "ctx", None),
        P("rollout", None, "ctx"),
        P(),
        P("rollout", "ctx", None),
        P("rollout", "ctx"),
        P("rollout"),
        P(),
    )
    out_specs = (
        P(("rollout", "ctx"), None),
        P(("rollout", "ctx"), None),
        P(None, ("rollout", "ctx")),
        P("rollout", "ctx", None),
        P("rollout", "ctx", None),
        P("rollout", "ctx", None),
        P("rollout", None, "ctx"),
        P(),
    )
    return jax.shard_map(
        per_device, mesh=mesh, in_specs=in_specs, out_specs=out_specs, check_vma=False
    )
```

```python
import jax
import jax.numpy as jnp
from jax import lax
from jax.experimental import pallas as pl
from jax.experimental.pallas import tpu as pltpu
from jax.sharding import PartitionSpec as P

HEADS = 40
HEAD_DIM = 64
STATE = 128
TOKENS = 128
CHANNELS = HEADS * HEAD_DIM
PAIRS = HEADS // 2
SLICES = 16
DEVICES = SLICES * SLICES
ROWS = CHANNELS // SLICES
GO = 2 * ROWS + 8
PIECE = 32
PER_SLICE = ROWS // PIECE
F32 = jnp.float32
BF16 = jnp.bfloat16
HIGHEST = lax.Precision.HIGHEST
VMEM_BYTES = 24 * 1024 * 1024
VMEM_MOST = 56 * 1024 * 1024
DOUBLING = (2, 8, 4, 1)
HALVING = (1, 4, 8, 2)
BOTH = ("rollout", "ctx")


def iota(shape, axis):
    return lax.broadcasted_iota(jnp.int32, shape, axis)


def halves(value):
    high = value.astype(BF16)
    return high, (value - high.astype(F32)).astype(BF16)


def dot(left, right):
    return jnp.dot(left, right, preferred_element_type=F32)


def dot_t(left, right, precision=None):
    return lax.dot_general(
        left, right, (((1,), (1,)), ((), ())), preferred_element_type=F32, precision=precision
    )


def exact_dot(left, right):
    return jnp.dot(left, right, preferred_element_type=F32, precision=HIGHEST)


def running_logs(steps, rate):
    earlier = (iota((TOKENS, TOKENS), 0) <= iota((TOKENS, TOKENS), 1)).astype(F32)
    return exact_dot(-steps * rate, earlier)


def transposed(rows, before=0):
    parts = [rows, jnp.zeros((TOKENS - before - rows.shape[0], TOKENS), F32)]
    if before:
        parts = [jnp.zeros((before, TOKENS), F32)] + parts
    return jnp.concatenate(parts, axis=0).T


def as_columns(row):
    return jnp.broadcast_to(row, (TOKENS, TOKENS)).T


def pair_rows(rows, pair):
    first = jnp.broadcast_to(rows[2 * pair : 2 * pair + 1], (HEAD_DIM, TOKENS))
    second = jnp.broadcast_to(rows[2 * pair + 1 : 2 * pair + 2], (HEAD_DIM, TOKENS))
    return jnp.concatenate([first, second], axis=0)


def column(columns, head):
    return jnp.broadcast_to(columns[:, head : head + 1], (TOKENS, TOKENS))


def pieces(pair):
    for part in range(4):
        place = 4 * pair + part
        yield part * PIECE, place // PER_SLICE, (place % PER_SLICE) * PIECE


def first_lanes():
    return iota((TOKENS, TOKENS), 1) < HEAD_DIM


def sides(block):
    zero = jnp.zeros((), BF16)
    half = first_lanes()
    return jnp.concatenate([jnp.where(half, block, zero), jnp.where(half, zero, block)], axis=0)


def span(pair):
    return slice(pair * TOKENS, (pair + 1) * TOKENS)


def gather(received, pair, order=None):
    places = order or range(SLICES)
    return jnp.concatenate(
        [
            received[places[owner], offset : offset + PIECE, :]
            for at, owner, offset in pieces(pair)
        ],
        axis=0,
    )


def doubled_order():
    places = []
    for owner in range(SLICES):
        place = 0
        for bit in DOUBLING:
            place = 2 * place + (1 if owner & bit else 0)
        places.append(place)
    return places


def pack_states(pack, base, tokens, rows, keys):
    twice = jnp.concatenate([keys, keys], axis=0)
    for pair in range(PAIRS):
        block = tokens[:, span(pair)].astype(F32).T
        high, low = halves(block * pair_rows(rows, pair))
        states = dot(jnp.concatenate([high, low], axis=1), twice)
        for at, owner, offset in pieces(pair):
            pack[owner, base + offset : base + offset + PIECE, :] = states[at : at + PIECE]


def rates(decay_log):
    heads = iota((HEADS, TOKENS), 0)
    logs = jnp.zeros((HEADS, TOKENS), F32)
    for head in range(HEADS):
        logs = jnp.where(heads == head, decay_log[head], logs)
    return jnp.exp(logs)


def prompt_logs_kernel(decay_log, steps, logs, total):
    running = running_logs(steps[...], rates(decay_log))
    logs[...] = running
    last = jnp.broadcast_to(running[:, TOKENS - 1 :], (HEADS, TOKENS))
    total[...] = transposed(last)[0:SLICES]


def first_kernel(
    decay_log, index, table, inputs, keys, queries, steps, upstream, mask, pack, reply_logs
):
    running = running_logs(steps[...], rates(decay_log))
    reply_logs[...] = running
    last = jnp.broadcast_to(running[:, TOKENS - 1 :], (HEADS, TOKENS))
    total = transposed(last)[0:8]
    for owner in range(SLICES):
        pack[owner, 2 * ROWS :, :] = total
    rows = jnp.exp(running) * (mask[...].astype(F32) * table[index[0]])
    pack_states(pack, 0, upstream, rows, queries[...])
    rows = jnp.exp(last - running) * steps[...]
    pack_states(pack, ROWS, inputs, rows, keys[...])


def prompt_states_kernel(inputs, keys, steps, logs, later, pack, ends):
    running = logs[...]
    after = as_columns(later[0:1, :])[:HEADS]
    rows = jnp.exp(running[:, TOKENS - 1 :] - running + after) * steps[...]
    ends[...] = rows
    pack_states(pack, 0, inputs, rows, keys[...])


def within_kernel(
    inputs, keys, queries, steps, upstream, mask_row, logs, near, mixed, row_sums, column_sums
):
    running = logs[...]
    columns = transposed(jnp.log(steps[...]) - running)
    causal = iota((TOKENS, TOKENS), 1) >= iota((TOKENS, TOKENS), 0)
    lanes = iota((TOKENS, TOKENS), 1)
    scores = dot_t(keys[...], queries[...])
    mask = as_columns(mask_row[...].astype(F32)).astype(BF16)
    total = jnp.zeros((TOKENS, TOKENS), F32)
    gathered = jnp.zeros((TOKENS, TOKENS), F32)
    for pair in range(PAIRS):
        pulled = upstream[:, span(pair)] * mask
        products = dot_t(sides(inputs[:, span(pair)]), pulled)
        highs, lows = [], []
        for side in range(2):
            head = 2 * pair + side
            gaps = running[head : head + 1] + column(columns, head)
            mixing = jnp.where(causal, jnp.exp(gaps), 0.0)
            weighted = mixing * products[side * TOKENS : (side + 1) * TOKENS]
            total = total + weighted
            terms = weighted * scores
            row_sums[head : head + 1, :] = jnp.sum(terms, axis=0, keepdims=True)
            gathered = jnp.where(lanes == head, jnp.sum(terms, axis=1, keepdims=True), gathered)
            high, low = halves(mixing * scores)
            highs.append(high)
            lows.append(low)
        both = sides(pulled)
        near[:, span(pair)] = dot(jnp.concatenate(highs, axis=1), both) + dot(
            jnp.concatenate(lows, axis=1), both
        )
    mixed[...] = total
    column_sums[...] = gathered.T[:HEADS]


def spread(columns, at):
    return jnp.broadcast_to(columns[:, at : at + 1], (ROWS, TOKENS))


def owner_columns(owner, rows):
    place = owner * ROWS + iota((ROWS, TOKENS), 0)
    chosen = (lax.shift_right_logical(place, 6) == iota((ROWS, TOKENS), 1)).astype(F32)
    pad = jnp.zeros((TOKENS - rows.shape[0], TOKENS), F32)
    return dot_t(chosen, jnp.concatenate([rows, pad], axis=0), HIGHEST)


def group_kernel(owner, received, after, start, totals):
    reply = jnp.concatenate(
        [received[c, 2 * ROWS : 2 * ROWS + 1, :] for c in range(SLICES)], axis=0
    )
    totals[...] = reply
    factors = jnp.exp(owner_columns(owner[0, 0], reply))
    pulled = jnp.zeros((ROWS, TOKENS), F32)
    for c in range(SLICES - 1, -1, -1):
        after[c] = pulled
        pulled = spread(factors, c) * pulled + received[c, 0:ROWS, :]
    start[...] = pulled


def carry_kernel(owner, totals, received, end_state, starts, flag):
    flag[...] = end_state[0:8, :]
    factors = jnp.exp(owner_columns(owner[0, 0], totals[...]))
    state = end_state[...]
    for c in range(SLICES):
        starts[c] = state
        if c < SLICES - 1:
            state = spread(factors, c) * state + received[c, ROWS : 2 * ROWS, :]


def backward_parts(inputs, pulls, ends, keys, near, scale, inputs_out, order=None):
    twice = jnp.concatenate([keys, keys], axis=1)
    wide = keys.astype(F32)
    lanes = iota((TOKENS, TOKENS), 1)
    half = first_lanes()
    total = jnp.zeros((TOKENS, TOKENS), F32)
    gathered = jnp.zeros((TOKENS, TOKENS), F32)
    columns = transposed(ends)
    for pair in range(PAIRS):
        high, low = halves(gather(pulls, pair, order))
        once = sides(inputs[:, span(pair)])
        backward = dot(
            jnp.concatenate([once, once], axis=1), jnp.concatenate([high, low], axis=0)
        )
        keyed = dot_t(twice, jnp.concatenate([high, low], axis=1))
        factors = []
        for side in range(2):
            head = 2 * pair + side
            factors.append(column(columns, head))
            part = factors[side] * backward[side * TOKENS : (side + 1) * TOKENS]
            total = total + part
            gathered = jnp.where(
                lanes == head, jnp.sum(part * wide, axis=1, keepdims=True), gathered
            )
        own = jnp.where(half, factors[0], factors[1]) * keyed
        if near is not None:
            own = near[:, span(pair)] * scale + own
        inputs_out[:, span(pair)] = own.astype(BF16)
    return total, gathered.T[:HEADS]


def reply_backward_kernel(
    index, table, inputs, keys, queries, steps, logs, pulls, near, mixed, inputs_out, keys_out, ended_out
):
    scale = table[index[0]]
    running = logs[...]
    ends = jnp.exp(running[:, TOKENS - 1 :] - running) * steps[...]
    total, ended = backward_parts(inputs, pulls, ends, keys[...], near, scale, inputs_out)
    high, low = halves(mixed[...] * scale)
    total = total + dot(high, queries[...]) + dot(low, queries[...])
    keys_out[...] = total.astype(BF16)
    ended_out[...] = ended


def log_sums(rows):
    lower = (iota((TOKENS, TOKENS), 0) < iota((TOKENS, TOKENS), 1)).astype(F32)
    return exact_dot(rows, lower)


def prompt_backward_kernel(
    decay_log, inputs, keys, steps, logs, ends, pulls, _,
    inputs_out, keys_out, owned_out, decay,
):
    rate = rates(decay_log)
    total, owned = backward_parts(
        inputs, pulls, ends[...], keys[...], None, None, inputs_out, doubled_order()
    )
    keys_out[...] = total.astype(BF16)
    owned_out[...] = owned
    inside = jnp.sum(-steps[...] * rate * log_sums(owned), axis=1, keepdims=True)
    sums = jnp.sum(owned, axis=1, keepdims=True)
    stacked = jnp.broadcast_to(
        jnp.concatenate([inside, sums, logs[:, TOKENS - 1 :]], axis=0), (3 * HEADS, TOKENS)
    )
    decay[...] = transposed(stacked)[0:8]


def reply_forward_kernel(
    decay_log, index, table, keys, queries, steps, upstream, mask_row, logs, starts, pulls, mixed,
    row_sums, column_sums, ended, prompt_decay, queries_out, steps_out, summary,
):
    scale = table[index[0]]
    running = logs[...]
    rate = rates(decay_log)
    reach = transposed(jnp.exp(running) * scale)
    mask = as_columns(mask_row[...].astype(F32)).astype(BF16)
    lanes = iota((TOKENS, TOKENS), 1)
    wide = queries[...].astype(F32)
    total = jnp.zeros((TOKENS, TOKENS), F32)
    reached = jnp.zeros((TOKENS, TOKENS), F32)
    overlaps = []
    for pair in range(PAIRS):
        state = gather(starts, pair)
        shared = state * gather(pulls, pair)
        overlaps.append(jnp.sum(shared[:HEAD_DIM], axis=0, keepdims=True))
        overlaps.append(jnp.sum(shared[HEAD_DIM:], axis=0, keepdims=True))
        high, low = halves(state)
        once = sides(upstream[:, span(pair)] * mask)
        forward = dot(
            jnp.concatenate([once, once], axis=1), jnp.concatenate([high, low], axis=0)
        )
        for side in range(2):
            head = 2 * pair + side
            part = column(reach, head) * forward[side * TOKENS : (side + 1) * TOKENS]
            total = total + part
            reached = jnp.where(
                lanes == head, jnp.sum(part * wide, axis=1, keepdims=True), reached
            )
    high, low = halves((mixed[...] * scale).T)
    total = total + dot(high, keys[...]) + dot(low, keys[...])
    queries_out[...] = total.astype(BF16)
    reached = reached.T[:HEADS]
    later = (iota((TOKENS, TOKENS), 0) >= iota((TOKENS, TOKENS), 1)).astype(F32)
    carried = jnp.sum(jnp.concatenate(overlaps, axis=0), axis=1, keepdims=True)
    carried = carried * jnp.exp(running[:, TOKENS - 1 :])
    closer = column_sums[...] * scale
    log_pull = (
        exact_dot(row_sums[...] * scale - closer + reached, later) + log_sums(ended[...]) + carried
    )
    steps_out[...] = (closer + ended[...]) / steps[...] - rate * log_pull
    local = jnp.sum(-steps[...] * rate * log_pull, axis=1, keepdims=True)
    row = transposed(jnp.broadcast_to(local, (HEADS, TOKENS)))[0:1] + prompt_decay[0:1]
    summary[...] = jnp.broadcast_to(row, (DEVICES, TOKENS))


def moved_lanes(rows, by):
    shift = (iota((TOKENS, TOKENS), 0) == iota((TOKENS, TOKENS), 1) + by).astype(F32)
    return exact_dot(rows, shift)


def finish_kernel(place, decay_log, received, owned, steps, steps_out, decay):
    rows = received[...]
    below = (iota((DEVICES, DEVICES), 0) > iota((DEVICES, DEVICES), 1)).astype(F32)
    before = exact_dot(below, moved_lanes(rows, HEADS))
    decay_rows = rows + before * moved_lanes(rows, 2 * HEADS)
    decay[...] = jnp.broadcast_to(jnp.sum(decay_rows, axis=0, keepdims=True), (8, TOKENS))
    mine = jnp.where(iota((DEVICES, TOKENS), 0) < place[0, 0], rows, 0.0)
    mine = as_columns(jnp.sum(mine, axis=0, keepdims=True))[HEADS : 2 * HEADS]
    steps_out[...] = owned[...] / steps[...] - rates(decay_log) * (log_sums(owned[...]) + mine)


def whole(dims):
    return pl.BlockSpec(dims, lambda step: (0,) * len(dims))


def on_device(kernel, out_shapes, scalars, flops, *operands, vmem=VMEM_BYTES):
    specs = [pl.BlockSpec(memory_space=pltpu.SMEM) for _ in range(scalars)]
    specs += [whole(x.shape) for x in operands[scalars:]]
    return pl.pallas_call(
        kernel,
        grid=(1,),
        out_shape=out_shapes,
        in_specs=specs,
        out_specs=[whole(x.shape) for x in out_shapes],
        compiler_params=pltpu.CompilerParams(vmem_limit_bytes=vmem),
        cost_estimate=pl.CostEstimate(flops=flops, bytes_accessed=1024, transcendentals=0),
    )(*operands)


def shape(*dims, dtype=F32):
    return jax.ShapeDtypeStruct(dims, dtype)


def swap(value, axis):
    return lax.all_to_all(value, axis, 0, 0, tiled=True)


def turn(block):
    pairs = [(a * SLICES + b, b * SLICES + a) for a in range(SLICES) for b in range(SLICES)]
    return lax.ppermute(block, BOTH, pairs)


def traded(value, axis, bit):
    return lax.ppermute(value, axis, [(at, at ^ bit) for at in range(SLICES)])


def later_sums(later, total, earlier):
    for step, bit in enumerate((1, 2, 4, 8)):
        other = traded(total, "rollout", bit)
        later = later + jnp.where(earlier[step] == 1, other, 0.0)
        total = total + other
    return later


def reduced_over_rows(states, earlier, beside):
    block = states.shape[1:]
    left = [8, 4, 2, 1]
    for bit in HALVING:
        side = 1 - earlier[(1, 2, 4, 8).index(bit)]
        axis = left.index(bit)
        split = states.reshape((2,) * len(left) + block)
        given = lax.dynamic_index_in_dim(split, 1 - side, axis, keepdims=False)
        kept = lax.dynamic_index_in_dim(split, side, axis, keepdims=False)
        left.remove(bit)
        flat = (2 ** len(left),) + block
        states = kept.reshape(flat) + traded(given.reshape(flat), "rollout", bit)
        if bit == HALVING[1]:
            states, beside = lax.optimization_barrier((states, beside))
    return states[0], beside


def doubled(parts, earlier, bits):
    for bit in bits:
        other = traded(parts, "rollout", bit)
        low = earlier[(1, 2, 4, 8).index(bit)] == 1
        first, second = jnp.where(low, parts, other), jnp.where(low, other, parts)
        parts = jnp.stack([first, second], axis=1).reshape((-1,) + parts.shape[1:])
    return parts


def per_device(
    prompt_inputs, prompt_keys, prompt_steps, reply_inputs, reply_keys, reply_queries,
    reply_steps, decay_log, upstream, loss_mask, advantage_index, advantage_table,
):
    reply_inputs, reply_keys, reply_queries = reply_inputs[0], reply_keys[0], reply_queries[0]
    reply_steps, upstream = reply_steps[0], upstream[0]
    scale = (advantage_index, advantage_table)
    row, mine = lax.axis_index("rollout"), lax.axis_index("ctx")
    place = (row * SLICES + mine).astype(jnp.int32).reshape(1, 1)
    owner = mine.astype(jnp.int32).reshape(1, 1)
    slices = shape(SLICES, ROWS, STATE)
    heads = shape(HEADS, TOKENS)
    square = shape(TOKENS, TOKENS)
    wide = shape(TOKENS, CHANNELS, dtype=BF16)
    narrow = shape(TOKENS, STATE, dtype=BF16)

    prompt_logs, prompt_total = on_device(
        prompt_logs_kernel, [heads, shape(SLICES, TOKENS)], 1, 10**6, decay_log, prompt_steps,
        vmem=VMEM_MOST,
    )
    earlier = [((row & bit) == 0).astype(jnp.int32) for bit in (1, 2, 4, 8)]
    group_totals = swap(prompt_total, "ctx")
    pack, reply_logs = on_device(
        first_kernel, [shape(SLICES, GO, STATE), heads], 3, 5 * 10**9,
        decay_log, *scale, reply_inputs, reply_keys, reply_queries, reply_steps, upstream,
        loss_mask, vmem=VMEM_MOST,
    )
    later = jnp.sum(
        jnp.where(jnp.arange(SLICES)[:, None] > mine, group_totals, 0.0), axis=0, keepdims=True
    )
    total = jnp.sum(group_totals, axis=0, keepdims=True)
    later, total = (jnp.broadcast_to(x, (8, TOKENS)) for x in (later, total))
    pack, later, total, owner, place, earlier = lax.optimization_barrier(
        (pack, later, total, owner, place, earlier)
    )
    received = swap(pack, "ctx")
    later = later_sums(later, total, earlier)
    prompt_states, prompt_ends = on_device(
        prompt_states_kernel, [slices, heads], 0, 3 * 10**6,
        prompt_inputs, prompt_keys, prompt_steps, prompt_logs, later,
    )
    near, mixed, row_sums, column_sums = on_device(
        within_kernel, [shape(TOKENS, CHANNELS), square, heads, heads], 0, 6 * 10**6,
        reply_inputs, reply_keys, reply_queries, reply_steps, upstream, loss_mask, reply_logs,
    )
    prompt_states, row_sums = reduced_over_rows(prompt_states, earlier, row_sums)
    received, prompt_states = lax.optimization_barrier((received, turn(prompt_states)))
    after, row_pulls, totals = on_device(
        group_kernel, [slices, shape(ROWS, STATE), shape(SLICES, STATE)], 1, 3 * 10**6,
        owner, received,
    )
    after = swap(after, "ctx")
    joint = jnp.concatenate([prompt_states, row_pulls], axis=0)
    for bit in (1, 2, 4, 8):
        joint = joint + traded(joint, "rollout", bit)
    starts, flag = on_device(
        carry_kernel, [slices, shape(8, STATE)], 1, 3 * 10**6,
        owner, totals, received, joint[:ROWS],
    )
    turned = turn(joint[ROWS:])
    turned, flag, after, near = lax.optimization_barrier((turned, flag, after, near))
    starts = swap(starts, "ctx")
    end_pull = doubled(turned[None], earlier, DOUBLING[:2])
    end_pull, after = lax.optimization_barrier((end_pull, after))
    reply_inputs_out, reply_keys_out, ended = on_device(
        reply_backward_kernel, [wide, narrow, heads], 2, 6 * 10**6,
        *scale, reply_inputs, reply_keys, reply_queries, reply_steps, reply_logs, after, near,
        mixed,
    )
    end_pull = doubled(end_pull, earlier, DOUBLING[2:3])
    end_pull, ended = lax.optimization_barrier((end_pull, ended))
    end_pull = doubled(end_pull, earlier, DOUBLING[3:])
    prompt_inputs_out, prompt_keys_out, owned, prompt_decay = on_device(
        prompt_backward_kernel, [wide, narrow, heads, shape(8, TOKENS)], 1, 6 * 10**6,
        decay_log, prompt_inputs, prompt_keys, prompt_steps, prompt_logs, prompt_ends, end_pull,
        flag,
    )
    reply_queries_out, reply_steps_out, summary = on_device(
        reply_forward_kernel, [narrow, heads, shape(DEVICES, TOKENS)], 3, 6 * 10**6,
        decay_log, *scale, reply_keys, reply_queries, reply_steps, upstream, loss_mask,
        reply_logs, starts, after, mixed, row_sums, column_sums, ended, prompt_decay,
        vmem=VMEM_MOST,
    )
    prompt_steps_out, decay = on_device(
        finish_kernel, [heads, shape(8, TOKENS)], 2, 10**8,
        place, decay_log, swap(summary, BOTH), owned, prompt_steps,
    )
    return (
        prompt_inputs_out, prompt_keys_out, prompt_steps_out, reply_inputs_out[None],
        reply_keys_out[None], reply_queries_out[None], reply_steps_out[None], decay[0, :HEADS],
    )


def solution(mesh):
    in_specs = (
        P(("rollout", "ctx"), None),
        P(("rollout", "ctx"), None),
        P(None, ("rollout", "ctx")),
        P("rollout", "ctx", None),
        P("rollout", "ctx", None),
        P("rollout", "ctx", None),
        P("rollout", None, "ctx"),
        P(),
        P("rollout", "ctx", None),
        P("rollout", "ctx"),
        P("rollout"),
        P(),
    )
    out_specs = (
        P(("rollout", "ctx"), None),
        P(("rollout", "ctx"), None),
        P(None, ("rollout", "ctx")),
        P("rollout", "ctx", None),
        P("rollout", "ctx", None),
        P("rollout", "ctx", None),
        P("rollout", None, "ctx"),
        P(),
    )
    return jax.shard_map(
        per_device, mesh=mesh, in_specs=in_specs, out_specs=out_specs, check_vma=False
    )
```
